32 devices in a mesh: tm: 16 (over z, x, core), fsdp: 2 (over y).
Axes of the slice: x: 2, y: 2, z: 4, core: 2. Of those that a mesh axis runs over, the one named last changes fastest.
Arguments:
- frames: bfloat16 [2, 2, 24576, 512], P(None, 'fsdp', 'tm'), may hold values from -6 to 6
- conditioning: bfloat16 [2, 2, 24576, 512], P(None, 'fsdp', 'tm'), may hold values from -6 to 6
- lengths: int32 [2, 2, 30], P(None, 'fsdp'), may hold values from 1 to 1600, 24576 in all within a row
- steps: int32 [2, 2, 30], P(None, 'fsdp'), may hold values from 0 to 999
- prompt: bfloat16 [2, 2, 256, 512], P(None, 'fsdp', 'tm'), may hold values from -6 to 6
- queries: float32 [32, 512], P('fsdp'), may hold values from -6 to 6
- w_step: float32 [512, 1024], P('fsdp'), may hold values from -0.25 to 0.25
- w_cond: float32 [512, 1024], P('fsdp'), may hold values from -0.25 to 0.25
- w_conv: float32 [3, 512, 1024], P(None, 'fsdp'), may hold values from -0.15625 to 0.15625
- w_query: float32 [512, 512], P('fsdp'), may hold values from -0.25 to 0.25
- w_key: float32 [512, 512], P('fsdp'), may hold values from -0.25 to 0.25
- w_value: float32 [512, 512], P('fsdp'), may hold values from -0.25 to 0.25
- w_out: float32 [512, 512], P('fsdp'), may hold values from -2 to 2
- w_film: float32 [512, 1024], P('fsdp'), may hold values from -2 to 2
- w_proj: float32 [512, 1024], P('fsdp'), may hold values from -0.25 to 0.25
- grad_res: bfloat16 [2, 2, 24576, 512], P(None, 'fsdp', 'tm'), may hold values from -6 to 6
- grad_skip: bfloat16 [2, 2, 24576, 512], P(None, 'fsdp', 'tm'), may hold values from -6 to 6
Outputs:
- res_out: bfloat16 [2, 2, 24576, 512], P(None, 'fsdp', 'tm')
- skip_out: bfloat16 [2, 2, 24576, 512], P(None, 'fsdp', 'tm')
- grad_frames: float32 [2, 2, 24576, 512], P(None, 'fsdp', 'tm')
- grad_prompt: float32 [2, 2, 256, 512], P(None, 'fsdp', 'tm')
- grad_queries: float32 [32, 512], P('fsdp')
- grad_step: float32 [512, 1024], P('fsdp')
- grad_cond: float32 [512, 1024], P('fsdp')
- grad_conv: float32 [3, 512, 1024], P(None, 'fsdp')
- grad_query: float32 [512, 512], P('fsdp')
- grad_key: float32 [512, 512], P('fsdp')
- grad_value: float32 [512, 512], P('fsdp')
- grad_out: float32 [512, 512], P('fsdp')
- grad_film: float32 [512, 1024], P('fsdp')
- grad_proj: float32 [512, 1024], P('fsdp')
The draws below stay inside these ranges and needn't reach their ends.
Inputs may be any that keep to these rules, and one draw needn't show every extreme that they name: Each pack's 30 lengths sum to its 24576 frames; the last entry is the padding at the pack's end; the longest entry is exactly 1600.
All inputs are finite; a program needn't handle non-finite values.
Results may differ from the reference program's by a relative error of at most 0.0085.
The reference program's roundings to bfloat16 on the way count: a program that leaves them out, or rounds other values in their place, can miss the bound.
Values may be sent and summed in bfloat16 or wider, within the bound.
No kernel may reach another device: no remote copies, remote signals or barrier semaphores. Data moves between devices by JAX's collectives and lax.ppermute only.
A program may use at most 104 MiB of HBM per device.

```python
import math
import jax
import jax.numpy as jnp
import numpy as np
from jax import lax

WIDTH = 512
HEADS = 8
QUERIES = 32
DILATION = 16
MICRO = 2
LONGEST = 1600
STEP_COUNT = 1000
PACK_FRAMES = 24576
PACKS = 2
UTTERS = 30
PROMPT_LEN = 256


def set_ends(array, key, smallest, largest):
    extent = array.shape
    place = [jax.random.randint(jax.random.fold_in(key, axis), (), 0, extent[axis]) for axis in range(len(extent))]
    array = array.at[tuple(place)].set(smallest)
    longest = extent.index(max(extent))
    place[longest] = (place[longest] + 1) % extent[longest]
    return array.at[tuple(place)].set(largest)


def block_scale(stream_key, extent, cuts, least, high):
    gain, own = 1.0, jax.random.fold_in(stream_key, 6)
    for dim, parts in cuts:
        steps = jnp.exp(jax.random.uniform(jax.random.fold_in(own, dim), (parts,), jnp.float32, least / len(cuts), high / len(cuts)))
        gain = gain * jnp.repeat(steps, extent[dim] // parts).reshape([-1 if axis == dim else 1 for axis in range(len(extent))])
    return gain


def length_profile(number_of, total, most, slope):
    loads = [(1 << 20) // math.isqrt(grade ** slope) + 1 for grade in range(2, number_of + 1)]
    surplus, given = total - most - (number_of - 1), [1] * (number_of - 1)
    while surplus > 0:
        candidates = [i for i in range(number_of - 1) if given[i] < most]
        mass, remaining = sum([loads[i] for i in candidates]), surplus
        for i in candidates:
            addition = min(most - given[i], max(1, remaining * loads[i] // mass), surplus)
            given[i] = given[i] + addition
            surplus = surplus - addition
    return np.array([most] + given)


def uneven_parts(stream_key, count, total, most, skew):
    if count == 2:
        one = jax.random.randint(stream_key, (), max(1, total - most), min(most, total - 1) + 1)
        return jnp.stack([one, total - one])
    tallies = jnp.asarray(length_profile(count, total, most, skew), jnp.int32)
    couples = (count - 1) // 2
    source_of, receiver = tallies[1:1 + 2 * couples:2], tallies[2:2 + 2 * couples:2]
    margin = jnp.minimum(source_of - 1, most - receiver)
    shifted = jax.random.randint(jax.random.fold_in(stream_key, 1), (couples,), 0, 1 << 20) % (margin + 1)
    tallies = tallies.at[1:1 + 2 * couples:2].set(source_of - shifted).at[2:2 + 2 * couples:2].set(receiver + shifted)
    return tallies[jax.random.permutation(jax.random.fold_in(stream_key, 2), count)]


def gaussian(rng, extent, width, limit, cuts=(), kind=jnp.bfloat16):
    entries = jax.random.normal(rng, extent, jnp.float32) * width
    if len(cuts) > 0:
        entries = block_scale(rng, extent, cuts, -0.22, 0.18) * entries
    return jnp.clip(entries, min=-limit, max=limit).astype(kind)


def setup_inputs(seed: int = 0) -> dict:
    streams_of = jax.random.split(jax.random.key(seed), 18)
    frames = gaussian(streams_of[0], (MICRO, PACKS, PACK_FRAMES, WIDTH), 1.0, 6.0, ((1, 2), (2, 16)))
    conditioning = gaussian(streams_of[1], (MICRO, PACKS, PACK_FRAMES, WIDTH), 1.0, 6.0, ((1, 2), (2, 16)))
    lengths = jax.vmap(lambda own: uneven_parts(own, UTTERS, PACK_FRAMES, LONGEST, 2))(jax.random.split(streams_of[2], MICRO * PACKS)).reshape((MICRO, PACKS, UTTERS)).astype(jnp.int32)
    steps = set_ends(jax.random.randint(streams_of[3], (MICRO, PACKS, UTTERS), 0, STEP_COUNT), jax.random.fold_in(streams_of[3], 1), 0, STEP_COUNT - 1).astype(jnp.int32)
    prompt = gaussian(streams_of[4], (MICRO, PACKS, PROMPT_LEN, WIDTH), 1.0, 6.0, ((1, 2), (2, 16)))
    queries = gaussian(streams_of[5], (QUERIES, WIDTH), 1.0, 6.0, ((0, 2),), jnp.float32)
    w_step = gaussian(streams_of[6], (WIDTH, 2 * WIDTH), WIDTH ** -0.5, 0.25, ((0, 2),), jnp.float32)
    w_cond = gaussian(streams_of[7], (WIDTH, 2 * WIDTH), WIDTH ** -0.5, 0.25, ((0, 2),), jnp.float32)
    w_conv = gaussian(streams_of[8], (3, WIDTH, 2 * WIDTH), (3 * WIDTH) ** -0.5, 0.15625, ((1, 2),), jnp.float32)
    w_query = gaussian(streams_of[9], (WIDTH, WIDTH), WIDTH ** -0.5, 0.25, ((0, 2),), jnp.float32)
    w_key = gaussian(streams_of[10], (WIDTH, WIDTH), WIDTH ** -0.5, 0.25, ((0, 2),), jnp.float32)
    w_value = gaussian(streams_of[11], (WIDTH, WIDTH), WIDTH ** -0.5, 0.25, ((0, 2),), jnp.float32)
    w_out = gaussian(streams_of[12], (WIDTH, WIDTH), 8 ** -0.5, 2.0, ((0, 2),), jnp.float32)
    w_film = gaussian(streams_of[13], (WIDTH, 2 * WIDTH), 8 ** -0.5, 2.0, ((0, 2),), jnp.float32)
    w_proj = gaussian(streams_of[14], (WIDTH, 2 * WIDTH), WIDTH ** -0.5, 0.25, ((0, 2),), jnp.float32)
    grad_res = gaussian(streams_of[15], (MICRO, PACKS, PACK_FRAMES, WIDTH), 1.0, 6.0, ((1, 2), (2, 16)))
    grad_skip = gaussian(streams_of[16], (MICRO, PACKS, PACK_FRAMES, WIDTH), 1.0, 6.0, ((1, 2), (2, 16)))
    return {"frames": frames, "conditioning": conditioning, "lengths": lengths, "steps": steps, "prompt": prompt, "queries": queries, "w_step": w_step, "w_cond": w_cond, "w_conv": w_conv, "w_query": w_query, "w_key": w_key, "w_value": w_value, "w_out": w_out, "w_film": w_film, "w_proj": w_proj, "grad_res": grad_res, "grad_skip": grad_skip}


@jax.custom_vjp
def low(v):
    return lax.optimization_barrier(v.astype(jnp.bfloat16)).astype(jnp.float32)

@jax.custom_vjp
def low_back(v):
    return v

def low_keep(v):
    return (low(v), None)

def low_pass(kept, grad):
    return (grad,)

def back_keep(v):
    return (v, None)

def back_low(kept, grad):
    return (low(grad),)
low.defvjp(low_keep, low_pass)
low_back.defvjp(back_keep, back_low)
PRECISE = lax.Precision.HIGHEST
SQRT_HALF = 0.7071067811865476

def segment_of(positions, pack_lengths):
    utter_ends = jnp.cumsum(pack_lengths)
    return lax.optimization_barrier(jnp.sum((positions[:, None] >= utter_ends[None, :]).astype(jnp.int32), axis=1))

def step_embedding(pack_steps):
    half_width = WIDTH // 2
    freqs = jnp.exp(jnp.arange(half_width).astype(jnp.float32) * (-math.log(10000.0) / half_width))
    angles = pack_steps.astype(jnp.float32)[:, None] * freqs[None, :]
    return jnp.concatenate([jnp.sin(angles), jnp.cos(angles)], axis=1)

def film_block(frame_rows, cond_rows, prompt_rows, weight_set, segment, live_mask, step_embed):
    lowered = [low(weight) for weight in weight_set]
    query_tokens, w_step, w_cond, w_conv, w_query, w_key, w_value, w_out, w_film, w_proj = lowered
    step_film = jnp.dot(low(step_embed), w_step, precision=PRECISE)
    film_first = low_back(step_film[segment] + jnp.dot(cond_rows, w_cond, precision=PRECISE))
    gain_first = film_first[:, :WIDTH]
    shift_first = film_first[:, WIDTH:]
    hidden = low(frame_rows * (1.0 + gain_first) + shift_first)
    padded = jnp.pad(hidden, ((DILATION, DILATION), (0, 0)))
    seg_padded = jnp.pad(segment, (DILATION, DILATION), constant_values=-1)
    conv_out = jnp.zeros((PACK_FRAMES, 2 * WIDTH), jnp.float32)
    for tap in range(3):
        rows = padded[tap * DILATION:tap * DILATION + PACK_FRAMES]
        same = (seg_padded[tap * DILATION:tap * DILATION + PACK_FRAMES] == segment).astype(jnp.float32)
        conv_out = conv_out + jnp.dot(rows * same[:, None], w_conv[tap], precision=PRECISE)
    conv_out = low_back(conv_out)
    activated = jnp.tanh(conv_out[:, :WIDTH]) * jax.nn.sigmoid(conv_out[:, WIDTH:])
    head_size = WIDTH // HEADS
    query_rows = low(jnp.dot(query_tokens, w_query, precision=PRECISE)).reshape(QUERIES, HEADS, head_size)
    key_rows = low(low_back(jnp.dot(prompt_rows, w_key, precision=PRECISE))).reshape(PROMPT_LEN, HEADS, head_size)
    value_rows = low(low_back(jnp.dot(prompt_rows, w_value, precision=PRECISE))).reshape(PROMPT_LEN, HEADS, head_size)
    scores = jnp.einsum('qhd,khd->hqk', query_rows, key_rows, precision=PRECISE) * (1.0 / math.sqrt(head_size))
    scores = low_back(scores)
    probs = jax.nn.softmax(scores, axis=-1)
    context = jnp.einsum('hqk,khd->qhd', low(probs), value_rows, precision=PRECISE).reshape(QUERIES, WIDTH)
    context = low(low_back(context))
    projected = jnp.dot(context, w_out, precision=PRECISE)
    summary = low(lax.optimization_barrier(jnp.mean(projected, axis=0)))
    film_second = jnp.dot(summary[None, :], w_film, precision=PRECISE)[0]
    gated_rows = low(activated * (1.0 + film_second[:WIDTH]) + film_second[WIDTH:])
    branch_out = low_back(jnp.dot(gated_rows, w_proj, precision=PRECISE))
    residual_out = (frame_rows + branch_out[:, :WIDTH]) * SQRT_HALF * live_mask[:, None]
    skip_rows = branch_out[:, WIDTH:] * live_mask[:, None]
    return (residual_out, skip_rows)

def reference(frames, conditioning, lengths, steps, prompt, queries, w_step, w_cond, w_conv, w_query, w_key, w_value, w_out, w_film, w_proj, grad_res, grad_skip):
    weights = (queries.astype(jnp.float32), w_step.astype(jnp.float32), w_cond.astype(jnp.float32), w_conv.astype(jnp.float32), w_query.astype(jnp.float32), w_key.astype(jnp.float32), w_value.astype(jnp.float32), w_out.astype(jnp.float32), w_film.astype(jnp.float32), w_proj.astype(jnp.float32))
    totals = tuple((jnp.zeros_like(weight) for weight in weights))
    positions = jnp.arange(PACK_FRAMES).astype(jnp.int32)
    res_micro, skip_micro, frame_micro, prompt_micro = ([], [], [], [])
    for micro_index in range(MICRO):
        res_packs, skip_packs, frame_packs, prompt_packs = ([], [], [], [])
        for pack_index in range(PACKS):
            segment = segment_of(positions, lengths[micro_index, pack_index])
            live_mask = (segment < UTTERS - 1).astype(jnp.float32)
            step_embed = step_embedding(steps[micro_index, pack_index])
            cond_rows = conditioning[micro_index, pack_index].astype(jnp.float32)

            def forward(frame_rows, prompt_rows, weight_set):
                return film_block(frame_rows, cond_rows, prompt_rows, weight_set, segment, live_mask, step_embed)
            outputs, pullback = jax.vjp(forward, frames[micro_index, pack_index].astype(jnp.float32), prompt[micro_index, pack_index].astype(jnp.float32), weights)
            cotangent = (grad_res[micro_index, pack_index].astype(jnp.float32), grad_skip[micro_index, pack_index].astype(jnp.float32))
            frame_grad, prompt_grad, weight_grads = pullback(cotangent)
            totals = tuple((total + grad for total, grad in zip(totals, weight_grads)))
            res_packs.append(outputs[0].astype(jnp.bfloat16))
            skip_packs.append(outputs[1].astype(jnp.bfloat16))
            frame_packs.append(frame_grad)
            prompt_packs.append(prompt_grad)
        res_micro.append(jnp.stack(res_packs))
        skip_micro.append(jnp.stack(skip_packs))
        frame_micro.append(jnp.stack(frame_packs))
        prompt_micro.append(jnp.stack(prompt_packs))
    return (jnp.stack(res_micro), jnp.stack(skip_micro), jnp.stack(frame_micro), jnp.stack(prompt_micro), totals[0], totals[1], totals[2], totals[3], totals[4], totals[5], totals[6], totals[7], totals[8], totals[9])
```

```python
import functools
import math

import jax
import jax.numpy as jnp
from jax import lax
from jax.experimental import pallas as pl
from jax.experimental.pallas import tpu as pltpu
from jax.sharding import PartitionSpec as P

HEADS = 8
QUERIES = 32
DILATION = 16
MICRO = 2
HALO = 2 * DILATION

SQRT_HALF = 0.7071067811865476
VMEM_LIMIT = 40 * 2**20
NT = ((1,), (1,))
TN = ((0,), (0,))
bf16 = jnp.bfloat16
f32 = jnp.float32


def dotf(left, right, dims=((1,), (0,))):
    return lax.dot_general(left, right, (dims, ((), ())), preferred_element_type=f32)


def lanes(block, width):
    return jnp.concatenate([block] * (width // block.shape[1]), axis=1)


VSPEC = pl.BlockSpec(memory_space=pltpu.VMEM)
SSPEC = pl.BlockSpec(memory_space=pltpu.SMEM)
ANYSPEC = pl.BlockSpec(memory_space=pl.ANY)


def fixed(array):
    return pltpu.with_memory_space_constraint(array, pltpu.VMEM), VSPEC


def whole(array):
    return pltpu.with_memory_space_constraint(array, pltpu.HBM), pl.BlockSpec(array.shape, lambda *_: (0,) * array.ndim)


def blocks(array, tile, first=0):
    return pltpu.with_memory_space_constraint(array, pltpu.HBM), pl.BlockSpec(
        (1, tile, array.shape[2]), lambda i, j: (i + first, j, 0)
    )


def hbm(array):
    return pltpu.with_memory_space_constraint(array, pltpu.HBM), pl.BlockSpec(memory_space=pltpu.HBM)


def scalars(array):
    return array, SSPEC


def call(kernel, grid, ins, outs, name, flops, scratch=(), after=(), aliases=None):
    count, waits = len(ins), len(after)

    def body(*refs):
        kernel(*refs[:count], *refs[count + waits :])

    return pl.pallas_call(
        body,
        grid=grid,
        in_specs=[spec for _, spec in ins] + [ANYSPEC] * waits,
        out_specs=[spec for _, spec in outs],
        out_shape=[out for out, _ in outs],
        scratch_shapes=scratch,
        input_output_aliases=aliases or {},
        cost_estimate=pl.CostEstimate(
            flops=int(flops), bytes_accessed=2**12, transcendentals=0
        ),
        compiler_params=pltpu.CompilerParams(vmem_limit_bytes=VMEM_LIMIT),
        name=name,
    )(*[array for array, _ in ins], *after)


def new(shape, kind=f32):
    return pltpu.HBM(shape, kind), pl.BlockSpec(shape, lambda *_: (0,) * len(shape))


def new_fixed(shape, kind=f32):
    return pltpu.VMEM(shape, kind), VSPEC


def new_hbm(shape, kind=f32):
    return pltpu.HBM(shape, kind), pl.BlockSpec(memory_space=pltpu.HBM)


def new_blocks(shape, kind, tile, first=0):
    return pltpu.HBM(shape, kind), pl.BlockSpec(
        (1, tile, shape[2]), lambda i, j: (i + first, j, 0)
    )


def split_rows(row, parts):
    terms = []
    for _ in range(parts):
        term = row.astype(bf16)
        terms.append(term)
        row = row - term.astype(f32)
    return terms


def pack_kernel(layouts, place, *refs):
    count = sum(map(len, layouts))
    weights, refs = list(refs[:count]), refs[count:]
    outs, helds, sems = refs[: len(layouts)], refs[len(layouts) : -1], refs[-1]
    copies = []
    for layout, held in zip(layouts, helds, strict=True):
        for row, column in layout:
            weight = weights.pop(0)
            views = [weight] if len(weight.shape) == 2 else [weight.at[t] for t in range(weight.shape[0])]
            rows = views[0].shape[0] // 4
            start = pl.multiple_of(place[3] * rows, rows)
            for t, view in enumerate(views):
                copies.append(
                    pltpu.make_async_copy(
                        view.at[pl.ds(start, rows)],
                        held.at[pl.ds(row + t * rows, rows), pl.ds(column, view.shape[1])],
                        sems.at[len(copies)],
                    )
                )
    for copy in copies:
        copy.start()
    for copy in copies:
        copy.wait()
    for out, held in zip(outs, helds, strict=True):
        out[...] = held[...].astype(bf16)


def edges_kernel(*refs):
    arrays, (last, first, sems) = refs[:-3], refs[-3:]
    copies = []
    for k, array in enumerate(arrays):
        rows = array.shape[1]
        copies.append(
            pltpu.make_async_copy(array.at[:, pl.ds(rows - HALO, HALO)], last.at[k], sems.at[2 * k])
        )
        copies.append(
            pltpu.make_async_copy(array.at[:, pl.ds(0, HALO)], first.at[k], sems.at[2 * k + 1])
        )
    for copy in copies:
        copy.start()
    for copy in copies:
        copy.wait()


def unpack_kernel(layout, members, place, *refs):
    count = len(layout)
    shards, (here, over, core, both) = refs[:count], refs[count : count + 4]
    fulls, copies = refs[count + 4 : 2 * count + 4], refs[2 * count + 4 :]
    member, quarter = place[2], place[3]
    sources = ((here, quarter), (over, quarter ^ 1), (core, quarter ^ 2), (both, quarter ^ 3))
    for shard, full, (row, column) in zip(shards, fulls, layout, strict=True):
        rows, width = shard.shape[-2:]
        part = rows // 4
        taps = 1 if len(shard.shape) == 2 else shard.shape[0]
        for t in range(taps):
            own = shard[...] if taps == 1 else shard[t]
            top = t * members * rows
            full[pl.ds(pl.multiple_of(top + member * rows, part), rows)] = own.astype(bf16)
            at = row + t * part
            for j in range(1, members):
                for source, q in sources:
                    start = pl.multiple_of(top + (member ^ j) * rows + q * part, part)
                    full[pl.ds(start, part)] = source[j - 1, at : at + part, column : column + width]
    for full, copy in zip(fulls, copies, strict=False):
        copy[...] = full[...]


def masks_kernel(rows, slot, total, place, lengths, masks, ends):
    micro, utters = lengths.shape
    hots = masks.shape[2] - 3 * 128
    lane = lax.broadcasted_iota(jnp.int32, (1, hots), 1)
    lane = jnp.where(lane >= micro * slot, lane - micro * slot, lane)
    row = lax.broadcasted_iota(jnp.int32, (hots, 128), 0)
    count = jnp.where(row < micro * slot, 1.0, 0.0).astype(bf16)
    first = place[1] * rows - HALO
    chunk = rows // 6
    for i in range(micro):
        opens = jnp.full((1, hots), total, jnp.int32)
        closes = jnp.zeros((1, hots), jnp.int32)
        end = jnp.int32(0)
        for u in range(utters):
            mine = lane == i * slot + u
            if u == utters - 1:
                alive_until = end
            opens = jnp.where(mine, end, opens)
            end = end + lengths[i, u]
            closes = jnp.where(mine, end, closes)

        def rows_of(start, size, i=i, opens=opens, closes=closes, alive_until=alive_until):
            position = lax.broadcasted_iota(jnp.int32, (size, hots), 0) + start

            def one_hot(offset):
                shifted = position + offset
                return jnp.where((shifted >= opens) & (shifted < closes), 1.0, 0.0).astype(bf16)

            here = one_hot(0)
            low = dotf(here * one_hot(-DILATION), count).astype(bf16)
            high = dotf(here * one_hot(DILATION), count).astype(bf16)
            alive = (position[:, :128] < alive_until) & (position[:, :128] >= 0)
            return jnp.concatenate(
                [low, high, jnp.where(alive, 1.0, 0.0).astype(bf16), here], axis=1
            )

        ends[i, 0:HALO] = rows_of(first, HALO)
        ends[i, HALO:] = rows_of(first + HALO + rows, HALO)

        @pl.loop(0, rows // chunk)
        def _(k, i=i, rows_of=rows_of):
            at = pl.multiple_of(k * chunk, chunk)
            masks[i, pl.ds(at, chunk)] = rows_of(first + HALO + at, chunk)


def film_kernel(
    tile, frames, cond, low, high, masks, ends, embed, w_step, w_cond, hidden, gain, film_rows
):
    i, j = pl.program_id(0), pl.program_id(1)
    width = frames.shape[2]
    rows = hidden.shape[1] - 2 * HALO - 2 * DILATION

    @pl.when((i == 0) & (j == 0))
    def _():
        step_film = dotf(embed[...], w_step[...])
        film_rows[...] = jnp.concatenate(split_rows(step_film, 2), axis=0)

    def film(frame_rows, cond_rows, hot):
        both = dotf(cond_rows, w_cond[...]) + dotf(hot, film_rows[...])
        gain_rows = both[:, :width]
        return (frame_rows.astype(f32) * (1.0 + gain_rows) + both[:, width:]).astype(bf16), gain_rows

    @pl.when(j == 0)
    def _():
        edge, _ = film(
            jnp.concatenate([low[0, i], high[0, i]], axis=0),
            jnp.concatenate([low[1, i], high[1, i]], axis=0),
            ends[i, :, 384:],
        )
        nothing = jnp.zeros((DILATION, width), bf16)
        hidden[i, 0:DILATION] = nothing
        hidden[i, DILATION : DILATION + HALO] = edge[:HALO]
        hidden[i, DILATION + HALO + rows : DILATION + 2 * HALO + rows] = edge[HALO:]
        hidden[i, DILATION + 2 * HALO + rows :] = nothing

    base = pl.multiple_of(j * tile, tile)
    own, gain_rows = film(frames[0], cond[0], masks[0, :, 384:])
    hidden[i, pl.ds(DILATION + HALO + base, tile)] = own
    gain[0] = gain_rows


def halves_of(core, width):
    mine = pl.multiple_of(core * width, width)
    other = pl.multiple_of((1 - core) * width, width)
    return mine, other


def conv_kernel(
    tile, place, hidden, masks, mask_ends, res, skip, low, high, w_conv, w_proj, film,
    d_conv, d_conv_copy, gated, sums, keep, send, proj_total, columns, sems,
):
    i, j = pl.program_id(0), pl.program_id(1)
    width = res.shape[2]
    rows = d_conv.shape[1] - 2 * HALO
    gain, shift = 1.0 + film[i, 0:1, :width], film[i, 0:1, width:]

    def body(before, here, after, keep_low, keep_high, alive, res_rows, skip_rows):
        taps = jnp.concatenate(
            [before * lanes(keep_low, width), here, after * lanes(keep_high, width)], axis=1
        )
        conv = dotf(taps, w_conv[...])
        th = jnp.tanh(conv[:, :width])
        sg = 0.5 + 0.5 * jnp.tanh(0.5 * conv[:, width:])
        alive = lanes(alive.astype(f32), width)
        branch = jnp.concatenate(
            [
                (res_rows.astype(f32) * (SQRT_HALF * alive)).astype(bf16),
                (skip_rows.astype(f32) * alive).astype(bf16),
            ],
            axis=1,
        )
        d_gated = dotf(branch, w_proj[...], NT)
        act = th * sg
        d_act = d_gated * gain
        left = (d_act * sg * (1.0 - th * th)).astype(bf16)
        right = (d_act * act * (1.0 - sg)).astype(bf16)
        return act, d_gated, branch, left, right

    @pl.when(j == 0)
    def _():
        def ends(ref, at):
            return jnp.concatenate(
                [ref[i, at : at + HALO], ref[i, at + HALO + rows : at + 2 * HALO + rows]], axis=0
            )

        _, _, _, left, right = body(
            ends(hidden, 0),
            ends(hidden, DILATION),
            ends(hidden, 2 * DILATION),
            mask_ends[i, :, 0:128],
            mask_ends[i, :, 128:256],
            mask_ends[i, :, 256:384],
            jnp.concatenate([low[2, i], high[2, i]], axis=0),
            jnp.concatenate([low[3, i], high[3, i]], axis=0),
        )
        d_conv[i, 0:HALO, :width] = left[:HALO]
        d_conv[i, 0:HALO, width:] = right[:HALO]
        d_conv[i, HALO + rows :, :width] = left[HALO:]
        d_conv[i, HALO + rows :, width:] = right[HALO:]
        columns[...] = jnp.zeros(columns.shape, f32)

    @pl.when((i == 0) & (j == 0))
    def _():
        sums[...] = jnp.zeros(sums.shape, f32)

    base = pl.multiple_of(j * tile, tile)

    def at(ref, offset):
        return ref[i, pl.ds(base + offset, tile)]

    act, d_gated, branch, left, right = body(
        at(hidden, HALO),
        at(hidden, HALO + DILATION),
        at(hidden, HALO + 2 * DILATION),
        masks[0, :, 0:128],
        masks[0, :, 128:256],
        masks[0, :, 256:384],
        res[0],
        skip[0],
    )
    d_conv[i, pl.ds(base + HALO, tile), :width] = left
    d_conv[i, pl.ds(base + HALO, tile), width:] = right
    gated_rows = (act * gain + shift).astype(bf16)
    gated[0] = gated_rows
    columns[:, :width] += jnp.sum((d_gated * act).reshape(tile // 8, 8, width), axis=0)
    columns[:, width:] += jnp.sum(d_gated.reshape(tile // 8, 8, width), axis=0)
    part = dotf(gated_rows, branch, TN)
    first = (i == 0) & (j == 0)

    @pl.when(first)
    def _():
        proj_total[...] = part

    @pl.when(jnp.logical_not(first))
    def _():
        proj_total[...] += part

    last = j == rows // tile - 1
    copies = [
        pltpu.make_async_copy(d_conv.at[m], d_conv_copy.at[m], sems.at[m]) for m in range(MICRO)
    ]
    for m in range(MICRO):
        pl.when(last & (i == m))(copies[m].start)

    @pl.when(last & (i == MICRO - 1))
    def _():
        for copy in copies:
            copy.wait()

    for m in range(MICRO):

        @pl.when(last & (i == m))
        def _(m=m):
            sums[m : m + 1] = jnp.sum(columns[...], axis=0, keepdims=True)

    @pl.when(last & (i == MICRO - 1))
    def _():
        mine, other = halves_of(place[0], width)
        send[0] = proj_total[:, pl.ds(other, width)].astype(bf16)
        keep[0] = proj_total[:, pl.ds(mine, width)]


def conv_grad_kernel(place, hidden, masks, d_conv, keep, send):
    t = pl.program_id(0)
    micro, width = hidden.shape[0], hidden.shape[2]
    rows = d_conv.shape[1] - 2 * HALO
    mine, other = halves_of(place[0], width)

    for tap, lane in ((0, 0), (1, None), (2, 128)):

        @pl.when(t == tap)
        def _(tap=tap, lane=lane):
            def tap_rows(i):
                part = hidden[i, HALO + DILATION * tap : HALO + DILATION * tap + rows]
                return part if lane is None else part * lanes(masks[i, :, lane : lane + 128], width)

            for columns, ref in ((other, send), (mine, keep)):
                total = dotf(tap_rows(0), d_conv[0, HALO : HALO + rows, pl.ds(columns, width)], TN)
                for i in range(1, micro):
                    total = total + dotf(
                        tap_rows(i), d_conv[i, HALO : HALO + rows, pl.ds(columns, width)], TN
                    )
                ref[tap] = total.astype(ref.dtype)


def hidden_grad_rows(tile, i, d_conv, masks, frames, gain, res, cond, w_conv, grad_frames, window, sems):
    j = pl.program_id(1)
    steps = pl.num_programs(1)
    width = frames.shape[2]

    def fetch(step):
        start = pl.multiple_of(HALO - DILATION + step * tile, DILATION)
        return pltpu.make_async_copy(
            d_conv.at[i, pl.ds(start, tile + 2 * DILATION)], window.at[step % 2], sems.at[step % 2]
        )

    @pl.when(j == 0)
    def _():
        fetch(0).start()

    @pl.when(j + 1 < steps)
    def _():
        fetch(j + 1).start()

    fetch(j).wait()
    slot = j % 2
    d_hidden = (
        dotf(window[slot, 2 * DILATION :] * lanes(masks[0, :, 128:256], 2 * width), w_conv[0], NT)
        + dotf(window[slot, DILATION : DILATION + tile], w_conv[1], NT)
        + dotf(window[slot, 0:tile] * lanes(masks[0, :, 0:128], 2 * width), w_conv[2], NT)
    )
    alive = lanes(masks[0, :, 256:384].astype(f32), width)
    grad_frames[0] = res[0].astype(f32) * (SQRT_HALF * alive) + d_hidden * (1.0 + gain[0])
    d_film = jnp.concatenate(
        [(d_hidden * frames[0].astype(f32)).astype(bf16), d_hidden.astype(bf16)], axis=1
    )
    return dotf(jnp.concatenate([cond[0], masks[0, :, 384:]], axis=1), d_film, TN)


def hidden_grad_first_kernel(
    tile, d_conv, masks, frames, gain, res, cond, w_conv, grad_frames, total, window, sems
):
    part = hidden_grad_rows(
        tile, 0, d_conv, masks, frames, gain, res, cond, w_conv, grad_frames, window, sems
    )
    j = pl.program_id(1)

    @pl.when(j == 0)
    def _():
        total[...] = part

    @pl.when(j > 0)
    def _():
        total[...] += part


def hidden_grad_last_kernel(
    tile, place, d_conv, masks, frames, gain, res, cond, w_conv, embed, earlier, _frames_0,
    grad_frames, keep, send, total, window, sems,
):
    part = hidden_grad_rows(
        tile, 1, d_conv, masks, frames, gain, res, cond, w_conv, grad_frames, window, sems
    )
    j = pl.program_id(1)
    width = frames.shape[2]

    @pl.when(j == 0)
    def _():
        total[...] = earlier[...] + part

    @pl.when(j > 0)
    def _():
        total[...] += part

    @pl.when(j == pl.num_programs(1) - 1)
    def _():
        mine, other = halves_of(place[0], width)
        count = embed.shape[0]
        for columns, ref in ((other, send), (mine, keep)):
            ref[0] = total[:width, pl.ds(columns, width)].astype(ref.dtype)
            d_step = total[width : width + count, pl.ds(columns, width)]
            step = jnp.zeros((width, width), f32)
            for term in split_rows(d_step, 3):
                step = step + dotf(embed[...], term, TN)
            ref[1] = step.astype(ref.dtype)


def out_kernel(gated, frames, masks, w_proj, res, skip):
    width = gated.shape[2]
    branch = dotf(gated[0], w_proj[...])
    alive = lanes(masks[0, :, 256:384].astype(f32), width)
    res[0] = ((frames[0].astype(f32) + branch[:, :width]) * (SQRT_HALF * alive)).astype(bf16)
    skip[0] = (branch[:, width:] * alive).astype(bf16)


def head_masks(width):
    column = lax.broadcasted_iota(jnp.int32, (1, width), 1)
    size = width // HEADS
    return [((column >= h * size) & (column < (h + 1) * size)).astype(f32) for h in range(HEADS)]


def attention_kernel(groups, place, *refs):
    pieces = refs[:groups]
    queries, w_query, w_key, w_value, w_out, w_film = refs[groups : groups + 6]
    film, prompt, probs, keys, values, spread, summaries, totals = refs[groups + 6 :]
    _, micro, shard, width = pieces[0].shape
    masks = head_masks(width)
    scale = 1.0 / math.sqrt(width // HEADS)
    for g, four in enumerate(pieces):
        for k in range(4):
            start = pl.multiple_of((place[1] ^ (4 * g + k)) * shard, shard)
            for i in range(micro):
                prompt[i, pl.ds(start, shard)] = four[k, i]
    query = dotf(queries[...], w_query[...])
    spread[...] = jnp.concatenate([(query * mask).astype(bf16) for mask in masks], axis=0)
    for i in range(micro):
        keys[i] = dotf(prompt[i], w_key[...]).astype(bf16)
        values[i] = dotf(prompt[i], w_value[...]).astype(bf16)
        scores = dotf(spread[...], keys[i], NT) * scale
        weights = jnp.exp(scores - jnp.max(scores, axis=1, keepdims=True))
        weights = weights / jnp.sum(weights, axis=1, keepdims=True)
        probs[i] = weights
        heads = dotf(weights.astype(bf16), values[i])
        context = heads[:QUERIES] * masks[0]
        for h in range(1, HEADS):
            context = context + heads[h * QUERIES : (h + 1) * QUERIES] * masks[h]
        context = context.astype(bf16)
        mixed = dotf(context, w_out[...])
        summary = jnp.mean(mixed, axis=0, keepdims=True).astype(bf16)
        summary = jnp.broadcast_to(summary.astype(f32), (8, width))
        summaries[i] = summary
        totals[i] = jnp.broadcast_to(
            jnp.sum(context.astype(f32), axis=0, keepdims=True), (8, width)
        )
        wide = jnp.concatenate([summary, summary], axis=0).astype(bf16)
        film[i] = dotf(wide, w_film[...])[:8]


def exact_dot(row, matrix):
    terms = split_rows(row, 3)
    stacked = jnp.concatenate(
        [term.astype(f32) for term in terms] + [jnp.zeros((13, row.shape[1]), f32)], axis=0
    )
    return jnp.sum(dotf(stacked.astype(bf16), matrix, NT), axis=0, keepdims=True)


SMALL_ROWS = QUERIES + 5 * 8


def attention_grad_kernel(
    place, sums, prompt, probs, keys, values, spread, summaries, totals, w_key, w_value, w_out, w_film,
    grad_prompt, keep, small, pair,
):
    micro, length, width = prompt.shape
    masks = head_masks(width)
    scale = 1.0 / math.sqrt(width // HEADS)
    mine, _ = halves_of(place[0], width)
    shard = grad_prompt.shape[1]
    own = pl.multiple_of(place[1] * shard, shard)
    d_query_total = jnp.zeros((QUERIES, width), f32)
    small[...] = jnp.zeros(small.shape, f32)
    for i in range(micro):
        d_film = sums[i : i + 1]
        d_mixed = exact_dot(d_film, w_film[...]) / QUERIES
        d_context = exact_dot(d_mixed, w_out[...]).astype(bf16).astype(f32)
        d_heads = jnp.concatenate(
            [d_context * mask for mask in masks] + [jnp.zeros((8, width), f32)], axis=0
        ).astype(bf16)
        d_probs = dotf(d_heads, values[i], NT)
        d_probs = jnp.concatenate(
            [jnp.broadcast_to(d_probs[h : h + 1], (QUERIES, length)) for h in range(HEADS)], axis=0
        )
        weights = probs[i]
        row_sums = jnp.sum(weights * d_probs, axis=1, keepdims=True)
        d_scores = (weights * (d_probs - row_sums)).astype(bf16)
        heads = dotf(d_scores, keys[i])
        d_query = heads[:QUERIES] * masks[0]
        for h in range(1, HEADS):
            d_query = d_query + heads[h * QUERIES : (h + 1) * QUERIES] * masks[h]
        d_query_total = d_query_total + d_query * scale
        pair[i, :, :width] = (dotf(d_scores, spread[...], TN) * scale).astype(bf16)
        wide = jnp.concatenate(
            [jnp.broadcast_to(d_context * mask, (QUERIES, width)) for mask in masks], axis=0
        ).astype(bf16)
        pair[i, :, width:] = dotf(weights.astype(bf16), wide, TN).astype(bf16)
        grad_prompt[i] = dotf(pair[i, pl.ds(own, shard), :width], w_key[...], NT) + dotf(
            pair[i, pl.ds(own, shard), width:], w_value[...], NT
        )
        rows = (summaries[i, 0:1], d_film[:, :width], d_film[:, width:], totals[i, 0:1], d_mixed)
        for k, row in enumerate(rows):
            at = QUERIES + 8 * k + i
            small[at : at + 1] = row
    small[0:QUERIES] = d_query_total
    grad = jnp.zeros((width, width), f32)
    for i in range(micro):
        grad = grad + dotf(prompt[i], pair[i, :, pl.ds(mine, width)], TN)
    keep[...] = grad


def exact_outer(left, right):
    one = [t.astype(f32) for t in split_rows(left, 3)]
    two = [t.astype(f32) for t in split_rows(right, 3)]
    picks = ((0, 0), (0, 1), (0, 2), (1, 0), (1, 1), (2, 0))
    stacked = [jnp.concatenate([side[p[k]] for p in picks], axis=0) for k, side in ((0, one), (1, two))]
    return dotf(stacked[0].astype(bf16), stacked[1].astype(bf16), TN)


def small_grad_kernel(place, packs, queries, w_query, g_queries, g_query, g_out, g_film, rows_of, queries_of):
    members, _, width = packs.shape
    member = place[2]
    shard = g_query.shape[0]
    start = pl.multiple_of(member * shard, shard)

    def group(k):
        at = QUERIES + 8 * k
        return jnp.concatenate([packs[m, at : at + 8] for m in range(members)], axis=0)

    rows_of[...] = exact_outer(
        group(0), jnp.concatenate([group(1), group(2)], axis=1)
    )
    g_film[...] = rows_of[pl.ds(start, shard)]
    rows_of[:, :width] = exact_outer(group(3), group(4))
    g_out[...] = rows_of[pl.ds(start, shard), :width]
    d_query = packs[0, 0:QUERIES]
    for m in range(1, members):
        d_query = d_query + packs[m, 0:QUERIES]
    rows_of[:, width:] = exact_outer(queries[...].astype(f32), d_query)
    g_query[...] = rows_of[pl.ds(start, shard), width:]
    terms = jnp.concatenate(split_rows(d_query, 3), axis=0)
    product = dotf(terms, w_query[...], NT)
    queries_of[...] = product[:QUERIES] + product[QUERIES : 2 * QUERIES] + product[2 * QUERIES :]
    count = g_queries.shape[0]
    for m in range(members):

        @pl.when(member == m)
        def _(m=m):
            g_queries[...] = queries_of[m * count : (m + 1) * count]


def swapped(array, axis, bit):
    count = lax.axis_size(axis)
    return lax.ppermute(array, axis, [(i, i ^ bit) for i in range(count)])


def bit_of(axis, bit):
    return (lax.axis_index(axis) // bit) % 2


def bits_of(axis):
    count = lax.axis_size(axis)
    assert count & (count - 1) == 0
    return [1 << b for b in range(count.bit_length() - 1)]


def rounded(array):
    return lax.reduce_precision(array, 8, 7)


def parted(total, axis, bit, dim):
    size = total.shape[dim] // 2
    mine = bit_of(axis, bit)
    away = lax.dynamic_slice_in_dim(total, (1 - mine) * size, size, dim).astype(bf16)
    return away, lax.dynamic_slice_in_dim(total, mine * size, size, dim)


def halvings(order):
    members = [("fsdp", bit, 1) for bit in reversed(bits_of("fsdp"))]
    second = [("tm", 2, 2)]
    return members + second if order == 0 else second + members


def doubled(mine, theirs, axis, bit, dim):
    clear = bit_of(axis, bit) == 0
    return jnp.concatenate(
        [jnp.where(clear, mine, theirs), jnp.where(clear, theirs, mine)], axis=dim
    )


def behind(array, *others):
    return lax.optimization_barrier((array, *others))[0]


def gathered(packed, members, *others):
    every = packed[None]
    for bit in bits_of("fsdp"):
        theirs = swapped(every, "fsdp", bit)
        every = theirs if members == 2 else jnp.concatenate([every, theirs], axis=0)
    here = every if members == 2 else every[1:]
    if others:
        here = behind(here, *others)
    over = swapped(here, "tm", 2)
    return here, over, swapped(here, "tm", 1), swapped(over, "tm", 1)


class Reduction:
    def __init__(self, halves):
        members = lax.axis_size("fsdp")
        self.steps = [halvings(k) for k in range(2)]
        self.totals = []
        for keeps, received in halves:
            total = jnp.concatenate(
                [k + r.astype(f32) for k, r in zip(keeps, received, strict=True)], axis=0
            )
            parts, rows, width = total.shape
            self.totals.append(total.reshape(parts, members, 2, rows // members // 2, width))
        self.depart()

    def depart(self):
        self.aways, self.kept = zip(
            *[parted(t, *s[0]) for t, s in zip(self.totals, self.steps, strict=True)], strict=True
        )

    def step(self):
        self.totals = [
            k + swapped(a, s[0][0], s[0][1]).astype(f32)
            for a, k, s in zip(self.aways, self.kept, self.steps, strict=True)
        ]
        self.steps = [s[1:] for s in self.steps]
        if self.steps[0]:
            self.depart()

    def finish(self):
        while self.steps[0]:
            self.step()
        total = jnp.concatenate(self.totals, axis=0)
        parts, rows, width = total.shape[0], total.shape[3], total.shape[4]
        total = total.reshape(parts, rows, width)
        away, kept = parted(total, "tm", 4, 1)
        total = kept + swapped(away, "tm", 4).astype(f32)
        for bit in bits_of("tm")[3:]:
            own = rounded(total)
            total = own + swapped(own.astype(bf16), "tm", bit).astype(f32)
        own = rounded(total).astype(bf16)
        for bit in (4, 2):
            own = doubled(own, swapped(own, "tm", bit), "tm", bit, 1)
        return own, swapped(own, "tm", 1)


def joined(pair, part):
    own, other = (a[part] for a in pair)
    return doubled(own, other, "tm", 1, own.ndim - 1).astype(f32)


def step_embedding(pack_steps, width):
    half_width = width // 2
    freqs = jnp.exp(jnp.arange(half_width).astype(f32) * (-math.log(10000.0) / half_width))
    angles = pack_steps.astype(f32)[:, None] * freqs[None, :]
    return jnp.concatenate([jnp.sin(angles), jnp.cos(angles)], axis=1)


def per_device(
    frames, conditioning, lengths, steps, prompt, queries, w_step, w_cond, w_conv, w_query, w_key,
    w_value, w_out, w_film, w_proj, grad_res, grad_skip,
):
    rows, width = frames.shape[2:]
    wide = 2 * width
    tile = rows // 3 if rows % 48 == 0 else rows
    tiles = (MICRO, rows // tile)
    tm_count, tm_index = lax.axis_size("tm"), lax.axis_index("tm")
    members, member = lax.axis_size("fsdp"), lax.axis_index("fsdp")
    shard_rows = w_cond.shape[0]
    shard_queries = queries.shape[0]
    frames, cond, res, skip = frames[:, 0], conditioning[:, 0], grad_res[:, 0], grad_skip[:, 0]
    core = tm_index % 2
    quarter = core * 2 + (tm_index // 2) % 2
    place = jnp.stack([core, tm_index, member, quarter]).astype(jnp.int32)
    product = 2 * MICRO * rows * width * wide

    part = shard_rows // 4

    def pack(weights, layouts, heights, name, after=()):
        return call(
            functools.partial(pack_kernel, layouts),
            (1,),
            [scalars(place)] + [hbm(w) for w in weights],
            [new_fixed((height, wide), bf16) for height in heights],
            name,
            10**5,
            scratch=[pltpu.VMEM((height, wide), f32) for height in heights]
            + [pltpu.SemaphoreType.DMA((10,))],
            after=after,
        )

    def unpack(weights, layout, quarters, name, *make):
        return call(
            functools.partial(unpack_kernel, layout, members),
            (1,),
            [scalars(place)] + [whole(w) for w in weights] + [whole(q) for q in quarters],
            [m((members * math.prod(w.shape[:-1]), w.shape[-1]), bf16) for m in make for w in weights],
            name,
            10**5,
        )

    first_weights = [w_cond, w_step]
    first_layout = [(0, 0), (part, 0)]
    second_weights = [w_key, w_value, w_query, w_out, w_film]
    second_layout = [(0, 0), (0, width), (part, 0), (part, width), (2 * part, 0)]
    third_weights = [w_conv, w_proj]
    third_layout = [(0, 0), (3 * part, 0)]
    (first,) = pack(first_weights, [first_layout], [2 * part], "pack_first")
    first_quarters = gathered(first, members)

    edge = (4, MICRO, HALO, width)
    last_rows, first_rows = call(
        edges_kernel,
        (1,),
        [hbm(a) for a in (frames, cond, res, skip)],
        [new_fixed(edge, bf16), new_fixed(edge, bf16)],
        "edges",
        10**5,
        scratch=[pltpu.SemaphoreType.DMA((8,))],
        after=[first],
    )
    low = lax.ppermute(last_rows, "tm", [(d, d + 1) for d in range(tm_count - 1)])
    high = lax.ppermute(first_rows, "tm", [(d + 1, d) for d in range(tm_count - 1)])

    utters = lengths.shape[2]
    slot = -(-utters // 32) * 32
    lane_count = 3 * 128 + 2 * MICRO * slot
    masks, mask_ends = call(
        functools.partial(masks_kernel, rows, slot, tm_count * rows),
        (1,),
        [scalars(place), scalars(lengths[:, 0])],
        [new((MICRO, rows, lane_count), bf16), new((MICRO, 2 * HALO, lane_count), bf16)],
        "masks",
        10**5,
        after=[last_rows],
    )
    own = prompt[:, 0]
    across = swapped(own, "tm", 2)
    near = jnp.stack([own, swapped(own, "tm", 1), across, swapped(across, "tm", 1)])
    second, third = pack(
        second_weights + third_weights,
        [second_layout, third_layout],
        [3 * part, 4 * part],
        "pack_rest",
        after=[masks, first_quarters[0], low, high, near],
    )

    pieces = [near] + [swapped(near, "tm", 4 * k) for k in range(1, tm_count // 4)]
    full_queries = queries.astype(bf16)
    for bit in bits_of("fsdp"):
        full_queries = doubled(full_queries, swapped(full_queries, "fsdp", bit), "fsdp", bit, 0)

    slots = jnp.pad(steps[:, 0], ((0, 0), (0, slot - utters))).reshape(-1)
    embed = step_embedding(slots, width).astype(bf16)

    full_cond, full_step = unpack(
        first_weights, first_layout, first_quarters, "unpack_first", new_fixed
    )
    hidden, gain = call(
        functools.partial(film_kernel, tile),
        tiles,
        [
            blocks(frames, tile),
            blocks(cond, tile),
            whole(low),
            whole(high),
            blocks(masks, tile),
            whole(mask_ends),
            whole(embed),
            fixed(full_step),
            fixed(full_cond),
        ],
        [
            new_fixed((MICRO, rows + 2 * HALO + 2 * DILATION, width), bf16),
            new_blocks((MICRO, rows, width), f32, tile),
        ],
        "film",
        10**5,
        scratch=[pltpu.VMEM((2 * MICRO * slot, wide), bf16)],
        after=[*pieces, full_queries],
    )

    full_key, full_value, full_query, full_out, full_film = unpack(
        second_weights, second_layout, gathered(second, members, hidden), "unpack_second", new
    )
    length = tm_count * prompt.shape[2]
    film, prompt_full, probs, keys, values, spread, summaries, totals = call(
        functools.partial(attention_kernel, len(pieces)),
        (1,),
        [scalars(place)]
        + [whole(a) for a in (*pieces, full_queries, full_query, full_key, full_value, full_out, full_film)],
        [
            new((MICRO, 8, wide)),
            new((MICRO, length, width), bf16),
            new((MICRO, HEADS * QUERIES, length)),
            new((MICRO, length, width), bf16),
            new((MICRO, length, width), bf16),
            new((HEADS * QUERIES, width), bf16),
            new((MICRO, 8, width)),
            new((MICRO, 8, width)),
        ],
        "attention",
        10**5,
    )

    full_conv, full_proj, conv_later, proj_later = unpack(
        third_weights, third_layout, gathered(third, members, hidden), "unpack_third", new_fixed, new
    )
    d_conv, d_conv_copy, gated, sums, proj_keep, proj_send = call(
        functools.partial(conv_kernel, tile),
        tiles,
        [
            scalars(place),
            fixed(hidden),
            blocks(masks, tile),
            whole(mask_ends),
            blocks(res, tile),
            blocks(skip, tile),
            whole(low),
            whole(high),
            fixed(full_conv),
            fixed(full_proj),
            whole(film),
        ],
        [
            new_fixed((MICRO, rows + 2 * HALO, wide), bf16),
            new_hbm((MICRO, rows + 2 * HALO, wide), bf16),
            new_blocks((MICRO, rows, width), bf16, tile),
            new((8, wide)),
            new((1, width, width)),
            new((1, width, width), bf16),
        ],
        "conv",
        5.5 * product,
        scratch=[
            pltpu.VMEM((width, wide), f32),
            pltpu.VMEM((8, wide), f32),
            pltpu.SemaphoreType.DMA((MICRO,)),
        ],
    )

    conv_keep, conv_send = call(
        conv_grad_kernel,
        (3,),
        [scalars(place), fixed(hidden), whole(masks), fixed(d_conv)],
        [new((3, width, width)), new((3, width, width), bf16)],
        "conv_grad",
        3 * product,
    )
    proj_received = swapped(proj_send, "tm", 1)
    conv_received = swapped(conv_send, "tm", 1)

    res_out, skip_out = call(
        out_kernel,
        tiles,
        [blocks(gated, tile), blocks(frames, tile), blocks(masks, tile), whole(proj_later)],
        [new_blocks((MICRO, rows, width), bf16, tile)] * 2,
        "outputs",
        product,
        after=[conv_send],
    )
    for bit in bits_of("tm"):
        sums = sums + swapped(sums, "tm", bit)

    conv_proj = Reduction(
        [
            ([conv_keep[:2]], [conv_received[:2]]),
            ([conv_keep[2:], proj_keep], [conv_received[2:], proj_received]),
        ]
    )
    stream = functools.partial(blocks, tile=tile)
    taps = conv_later.reshape(3, width, wide)
    window = [
        pltpu.VMEM((2, tile + 2 * DILATION, wide), bf16),
        pltpu.SemaphoreType.DMA((2,)),
    ]
    film_height = width + lane_count - 3 * 128
    grad_frames, total = call(
        functools.partial(hidden_grad_first_kernel, tile),
        (1, rows // tile),
        [hbm(d_conv_copy)] + [stream(a) for a in (masks, frames, gain, res, cond)] + [whole(taps)],
        [new_blocks((MICRO, rows, width), f32, tile), new((film_height, wide))],
        "hidden_grad_first",
        2.25 * product,
        scratch=window,
        after=[*conv_proj.aways, res_out],
    )
    grad_prompt, pair, small = call(
        attention_grad_kernel,
        (1,),
        [scalars(place)]
        + [
            whole(a)
            for a in (
                sums, prompt_full, probs, keys, values, spread, summaries, totals, full_key, full_value, full_out,
                full_film,
            )
        ],
        [new((MICRO, length // tm_count, width)), new((width, width)), new((SMALL_ROWS, width))],
        "attention_grad",
        product / 2,
        scratch=[pltpu.VMEM((MICRO, length, wide), bf16)],
    )
    conv_proj.step()
    grad_frames, keep, send = call(
        functools.partial(hidden_grad_last_kernel, tile),
        (1, rows // tile),
        [scalars(place), hbm(d_conv_copy)]
        + [stream(a, first=1) for a in (masks, frames, gain, res, cond)]
        + [whole(taps), whole(embed), whole(total), hbm(grad_frames)],
        [
            new_blocks((MICRO, rows, width), f32, tile, first=1),
            new((2, width, width)),
            new((2, width, width), bf16),
        ],
        "hidden_grad_last",
        2.25 * product,
        scratch=[pltpu.VMEM((film_height, wide), f32), *window],
        after=[*conv_proj.aways, small],
        aliases={10: 0},
    )
    received = swapped(send, "tm", 1)
    cond_step = Reduction([([keep[:1]], [received[:1]]), ([keep[1:]], [received[1:]])])

    for bit in reversed(bits_of("fsdp")):
        away, pair = parted(pair, "fsdp", bit, 0)
        pair = pair + swapped(away, "fsdp", bit).astype(f32)
    pair = rounded(pair).astype(bf16)
    pair_other = swapped(pair, "tm", 1)
    clear = bit_of("tm", 1) == 0
    grad_key = jnp.where(clear, pair, pair_other).astype(f32)
    grad_value = jnp.where(clear, pair_other, pair).astype(f32)

    packs = small[None]
    for bit in bits_of("fsdp"):
        packs = jnp.concatenate([packs, swapped(packs, "fsdp", bit)], axis=0)
    grad_queries, grad_query, grad_out, grad_film = call(
        small_grad_kernel,
        (1,),
        [scalars(place), whole(packs), whole(full_queries), whole(full_query)],
        [
            new((shard_queries, width)),
            new((shard_rows, width)),
            new((shard_rows, width)),
            new((shard_rows, wide)),
        ],
        "small_grads",
        product / 10,
        scratch=[pltpu.VMEM((width, wide), f32), pltpu.VMEM((QUERIES, width), f32)],
    )

    conv_proj = conv_proj.finish()
    cond_step = cond_step.finish()
    return (
        res_out[:, None],
        skip_out[:, None],
        grad_frames[:, None],
        grad_prompt[:, None],
        grad_queries,
        joined(cond_step, 1),
        joined(cond_step, 0),
        joined(conv_proj, slice(0, 3)),
        grad_query,
        grad_key,
        grad_value,
        grad_out,
        grad_film,
        joined(conv_proj, 3),
    )


def solution(mesh):
    packed = P(None, "fsdp", "tm", None)
    short = P(None, "fsdp", None)
    weight = P("fsdp", None)
    taps = P(None, "fsdp", None)
    in_specs = (packed, packed, short, short, packed) + (weight,) * 3 + (taps,) + (weight,) * 6 + (packed,) * 2
    out_specs = (packed,) * 4 + (weight,) * 3 + (taps,) + (weight,) * 6
    return jax.shard_map(
        per_device, mesh=mesh, in_specs=in_specs, out_specs=out_specs, check_vma=False
    )
```

```python
import functools
import math

import jax
import jax.numpy as jnp
from jax import lax
from jax.experimental import pallas as pl
from jax.experimental.pallas import tpu as pltpu
from jax.sharding import PartitionSpec as P

HEADS = 8
QUERIES = 32
DILATION = 16
MICRO = 2
HALO = 2 * DILATION

SQRT_HALF = 0.7071067811865476
VMEM_LIMIT = 40 * 2**20
NT = ((1,), (1,))
TN = ((0,), (0,))
bf16 = jnp.bfloat16
f32 = jnp.float32


def dotf(left, right, dims=((1,), (0,))):
    return lax.dot_general(left, right, (dims, ((), ())), preferred_element_type=f32)


def lanes(block, width):
    return jnp.concatenate([block] * (width // block.shape[1]), axis=1)


VSPEC = pl.BlockSpec(memory_space=pltpu.VMEM)
SSPEC = pl.BlockSpec(memory_space=pltpu.SMEM)
ANYSPEC = pl.BlockSpec(memory_space=pl.ANY)


def fixed(array):
    return pltpu.with_memory_space_constraint(array, pltpu.VMEM), VSPEC


def whole(array):
    return pltpu.with_memory_space_constraint(array, pltpu.HBM), pl.BlockSpec(array.shape, lambda *_: (0,) * array.ndim)


def blocks(array, tile, first=0):
    return pltpu.with_memory_space_constraint(array, pltpu.HBM), pl.BlockSpec(
        (1, tile, array.shape[2]), lambda i, j: (i + first, j, 0)
    )


def hbm(array):
    return pltpu.with_memory_space_constraint(array, pltpu.HBM), pl.BlockSpec(memory_space=pltpu.HBM)


def scalars(array):
    return array, SSPEC


def call(kernel, grid, ins, outs, name, micros, scratch=(), after=(), aliases=None):
    count, waits = len(ins), len(after)

    def body(*refs):
        kernel(*refs[:count], *refs[count + waits :])

    return pl.pallas_call(
        body,
        grid=grid,
        in_specs=[spec for _, spec in ins] + [ANYSPEC] * waits,
        out_specs=[spec for _, spec in outs],
        out_shape=[out for out, _ in outs],
        scratch_shapes=scratch,
        input_output_aliases=aliases or {},
        cost_estimate=pl.CostEstimate(
            flops=int(micros * 1e9), bytes_accessed=2**12, transcendentals=0
        ),
        compiler_params=pltpu.CompilerParams(vmem_limit_bytes=VMEM_LIMIT),
        name=name,
    )(*[array for array, _ in ins], *after)


def new(shape, kind=f32):
    return pltpu.HBM(shape, kind), pl.BlockSpec(shape, lambda *_: (0,) * len(shape))


def new_fixed(shape, kind=f32):
    return pltpu.VMEM(shape, kind), VSPEC


def new_hbm(shape, kind=f32):
    return pltpu.HBM(shape, kind), pl.BlockSpec(memory_space=pltpu.HBM)


def new_blocks(shape, kind, tile, first=0):
    return pltpu.HBM(shape, kind), pl.BlockSpec(
        (1, tile, shape[2]), lambda i, j: (i + first, j, 0)
    )


def split_rows(row, parts):
    terms = []
    for _ in range(parts):
        term = row.astype(bf16)
        terms.append(term)
        row = row - term.astype(f32)
    return terms


def pack_kernel(layouts, place, *refs):
    count = sum(len(layout) - 1 for layout in layouts)
    weights, refs = list(refs[:count]), refs[count:]
    outs, helds, sems = refs[: len(layouts)], refs[len(layouts) : -1], refs[-1]
    copies = []
    for (which, *layout), held in zip(layouts, helds, strict=True):
        for row, column, *tap in layout:
            weight = weights.pop(0)
            view = weight.at[tap[0]] if tap else weight
            rows = view.shape[0] // 4
            start = pl.multiple_of(place[which] * rows, rows)
            copies.append(
                pltpu.make_async_copy(
                    view.at[pl.ds(start, rows)],
                    held.at[pl.ds(row, rows), pl.ds(column, view.shape[1])],
                    sems.at[len(copies)],
                )
            )
    for copy in copies:
        copy.start()
    for copy in copies:
        copy.wait()
    for out, held in zip(outs, helds, strict=True):
        out[...] = held[...].astype(bf16)


def edges_kernel(*refs):
    arrays, (last, first, sems) = refs[:-3], refs[-3:]
    copies = []
    for k, array in enumerate(arrays):
        rows = array.shape[1]
        copies.append(
            pltpu.make_async_copy(array.at[:, pl.ds(rows - HALO, HALO)], last.at[k], sems.at[2 * k])
        )
        copies.append(
            pltpu.make_async_copy(array.at[:, pl.ds(0, HALO)], first.at[k], sems.at[2 * k + 1])
        )
    for copy in copies:
        copy.start()
    for copy in copies:
        copy.wait()


def own_kernel(*refs):
    count = len(refs) // 2
    for shard, low in zip(refs[:count], refs[count:], strict=True):
        low[...] = shard[...].astype(bf16)


def assemble(place, members, layout, shards, sources, fulls):
    member = place[2]
    for shard, full, (row, column) in zip(shards, fulls, layout, strict=True):
        rows, width = shard.shape
        part = rows // 4
        full[pl.ds(pl.multiple_of(member * rows, part), rows)] = shard[...]
        for j in range(1, members):
            for source, quarter in sources:
                start = pl.multiple_of((member ^ j) * rows + quarter * part, part)
                full[pl.ds(start, part)] = source[j - 1, row : row + part, column : column + width]


def quarters_of(place, arrays, which=3):
    return [(array, place[which] ^ k) for k, array in enumerate(arrays)]


def masks_kernel(rows, slot, total, place, lengths, masks, hot, ends, hot_ends):
    micro, utters = lengths.shape
    hots = hot.shape[2]
    lane = lax.broadcasted_iota(jnp.int32, (1, hots), 1)
    lane = jnp.where(lane >= micro * slot, lane - micro * slot, lane)
    row = lax.broadcasted_iota(jnp.int32, (hots, 128), 0)
    count = jnp.where(row < micro * slot, 1.0, 0.0).astype(bf16)
    first = place[1] * rows - HALO
    chunk = rows // 6
    for i in range(micro):
        opens = jnp.full((1, hots), total, jnp.int32)
        closes = jnp.zeros((1, hots), jnp.int32)
        end = jnp.int32(0)
        for u in range(utters):
            mine = lane == i * slot + u
            if u == utters - 1:
                alive_until = end
            opens = jnp.where(mine, end, opens)
            end = end + lengths[i, u]
            closes = jnp.where(mine, end, closes)

        def rows_of(start, size, i=i, opens=opens, closes=closes, alive_until=alive_until):
            position = lax.broadcasted_iota(jnp.int32, (size, hots), 0) + start

            def one_hot(offset):
                shifted = position + offset
                return jnp.where((shifted >= opens) & (shifted < closes), 1.0, 0.0).astype(bf16)

            here = one_hot(0)
            low = dotf(here * one_hot(-DILATION), count).astype(bf16)
            high = dotf(here * one_hot(DILATION), count).astype(bf16)
            alive = (position[:, :128] < alive_until) & (position[:, :128] >= 0)
            alive = jnp.where(alive, 1.0, 0.0).astype(bf16)
            return jnp.concatenate([low, high, alive], axis=1), here

        ends[i, 0:HALO], hot_ends[i, 0:HALO] = rows_of(first, HALO)
        ends[i, HALO:], hot_ends[i, HALO:] = rows_of(first + HALO + rows, HALO)

        @pl.loop(0, rows // chunk)
        def _(k, i=i, rows_of=rows_of):
            at = pl.multiple_of(k * chunk, chunk)
            some, here = rows_of(first + HALO + at, chunk)
            masks[i, pl.ds(at, chunk)] = some
            hot[i, pl.ds(at, chunk)] = here


def film_kernel(
    tile, members, layout, place, frames, cond, low, high, hots, hot_ends, embed, own_cond, own_step, here, over, core, both,
    hidden, gain_cond, gain_step, w_cond, w_step, film_rows,
):
    i, j = pl.program_id(0), pl.program_id(1)
    width = frames.shape[2]
    rows = hidden.shape[1] - 2 * HALO - 2 * DILATION

    @pl.when((i == 0) & (j == 0))
    def _():
        sources = quarters_of(place, (here, over, core, both))
        assemble(place, members, layout, (own_cond, own_step), sources, (w_cond, w_step))
        step_film = dotf(embed[...], w_step[...])
        film_rows[...] = jnp.concatenate(split_rows(step_film, 2), axis=0)
        gain_cond[...] = w_cond[:, :width]
        gain_step[...] = film_rows[:, :width]

    def film(frame_rows, cond_rows, hot):
        both = dotf(cond_rows, w_cond[...]) + dotf(hot, film_rows[...])
        return (frame_rows.astype(f32) * (1.0 + both[:, :width]) + both[:, width:]).astype(bf16)

    @pl.when(j == 0)
    def _():
        edge = film(
            jnp.concatenate([low[0, i], high[0, i]], axis=0),
            jnp.concatenate([low[1, i], high[1, i]], axis=0),
            hot_ends[i],
        )
        nothing = jnp.zeros((DILATION, width), bf16)
        hidden[i, 0:DILATION] = nothing
        hidden[i, DILATION : DILATION + HALO] = edge[:HALO]
        hidden[i, DILATION + HALO + rows : DILATION + 2 * HALO + rows] = edge[HALO:]
        hidden[i, DILATION + 2 * HALO + rows :] = nothing

    base = pl.multiple_of(j * tile, tile)
    hidden[i, pl.ds(DILATION + HALO + base, tile)] = film(frames[0], cond[0], hots[0])


def halves_of(core, width):
    mine = pl.multiple_of(core * width, width)
    other = pl.multiple_of((1 - core) * width, width)
    return mine, other


def conv_kernel(
    tile, members, layout, place, hidden, masks, mask_ends, frames, res, skip, low, high, film, own_conv, own_proj,
    here, over, core, both,
    d_conv, d_conv_copy, conv_copy, sums, keep, send, res_out, skip_out,
    w_conv, w_proj, proj_total, columns, sems,
):
    i, j = pl.program_id(0), pl.program_id(1)
    width = res.shape[2]
    rows = d_conv.shape[1] - 2 * HALO
    gain, shift = 1.0 + film[i, 0:1, :width], film[i, 0:1, width:]
    first = (i == 0) & (j == 0)
    weights_away = pltpu.make_async_copy(w_conv, conv_copy, sems.at[2])

    @pl.when(first)
    def _():
        shard = own_proj.shape[0]
        own = [own_conv.at[pl.ds(t * shard, shard)] for t in range(3)]
        full = [w_conv.at[pl.ds(t * width, width)] for t in range(3)]
        sources = quarters_of(place, (here, over, core, both), 4)
        assemble(place, members, layout, [*own, own_proj], sources, [*full, w_proj])
        weights_away.start()
        sums[...] = jnp.zeros(sums.shape, f32)

    def body(before, now, later, keep_low, keep_high, alive, res_rows, skip_rows):
        taps = jnp.concatenate(
            [before * lanes(keep_low, width), now, later * lanes(keep_high, width)], axis=1
        )
        conv = dotf(taps, w_conv[...])
        th = jnp.tanh(conv[:, :width])
        sg = 0.5 + 0.5 * jnp.tanh(0.5 * conv[:, width:])
        alive = lanes(alive.astype(f32), width)
        branch = jnp.concatenate(
            [
                (res_rows.astype(f32) * (SQRT_HALF * alive)).astype(bf16),
                (skip_rows.astype(f32) * alive).astype(bf16),
            ],
            axis=1,
        )
        d_gated = dotf(branch, w_proj[...], NT)
        act = th * sg
        d_act = d_gated * gain
        left = (d_act * sg * (1.0 - th * th)).astype(bf16)
        right = (d_act * act * (1.0 - sg)).astype(bf16)
        return act, d_gated, branch, alive, left, right

    @pl.when(j == 0)
    def _():
        def ends(ref, at):
            return jnp.concatenate(
                [ref[i, at : at + HALO], ref[i, at + HALO + rows : at + 2 * HALO + rows]], axis=0
            )

        *_, left, right = body(
            ends(hidden, 0),
            ends(hidden, DILATION),
            ends(hidden, 2 * DILATION),
            mask_ends[i, :, 0:128],
            mask_ends[i, :, 128:256],
            mask_ends[i, :, 256:384],
            jnp.concatenate([low[2, i], high[2, i]], axis=0),
            jnp.concatenate([low[3, i], high[3, i]], axis=0),
        )
        d_conv[i, 0:HALO, :width] = left[:HALO]
        d_conv[i, 0:HALO, width:] = right[:HALO]
        d_conv[i, HALO + rows :, :width] = left[HALO:]
        d_conv[i, HALO + rows :, width:] = right[HALO:]
        columns[...] = jnp.zeros(columns.shape, f32)

    base = pl.multiple_of(j * tile, tile)

    def at(ref, offset):
        return ref[i, pl.ds(base + offset, tile)]

    act, d_gated, branch, alive, left, right = body(
        at(hidden, HALO),
        at(hidden, HALO + DILATION),
        at(hidden, HALO + 2 * DILATION),
        masks[0, :, 0:128],
        masks[0, :, 128:256],
        masks[0, :, 256:384],
        res[0],
        skip[0],
    )
    d_conv[i, pl.ds(base + HALO, tile), :width] = left
    d_conv[i, pl.ds(base + HALO, tile), width:] = right
    gated_rows = (act * gain + shift).astype(bf16)
    columns[:, :width] += jnp.sum((d_gated * act).reshape(tile // 8, 8, width), axis=0)
    columns[:, width:] += jnp.sum(d_gated.reshape(tile // 8, 8, width), axis=0)
    part = dotf(gated_rows, branch, TN)
    out = dotf(gated_rows, w_proj[...])
    res_out[0] = ((frames[0].astype(f32) + out[:, :width]) * (SQRT_HALF * alive)).astype(bf16)
    skip_out[0] = (out[:, width:] * alive).astype(bf16)

    @pl.when(first)
    def _():
        proj_total[...] = part

    @pl.when(jnp.logical_not(first))
    def _():
        proj_total[...] += part

    last = j == rows // tile - 1
    copies = [
        pltpu.make_async_copy(d_conv.at[m], d_conv_copy.at[m], sems.at[m]) for m in range(MICRO)
    ]
    for m in range(MICRO):
        pl.when(last & (i == m))(copies[m].start)

        @pl.when(last & (i == m))
        def _(m=m):
            sums[m : m + 1] = jnp.sum(columns[...], axis=0, keepdims=True)

    @pl.when(last & (i == MICRO - 1))
    def _():
        mine, other = halves_of(place[0], width)
        send[0] = proj_total[:, pl.ds(other, width)].astype(bf16)
        keep[0] = proj_total[:, pl.ds(mine, width)]
        for copy in (*copies, weights_away):
            copy.wait()


def conv_grad_kernel(place, hidden, masks, d_conv, keep, send):
    t = pl.program_id(0)
    micro, width = hidden.shape[0], hidden.shape[2]
    rows = d_conv.shape[1] - 2 * HALO
    mine, other = halves_of(place[0], width)

    for tap, lane in ((0, 0), (1, None), (2, 128)):

        @pl.when(t == tap)
        def _(tap=tap, lane=lane):
            def tap_rows(i):
                part = hidden[i, HALO + DILATION * tap : HALO + DILATION * tap + rows]
                return part if lane is None else part * lanes(masks[i, :, lane : lane + 128], width)

            for columns, ref in ((other, send), (mine, keep)):
                total = dotf(tap_rows(0), d_conv[0, HALO : HALO + rows, pl.ds(columns, width)], TN)
                for i in range(1, micro):
                    total = total + dotf(
                        tap_rows(i), d_conv[i, HALO : HALO + rows, pl.ds(columns, width)], TN
                    )
                ref[tap] = total.astype(ref.dtype)


def hidden_grad_kernel(
    tile, place, d_conv, masks, hots, frames, res, cond, w_conv, gain_cond, gain_step, embed,
    grad_frames, keep, send, total, window, sems,
):
    i, j = pl.program_id(0), pl.program_id(1)
    steps = pl.num_programs(1)
    width = frames.shape[2]
    now = i * steps + j

    def fetch(step):
        start = pl.multiple_of(HALO - DILATION + (step % steps) * tile, DILATION)
        return pltpu.make_async_copy(
            d_conv.at[step // steps, pl.ds(start, tile + 2 * DILATION)],
            window.at[step % 2],
            sems.at[step % 2],
        )

    @pl.when(now == 0)
    def _():
        fetch(0).start()

    @pl.when(now + 1 < MICRO * steps)
    def _():
        fetch(now + 1).start()

    gain = dotf(cond[0], gain_cond[...]) + dotf(hots[0], gain_step[...])
    fetch(now).wait()
    slot = now % 2
    d_hidden = (
        dotf(window[slot, 2 * DILATION :] * lanes(masks[0, :, 128:256], 2 * width), w_conv[0], NT)
        + dotf(window[slot, DILATION : DILATION + tile], w_conv[1], NT)
        + dotf(window[slot, 0:tile] * lanes(masks[0, :, 0:128], 2 * width), w_conv[2], NT)
    )
    alive = lanes(masks[0, :, 256:384].astype(f32), width)
    grad_frames[0] = res[0].astype(f32) * (SQRT_HALF * alive) + d_hidden * (1.0 + gain)
    d_film = jnp.concatenate(
        [(d_hidden * frames[0].astype(f32)).astype(bf16), d_hidden.astype(bf16)], axis=1
    )
    part = dotf(jnp.concatenate([cond[0], hots[0]], axis=1), d_film, TN)

    @pl.when(now == 0)
    def _():
        total[...] = part

    @pl.when(now > 0)
    def _():
        total[...] += part

    @pl.when(now == MICRO * steps - 1)
    def _():
        mine, other = halves_of(place[0], width)
        count = embed.shape[0]
        for columns, ref in ((other, send), (mine, keep)):
            ref[0] = total[:width, pl.ds(columns, width)].astype(ref.dtype)
            d_step = total[width : width + count, pl.ds(columns, width)]
            step = jnp.zeros((width, width), f32)
            for term in split_rows(d_step, 3):
                step = step + dotf(embed[...], term, TN)
            ref[1] = step.astype(ref.dtype)


def head_masks(width):
    column = lax.broadcasted_iota(jnp.int32, (1, width), 1)
    size = width // HEADS
    return [((column >= h * size) & (column < (h + 1) * size)).astype(f32) for h in range(HEADS)]


def attention_kernel(groups, members, layout, place, *refs):
    pieces = refs[:groups]
    queries, *parts = refs[groups : groups + 10]
    film, prompt, probs, keys, values, spread, summaries, totals, *fulls = refs[groups + 10 :]
    assemble(place, members, layout, parts[:5], quarters_of(place, parts[5:]), fulls)
    w_key, w_value, w_query, w_out, w_film = fulls
    _, micro, shard, width = pieces[0].shape
    masks = head_masks(width)
    scale = 1.0 / math.sqrt(width // HEADS)
    for g, four in enumerate(pieces):
        for k in range(4):
            start = pl.multiple_of((place[1] ^ (4 * g + k)) * shard, shard)
            for i in range(micro):
                prompt[i, pl.ds(start, shard)] = four[k, i]
    query = dotf(queries[...], w_query[...])
    spread[...] = jnp.concatenate([(query * mask).astype(bf16) for mask in masks], axis=0)
    for i in range(micro):
        keys[i] = dotf(prompt[i], w_key[...]).astype(bf16)
        values[i] = dotf(prompt[i], w_value[...]).astype(bf16)
        scores = dotf(spread[...], keys[i], NT) * scale
        weights = jnp.exp(scores - jnp.max(scores, axis=1, keepdims=True))
        weights = weights / jnp.sum(weights, axis=1, keepdims=True)
        probs[i] = weights
        heads = dotf(weights.astype(bf16), values[i])
        context = heads[:QUERIES] * masks[0]
        for h in range(1, HEADS):
            context = context + heads[h * QUERIES : (h + 1) * QUERIES] * masks[h]
        context = context.astype(bf16)
        mixed = dotf(context, w_out[...])
        summary = jnp.mean(mixed, axis=0, keepdims=True).astype(bf16)
        summary = jnp.broadcast_to(summary.astype(f32), (8, width))
        summaries[i] = summary
        totals[i] = jnp.broadcast_to(
            jnp.sum(context.astype(f32), axis=0, keepdims=True), (8, width)
        )
        wide = jnp.concatenate([summary, summary], axis=0).astype(bf16)
        film[i] = dotf(wide, w_film[...])[:8]


def exact_dot(row, matrix):
    terms = split_rows(row, 3)
    stacked = jnp.concatenate(
        [term.astype(f32) for term in terms] + [jnp.zeros((13, row.shape[1]), f32)], axis=0
    )
    return jnp.sum(dotf(stacked.astype(bf16), matrix, NT), axis=0, keepdims=True)


SMALL_ROWS = QUERIES + 5 * 8


def attention_grad_kernel(
    place, sums, prompt, probs, keys, values, spread, summaries, totals, w_key, w_value, w_out, w_film,
    grad_prompt, keep, small, pair,
):
    micro, length, width = prompt.shape
    masks = head_masks(width)
    scale = 1.0 / math.sqrt(width // HEADS)
    mine, _ = halves_of(place[0], width)
    shard = grad_prompt.shape[1]
    own = pl.multiple_of(place[1] * shard, shard)
    d_query_total = jnp.zeros((QUERIES, width), f32)
    small[...] = jnp.zeros(small.shape, f32)
    for i in range(micro):
        d_film = sums[i : i + 1]
        d_mixed = exact_dot(d_film, w_film[...]) / QUERIES
        d_context = exact_dot(d_mixed, w_out[...]).astype(bf16).astype(f32)
        d_heads = jnp.concatenate(
            [d_context * mask for mask in masks] + [jnp.zeros((8, width), f32)], axis=0
        ).astype(bf16)
        d_probs = dotf(d_heads, values[i], NT)
        d_probs = jnp.concatenate(
            [jnp.broadcast_to(d_probs[h : h + 1], (QUERIES, length)) for h in range(HEADS)], axis=0
        )
        weights = probs[i]
        row_sums = jnp.sum(weights * d_probs, axis=1, keepdims=True)
        d_scores = (weights * (d_probs - row_sums)).astype(bf16)
        heads = dotf(d_scores, keys[i])
        d_query = heads[:QUERIES] * masks[0]
        for h in range(1, HEADS):
            d_query = d_query + heads[h * QUERIES : (h + 1) * QUERIES] * masks[h]
        d_query_total = d_query_total + d_query * scale
        pair[i, :, :width] = (dotf(d_scores, spread[...], TN) * scale).astype(bf16)
        wide = jnp.concatenate(
            [jnp.broadcast_to(d_context * mask, (QUERIES, width)) for mask in masks], axis=0
        ).astype(bf16)
        pair[i, :, width:] = dotf(weights.astype(bf16), wide, TN).astype(bf16)
        grad_prompt[i] = dotf(pair[i, pl.ds(own, shard), :width], w_key[...], NT) + dotf(
            pair[i, pl.ds(own, shard), width:], w_value[...], NT
        )
        rows = (summaries[i, 0:1], d_film[:, :width], d_film[:, width:], totals[i, 0:1], d_mixed)
        for k, row in enumerate(rows):
            at = QUERIES + 8 * k + i
            small[at : at + 1] = row
    small[0:QUERIES] = d_query_total
    grad = jnp.zeros((width, width), f32)
    for i in range(micro):
        grad = grad + dotf(prompt[i], pair[i, :, pl.ds(mine, width)], TN)
    keep[...] = grad


def exact_outer(left, right):
    one = [t.astype(f32) for t in split_rows(left, 3)]
    two = [t.astype(f32) for t in split_rows(right, 3)]
    picks = ((0, 0), (0, 1), (0, 2), (1, 0), (1, 1), (2, 0))
    stacked = [jnp.concatenate([side[p[k]] for p in picks], axis=0) for k, side in ((0, one), (1, two))]
    return dotf(stacked[0].astype(bf16), stacked[1].astype(bf16), TN)


def small_grad_kernel(place, packs, queries, w_query, g_queries, g_query, g_out, g_film, rows_of, queries_of):
    members, _, width = packs.shape
    member = place[2]
    shard = g_query.shape[0]
    start = pl.multiple_of(member * shard, shard)

    def group(k):
        at = QUERIES + 8 * k
        return jnp.concatenate([packs[m, at : at + 8] for m in range(members)], axis=0)

    rows_of[...] = exact_outer(
        group(0), jnp.concatenate([group(1), group(2)], axis=1)
    )
    g_film[...] = rows_of[pl.ds(start, shard)]
    rows_of[:, :width] = exact_outer(group(3), group(4))
    g_out[...] = rows_of[pl.ds(start, shard), :width]
    d_query = packs[0, 0:QUERIES]
    for m in range(1, members):
        d_query = d_query + packs[m, 0:QUERIES]
    rows_of[:, width:] = exact_outer(queries[...].astype(f32), d_query)
    g_query[...] = rows_of[pl.ds(start, shard), width:]
    terms = jnp.concatenate(split_rows(d_query, 3), axis=0)
    product = dotf(terms, w_query[...], NT)
    queries_of[...] = product[:QUERIES] + product[QUERIES : 2 * QUERIES] + product[2 * QUERIES :]
    count = g_queries.shape[0]
    for m in range(members):

        @pl.when(member == m)
        def _(m=m):
            g_queries[...] = queries_of[m * count : (m + 1) * count]


def swapped(array, axis, bit):
    count = lax.axis_size(axis)
    return lax.ppermute(array, axis, [(i, i ^ bit) for i in range(count)])


def bit_of(axis, bit):
    return (lax.axis_index(axis) // bit) % 2


def bits_of(axis):
    count = lax.axis_size(axis)
    assert count & (count - 1) == 0
    return [1 << b for b in range(count.bit_length() - 1)]


def rounded(array):
    return lax.reduce_precision(array, 8, 7)


def parted(total, axis, bit, dim):
    size = total.shape[dim] // 2
    mine = bit_of(axis, bit)
    away = lax.dynamic_slice_in_dim(total, (1 - mine) * size, size, dim).astype(bf16)
    return away, lax.dynamic_slice_in_dim(total, mine * size, size, dim)


def halvings(order):
    members = [("fsdp", bit, 1) for bit in reversed(bits_of("fsdp"))]
    second = [("tm", 2, 2)]
    return members + second if order == 0 else second + members


def doubled(mine, theirs, axis, bit, dim):
    clear = bit_of(axis, bit) == 0
    return jnp.concatenate(
        [jnp.where(clear, mine, theirs), jnp.where(clear, theirs, mine)], axis=dim
    )


def behind(array, *others):
    return lax.optimization_barrier((array, *others))[0]


def gathered(packed, members, early=(), late=(), bit_2=2):
    every = packed[None]
    for bit in bits_of("fsdp"):
        theirs = swapped(every, "fsdp", bit)
        every = theirs if members == 2 else jnp.concatenate([every, theirs], axis=0)
    here = every if members == 2 else every[1:]
    if early:
        here = behind(here, *early)
    over = swapped(here, "tm", bit_2)
    if late:
        over = behind(over, *late)
    return here, over, swapped(here, "tm", 1), swapped(over, "tm", 1)


class Reduction:
    def __init__(self, halves):
        members = lax.axis_size("fsdp")
        self.steps = [halvings(k) for k in range(2)]
        self.totals = []
        for keeps, received in halves:
            total = jnp.concatenate(
                [k + r.astype(f32) for k, r in zip(keeps, received, strict=True)], axis=0
            )
            parts, rows, width = total.shape
            self.totals.append(total.reshape(parts, members, 2, rows // members // 2, width))
        self.send()

    def send(self):
        pairs = [parted(t, *s[0]) for t, s in zip(self.totals, self.steps, strict=True)]
        self.aways, self.kept = zip(*pairs, strict=True)
        self.raw = [swapped(a, *s[0][:2]) for a, s in zip(self.aways, self.steps, strict=True)]

    def absorb(self, *others):
        self.totals = [
            k + behind(r, *others).astype(f32) for k, r in zip(self.kept, self.raw, strict=True)
        ]
        self.steps = [s[1:] for s in self.steps]
        if self.steps[0]:
            self.send()

    def absorb_all(self, *others):
        while self.steps[0]:
            self.absorb(*others)

    def start_third(self):
        total = jnp.concatenate(self.totals, axis=0)
        total = total.reshape(total.shape[0], total.shape[3], total.shape[4])
        self.away, self.own = parted(total, "tm", 4, 1)
        self.raw = swapped(self.away, "tm", 4)

    def fold(self, *others):
        self.total = self.own + behind(self.raw, *others).astype(f32)

    def start_double(self, bit):
        self.own = rounded(self.total)
        self.away = self.own.astype(bf16)
        self.raw = swapped(self.away, "tm", bit)

    def start_gather(self):
        self.away = rounded(self.total).astype(bf16)
        self.raw = [swapped(self.away, "tm", bits) for bits in (4, 2, 6)]

    def gather(self):
        clear = bit_of("tm", 4) == 0
        pairs = []
        for one, two in ((self.away, self.raw[0]), (self.raw[1], self.raw[2])):
            pairs.append([jnp.where(clear, one, two), jnp.where(clear, two, one)])
        clear = bit_of("tm", 2) == 0
        rows = [jnp.where(clear, a, b) for a, b in zip(pairs[0] + pairs[1], pairs[1] + pairs[0], strict=True)]
        own = jnp.concatenate(rows, axis=1)
        return own, swapped(own, "tm", 1)


def join_kernel(place, own, other, *outs):
    width = own.shape[2]
    mine, theirs = halves_of(place[0], width)
    first = 0
    for out in outs:
        for source, columns in ((own, mine), (other, theirs)):
            if len(out.shape) == 2:
                out[:, pl.ds(columns, width)] = source[first].astype(f32)
            else:
                count = out.shape[0]
                out[:, :, pl.ds(columns, width)] = source[first : first + count].astype(f32)
        first += 1 if len(out.shape) == 2 else out.shape[0]


def step_embedding(pack_steps, width):
    half_width = width // 2
    freqs = jnp.exp(jnp.arange(half_width).astype(f32) * (-math.log(10000.0) / half_width))
    angles = pack_steps.astype(f32)[:, None] * freqs[None, :]
    return jnp.concatenate([jnp.sin(angles), jnp.cos(angles)], axis=1)


def per_device(
    frames, conditioning, lengths, steps, prompt, queries, w_step, w_cond, w_conv, w_query, w_key,
    w_value, w_out, w_film, w_proj, grad_res, grad_skip,
):
    rows, width = frames.shape[2:]
    wide = 2 * width
    tile = rows // 3 if rows % 48 == 0 else rows
    tiles = (MICRO, rows // tile)
    tm_count, tm_index = lax.axis_size("tm"), lax.axis_index("tm")
    members, member = lax.axis_size("fsdp"), lax.axis_index("fsdp")
    shard_rows = w_cond.shape[0]
    shard_queries = queries.shape[0]
    frames, cond, res, skip = frames[:, 0], conditioning[:, 0], grad_res[:, 0], grad_skip[:, 0]
    core = tm_index % 2
    quarter = core * 2 + (tm_index // 2) % 2
    other_quarter = core * 2 + (tm_index // 4) % 2
    place = jnp.stack([core, tm_index, member, quarter, other_quarter]).astype(jnp.int32)

    part = shard_rows // 4

    def pack(weights, layouts, heights, name, after=()):
        return call(
            functools.partial(pack_kernel, layouts),
            (1,),
            [scalars(place)] + [hbm(w) for w in weights],
            [new_fixed((height, wide), bf16) for height in heights],
            name,
            2,
            scratch=[pltpu.VMEM((height, wide), f32) for height in heights]
            + [pltpu.SemaphoreType.DMA((10,))],
            after=after,
        )

    layout_1 = [(0, 0), (part, 0)]
    layout_2 = [(0, 0), (0, width), (part, 0), (part, width), (2 * part, 0)]
    layout_3 = [(k * part, 0) for k in range(4)]
    taps_3 = [4, (0, 0, 0), (part, 0, 1), (2 * part, 0, 2), (3 * part, 0)]
    (first,) = pack([w_cond, w_step], [[3, *layout_1]], [2 * part], "pack_first")

    edge = (4, MICRO, HALO, width)
    last_rows, first_rows = call(
        edges_kernel,
        (1,),
        [hbm(a) for a in (frames, cond, res, skip)],
        [new_fixed(edge, bf16), new_fixed(edge, bf16)],
        "edges",
        1.1,
        scratch=[pltpu.SemaphoreType.DMA((8,))],
        after=[first],
    )
    low = lax.ppermute(last_rows, "tm", [(d, d + 1) for d in range(tm_count - 1)])
    high = lax.ppermute(first_rows, "tm", [(d + 1, d) for d in range(tm_count - 1)])

    second, third = pack(
        [w_key, w_value, w_query, w_out, w_film, w_conv, w_conv, w_conv, w_proj],
        [[3, *layout_2], taps_3],
        [3 * part, 4 * part],
        "pack_rest",
        after=[last_rows],
    )
    utters = lengths.shape[2]
    slot = -(-utters // 32) * 32
    hots = 2 * MICRO * slot
    masks, hot, mask_ends, hot_ends = call(
        functools.partial(masks_kernel, rows, slot, tm_count * rows),
        (1,),
        [scalars(place), scalars(lengths[:, 0])],
        [new((MICRO, n, lane), bf16) for n in (rows, 2 * HALO) for lane in (384, hots)],
        "masks",
        5,
        after=[second],
    )
    own = prompt[:, 0]
    across = swapped(own, "tm", 2)
    near = jnp.stack([own, swapped(own, "tm", 1), across, swapped(across, "tm", 1)])
    own_cond, own_step, *own_second, own_conv, own_proj = call(
        own_kernel,
        (1,),
        [
            whole(w)
            for w in (w_cond, w_step, w_key, w_value, w_query, w_out, w_film, w_conv.reshape(-1, wide), w_proj)
        ],
        [new_fixed(w.shape, bf16) for w in (w_cond, w_step)]
        + [
            new(w.shape, bf16)
            for w in (w_key, w_value, w_query, w_out, w_film, w_conv.reshape(-1, wide), w_proj)
        ],
        "own_shards",
        4,
        after=[mask_ends, near],
    )
    first_quarters = gathered(first, members, early=[mask_ends], late=[own_cond])
    pieces = [near] + [swapped(near, "tm", 4 * k) for k in range(1, tm_count // 4)]
    full_queries = queries.astype(bf16)
    for bit in bits_of("fsdp"):
        full_queries = doubled(full_queries, swapped(full_queries, "fsdp", bit), "fsdp", bit, 0)

    slots = jnp.pad(steps[:, 0], ((0, 0), (0, slot - utters))).reshape(-1)
    embed = step_embedding(slots, width).astype(bf16)

    hidden, gain_cond, gain_step = call(
        functools.partial(film_kernel, tile, members, layout_1),
        tiles,
        [
            scalars(place),
            blocks(frames, tile),
            blocks(cond, tile),
            whole(low),
            whole(high),
            blocks(hot, tile),
            whole(hot_ends),
            whole(embed),
            fixed(own_cond),
            fixed(own_step),
            *[fixed(q) for q in first_quarters],
        ],
        [
            new_fixed((MICRO, rows + 2 * HALO + 2 * DILATION, width), bf16),
            new((width, width), bf16),
            new((hots, width), bf16),
        ],
        "film",
        10,
        scratch=[
            pltpu.VMEM((width, wide), bf16),
            pltpu.VMEM((width, wide), bf16),
            pltpu.VMEM((hots, wide), bf16),
        ],
        after=[*pieces, full_queries],
    )
    second_quarters = gathered(second, members, early=[own_cond], late=[gain_step])
    third_quarters = gathered(third, members, early=[own_cond], late=[gain_step], bit_2=4)
    length = tm_count * prompt.shape[2]
    film, prompt_full, probs, keys, values, spread, summaries, totals, *fulls = call(
        functools.partial(attention_kernel, len(pieces), members, layout_2),
        (1,),
        [scalars(place)]
        + [whole(a) for a in (*pieces, full_queries)]
        + [whole(a) for a in own_second]
        + [fixed(a) for a in second_quarters],
        [
            new((MICRO, 8, wide)),
            new((MICRO, length, width), bf16),
            new((MICRO, HEADS * QUERIES, length)),
            new((MICRO, length, width), bf16),
            new((MICRO, length, width), bf16),
            new((HEADS * QUERIES, width), bf16),
            new((MICRO, 8, width)),
            new((MICRO, 8, width)),
            *[new((width, width), bf16)] * 4,
            new((width, wide), bf16),
        ],
        "attention",
        5,
    )

    full_key, full_value, full_query, full_out, full_film = fulls

    d_conv, d_conv_copy, conv_copy, sums, proj_keep, proj_send, res_out, skip_out = call(
        functools.partial(conv_kernel, tile, members, layout_3),
        tiles,
        [
            scalars(place),
            fixed(hidden),
            blocks(masks, tile),
            whole(mask_ends),
            blocks(frames, tile),
            blocks(res, tile),
            blocks(skip, tile),
            whole(low),
            whole(high),
            whole(film),
            whole(own_conv),
            whole(own_proj),
            *[fixed(q) for q in third_quarters],
        ],
        [
            new_fixed((MICRO, rows + 2 * HALO, wide), bf16),
            new_hbm((MICRO, rows + 2 * HALO, wide), bf16),
            new_hbm((3 * width, wide), bf16),
            new((8, wide)),
            new_fixed((1, width, width)),
            new_fixed((1, width, width), bf16),
            new_blocks((MICRO, rows, width), bf16, tile),
            new_blocks((MICRO, rows, width), bf16, tile),
        ],
        "conv",
        32,
        scratch=[
            pltpu.VMEM((3 * width, wide), bf16),
            pltpu.VMEM((width, wide), bf16),
            pltpu.VMEM((width, wide), f32),
            pltpu.VMEM((8, wide), f32),
            pltpu.SemaphoreType.DMA((3,)),
        ],
    )

    proj_received = swapped(proj_send, "tm", 1)
    sums_near = swapped(sums, "tm", 1)
    conv_keep, conv_send = call(
        conv_grad_kernel,
        (3,),
        [scalars(place), fixed(hidden), whole(masks), fixed(d_conv)],
        [new_fixed((3, width, width)), new_fixed((3, width, width), bf16)],
        "conv_grad",
        13.5,
    )
    conv_received = swapped(conv_send, "tm", 1)
    sums = sums + behind(sums_near, conv_send)
    sums_far = swapped(sums, "tm", 2)
    conv_proj = Reduction(
        [
            ([conv_keep[:2]], [conv_received[:2]]),
            ([conv_keep[2:], proj_keep], [conv_received[2:], proj_received]),
        ]
    )
    sums = sums + behind(sums_far, *conv_proj.aways)
    sums_far = swapped(sums, "tm", 4)
    grad_frames, keep, send = call(
        functools.partial(hidden_grad_kernel, tile),
        tiles,
        [scalars(place), hbm(d_conv_copy)]
        + [blocks(a, tile) for a in (masks, hot, frames, res, cond)]
        + [whole(a) for a in (conv_copy.reshape(3, width, wide), gain_cond, gain_step, embed)],
        [
            new_blocks((MICRO, rows, width), f32, tile),
            new_fixed((2, width, width)),
            new_fixed((2, width, width), bf16),
        ],
        "hidden_grad",
        27,
        scratch=[
            pltpu.VMEM((width + hots, wide), f32),
            pltpu.VMEM((2, tile + 2 * DILATION, wide), bf16),
            pltpu.SemaphoreType.DMA((2,)),
        ],
        after=[*conv_proj.aways, sums],
    )
    send, sums_far, *conv_proj.raw = lax.optimization_barrier((send, sums_far, *conv_proj.raw))
    received = swapped(send, "tm", 1)
    conv_proj.absorb()
    sums = sums + sums_far
    for bit in bits_of("tm")[3:-1]:
        sums = sums + swapped(sums, "tm", bit)
    sums_far = swapped(sums, "tm", bits_of("tm")[-1])
    received = behind(received, *conv_proj.aways, sums)
    cond_step = Reduction([([keep[:1]], [received[:1]]), ([keep[1:]], [received[1:]])])
    sums = sums + behind(sums_far, *cond_step.aways)
    grad_prompt, pair, small = call(
        attention_grad_kernel,
        (1,),
        [scalars(place)]
        + [
            whole(a)
            for a in (
                sums, prompt_full, probs, keys, values, spread, summaries, totals, full_key, full_value, full_out,
                full_film,
            )
        ],
        [new((MICRO, length // tm_count, width)), new((width, width)), new((SMALL_ROWS, width))],
        "attention_grad",
        7,
        scratch=[pltpu.VMEM((MICRO, length, wide), bf16)],
    )
    small, pair, *raw = lax.optimization_barrier((small, pair, *conv_proj.raw, *cond_step.raw))
    conv_proj.raw, cond_step.raw = raw[:2], raw[2:]
    conv_proj.absorb_all()
    conv_proj.start_third()
    cond_step.absorb_all(conv_proj.away)
    cond_step.start_third()

    for bit in reversed(bits_of("fsdp")):
        away, pair = parted(pair, "fsdp", bit, 0)
        pair = pair + swapped(away, "fsdp", bit).astype(f32)
    pair = rounded(pair).astype(bf16)
    pair_other = swapped(pair, "tm", 1)
    clear = bit_of("tm", 1) == 0
    grad_key = jnp.where(clear, pair, pair_other).astype(f32)
    grad_value = jnp.where(clear, pair_other, pair).astype(f32)

    packs = small[None]
    for bit in bits_of("fsdp"):
        packs = jnp.concatenate([packs, swapped(packs, "fsdp", bit)], axis=0)
    grad_queries, grad_query, grad_out, grad_film = call(
        small_grad_kernel,
        (1,),
        [scalars(place), whole(packs), whole(full_queries), whole(full_query)],
        [
            new((shard_queries, width)),
            new((shard_rows, width)),
            new((shard_rows, width)),
            new((shard_rows, wide)),
        ],
        "small_grads",
        3.3,
        scratch=[pltpu.VMEM((width, wide), f32), pltpu.VMEM((QUERIES, width), f32)],
    )

    def join(halves, shapes, name):
        return call(
            join_kernel,
            (1,),
            [scalars(place)] + [fixed(a) for a in halves],
            [new(shape) for shape in shapes],
            name,
            3,
        )

    flat, tall = (shard_rows, wide), (3, shard_rows, wide)
    conv_proj.fold()
    for bit in bits_of("tm")[3:]:
        conv_proj.start_double(bit)
        cond_step.fold(grad_queries)
        cond_step.start_double(bit)
        conv_proj.fold(cond_step.away)
    conv_proj.start_gather()
    cond_step.fold(conv_proj.away)
    cond_step.start_gather()
    conv_proj = conv_proj.gather()
    cond_step = cond_step.gather()
    grad_cond, grad_step = join(cond_step, [flat, flat], "join_cond_step")
    grad_conv, grad_proj = join(conv_proj, [tall, flat], "join_conv_proj")
    return (
        res_out[:, None],
        skip_out[:, None],
        grad_frames[:, None],
        grad_prompt[:, None],
        grad_queries,
        grad_step,
        grad_cond,
        grad_conv,
        grad_query,
        grad_key,
        grad_value,
        grad_out,
        grad_film,
        grad_proj,
    )


def solution(mesh):
    packed = P(None, "fsdp", "tm", None)
    short = P(None, "fsdp", None)
    weight = P("fsdp", None)
    taps = P(None, "fsdp", None)
    in_specs = (packed, packed, short, short, packed) + (weight,) * 3 + (taps,) + (weight,) * 6 + (packed,) * 2
    out_specs = (packed,) * 4 + (weight,) * 3 + (taps,) + (weight,) * 6
    return jax.shard_map(
        per_device, mesh=mesh, in_specs=in_specs, out_specs=out_specs, check_vma=False
    )
```

```python
import functools
import math

import jax
import jax.numpy as jnp
from jax import lax
from jax.experimental import pallas as pl
from jax.experimental.pallas import tpu as pltpu
from jax.sharding import PartitionSpec as P

HEADS = 8
QUERIES = 32
DILATION = 16
MICRO = 2
HALO = 2 * DILATION

SQRT_HALF = 0.7071067811865476
VMEM_LIMIT = 40 * 2**20
CONV_TILE, CONV_SUBS = 768, 1
HIDDEN_TILE, HIDDEN_SUBS = 768, 1
NT = ((1,), (1,))
TN = ((0,), (0,))
bf16 = jnp.bfloat16
f32 = jnp.float32


def dotf(left, right, dims=((1,), (0,))):
    return lax.dot_general(left, right, (dims, ((), ())), preferred_element_type=f32)


def lanes(block, width):
    return jnp.concatenate([block] * (width // block.shape[1]), axis=1)


VSPEC = pl.BlockSpec(memory_space=pltpu.VMEM)
SSPEC = pl.BlockSpec(memory_space=pltpu.SMEM)
ANYSPEC = pl.BlockSpec(memory_space=pl.ANY)


def fixed(array):
    return pltpu.with_memory_space_constraint(array, pltpu.VMEM), VSPEC


def whole(array):
    return pltpu.with_memory_space_constraint(array, pltpu.HBM), pl.BlockSpec(array.shape, lambda *_: (0,) * array.ndim)


def blocks(array, tile, first=0):
    return pltpu.with_memory_space_constraint(array, pltpu.HBM), pl.BlockSpec(
        (1, tile, array.shape[2]), lambda i, j: (i + first, j, 0)
    )


def hbm(array):
    return pltpu.with_memory_space_constraint(array, pltpu.HBM), pl.BlockSpec(memory_space=pltpu.HBM)


def scalars(array):
    return array, SSPEC


def call(kernel, grid, ins, outs, name, micros, scratch=(), after=(), aliases=None):
    count, waits = len(ins), len(after)

    def body(*refs):
        kernel(*refs[:count], *refs[count + waits :])

    return pl.pallas_call(
        body,
        grid=grid,
        in_specs=[spec for _, spec in ins] + [ANYSPEC] * waits,
        out_specs=[spec for _, spec in outs],
        out_shape=[out for out, _ in outs],
        scratch_shapes=scratch,
        input_output_aliases=aliases or {},
        cost_estimate=pl.CostEstimate(
            flops=int(micros * 1e9), bytes_accessed=2**12, transcendentals=0
        ),
        compiler_params=pltpu.CompilerParams(vmem_limit_bytes=VMEM_LIMIT),
        name=name,
    )(*[array for array, _ in ins], *after)


def new(shape, kind=f32):
    return pltpu.HBM(shape, kind), pl.BlockSpec(shape, lambda *_: (0,) * len(shape))


def new_fixed(shape, kind=f32):
    return pltpu.VMEM(shape, kind), VSPEC


def new_hbm(shape, kind=f32):
    return pltpu.HBM(shape, kind), pl.BlockSpec(memory_space=pltpu.HBM)


def new_blocks(shape, kind, tile, first=0):
    return pltpu.HBM(shape, kind), pl.BlockSpec(
        (1, tile, shape[2]), lambda i, j: (i + first, j, 0)
    )


def split_rows(row, parts):
    terms = []
    for _ in range(parts):
        term = row.astype(bf16)
        terms.append(term)
        row = row - term.astype(f32)
    return terms


def pack_kernel(layouts, place, *refs):
    count = sum(len(layout) - 1 for layout in layouts)
    weights, refs = list(refs[:count]), refs[count:]
    outs, helds, sems = refs[: len(layouts)], refs[len(layouts) : -1], refs[-1]
    copies = []
    for (which, *layout), held in zip(layouts, helds, strict=True):
        for row, column, *tap in layout:
            weight = weights.pop(0)
            view = weight.at[tap[0]] if tap else weight
            rows = view.shape[0] // 4
            start = pl.multiple_of(place[which] * rows, rows)
            copies.append(
                pltpu.make_async_copy(
                    view.at[pl.ds(start, rows)],
                    held.at[pl.ds(row, rows), pl.ds(column, view.shape[1])],
                    sems.at[len(copies)],
                )
            )
    for copy in copies:
        copy.start()
    for copy in copies:
        copy.wait()
    for out, held in zip(outs, helds, strict=True):
        out[...] = held[...].astype(bf16)


def edges_kernel(*refs):
    arrays, (last, first, sems) = refs[:-3], refs[-3:]
    copies = []
    for k, array in enumerate(arrays):
        rows = array.shape[1]
        copies.append(
            pltpu.make_async_copy(array.at[:, pl.ds(rows - HALO, HALO)], last.at[k], sems.at[2 * k])
        )
        copies.append(
            pltpu.make_async_copy(array.at[:, pl.ds(0, HALO)], first.at[k], sems.at[2 * k + 1])
        )
    for copy in copies:
        copy.start()
    for copy in copies:
        copy.wait()


def assemble(place, members, layout, shards, sources, fulls):
    member = place[2]
    for shard, full, (row, column) in zip(shards, fulls, layout, strict=True):
        rows, width = shard.shape
        part = rows // 4
        full[pl.ds(pl.multiple_of(member * rows, part), rows)] = shard[...].astype(bf16)
        for j in range(1, members):
            for source, quarter in sources:
                start = pl.multiple_of((member ^ j) * rows + quarter * part, part)
                full[pl.ds(start, part)] = source[j - 1, row : row + part, column : column + width]


def quarters_of(place, arrays, which=3):
    return [(array, place[which] ^ k) for k, array in enumerate(arrays)]


def masks_kernel(rows, slot, total, place, lengths, masks, hot, ends, hot_ends):
    micro, utters = lengths.shape
    hots = hot.shape[2]
    lane = lax.broadcasted_iota(jnp.int32, (1, hots), 1)
    lane = jnp.where(lane >= micro * slot, lane - micro * slot, lane)
    row = lax.broadcasted_iota(jnp.int32, (hots, 128), 0)
    count = jnp.where(row < micro * slot, 1.0, 0.0).astype(bf16)
    first = place[1] * rows - HALO
    chunk = rows // 6
    for i in range(micro):
        opens = jnp.full((1, hots), total, jnp.int32)
        closes = jnp.zeros((1, hots), jnp.int32)
        end = jnp.int32(0)
        for u in range(utters):
            mine = lane == i * slot + u
            if u == utters - 1:
                alive_until = end
            opens = jnp.where(mine, end, opens)
            end = end + lengths[i, u]
            closes = jnp.where(mine, end, closes)

        def rows_of(start, size, i=i, opens=opens, closes=closes, alive_until=alive_until):
            position = lax.broadcasted_iota(jnp.int32, (size, hots), 0) + start

            def one_hot(offset):
                shifted = position + offset
                return jnp.where((shifted >= opens) & (shifted < closes), 1.0, 0.0).astype(bf16)

            here = one_hot(0)
            low = dotf(here * one_hot(-DILATION), count).astype(bf16)
            high = dotf(here * one_hot(DILATION), count).astype(bf16)
            alive = (position[:, :128] < alive_until) & (position[:, :128] >= 0)
            alive = jnp.where(alive, 1.0, 0.0).astype(bf16)
            return jnp.concatenate([low, high, alive], axis=1), here

        ends[i, 0:HALO], hot_ends[i, 0:HALO] = rows_of(first, HALO)
        ends[i, HALO:], hot_ends[i, HALO:] = rows_of(first + HALO + rows, HALO)

        @pl.loop(0, rows // chunk)
        def _(k, i=i, rows_of=rows_of):
            at = pl.multiple_of(k * chunk, chunk)
            some, here = rows_of(first + HALO + at, chunk)
            masks[i, pl.ds(at, chunk)] = some
            hot[i, pl.ds(at, chunk)] = here


def film_kernel(
    tile, members, layout, place, frames, cond, low, high, hots, hot_ends, embed, own_cond, own_step, here, over, core, both,
    hidden, gain_cond, gain_step, w_cond, w_step, film_rows,
):
    i, j = pl.program_id(0), pl.program_id(1)
    width = frames.shape[2]
    rows = hidden.shape[1] - 2 * HALO - 2 * DILATION

    @pl.when((i == 0) & (j == 0))
    def _():
        sources = quarters_of(place, (here, over, core, both))
        assemble(place, members, layout, (own_cond, own_step), sources, (w_cond, w_step))
        step_film = dotf(embed[...], w_step[...])
        film_rows[...] = jnp.concatenate(split_rows(step_film, 2), axis=0)
        gain_cond[...] = w_cond[:, :width]
        gain_step[...] = film_rows[:, :width]

    def film(frame_rows, cond_rows, hot):
        both = dotf(cond_rows, w_cond[...]) + dotf(hot, film_rows[...])
        return (frame_rows.astype(f32) * (1.0 + both[:, :width]) + both[:, width:]).astype(bf16)

    @pl.when(j == 0)
    def _():
        edge = film(
            jnp.concatenate([low[0, i], high[0, i]], axis=0),
            jnp.concatenate([low[1, i], high[1, i]], axis=0),
            hot_ends[i],
        )
        nothing = jnp.zeros((DILATION, width), bf16)
        hidden[i, 0:DILATION] = nothing
        hidden[i, DILATION : DILATION + HALO] = edge[:HALO]
        hidden[i, DILATION + HALO + rows : DILATION + 2 * HALO + rows] = edge[HALO:]
        hidden[i, DILATION + 2 * HALO + rows :] = nothing

    base = pl.multiple_of(j * tile, tile)
    hidden[i, pl.ds(DILATION + HALO + base, tile)] = film(frames[0], cond[0], hots[0])


def halves_of(core, width):
    mine = pl.multiple_of(core * width, width)
    other = pl.multiple_of((1 - core) * width, width)
    return mine, other


def conv_kernel(
    tile, members, layout, place, hidden, masks, mask_ends, frames, res, skip, low, high, film, own_conv, own_proj,
    here, over, core, both,
    d_conv, d_conv_copy, conv_copy, sums, keep, send, res_out, skip_out,
    w_conv, w_proj, proj_total, columns, sems,
):
    i, j = pl.program_id(0), pl.program_id(1)
    width = res.shape[2]
    rows = d_conv.shape[1] - 2 * HALO
    gain, shift = 1.0 + film[i, 0:1, :width], film[i, 0:1, width:]
    first = (i == 0) & (j == 0)
    weights_away = pltpu.make_async_copy(w_conv, conv_copy, sems.at[2])

    @pl.when(first)
    def _():
        own = [own_conv.at[t] for t in range(3)]
        full = [w_conv.at[pl.ds(t * width, width)] for t in range(3)]
        sources = quarters_of(place, (here, over, core, both), 4)
        assemble(place, members, layout, [*own, own_proj], sources, [*full, w_proj])
        weights_away.start()
        sums[...] = jnp.zeros(sums.shape, f32)

    def body(before, now, later, keep_low, keep_high, alive, res_rows, skip_rows):
        taps = jnp.concatenate(
            [before * lanes(keep_low, width), now, later * lanes(keep_high, width)], axis=1
        )
        conv = dotf(taps, w_conv[...])
        th = jnp.tanh(conv[:, :width])
        sg = 0.5 + 0.5 * jnp.tanh(0.5 * conv[:, width:])
        alive = lanes(alive.astype(f32), width)
        branch = jnp.concatenate(
            [
                (res_rows.astype(f32) * (SQRT_HALF * alive)).astype(bf16),
                (skip_rows.astype(f32) * alive).astype(bf16),
            ],
            axis=1,
        )
        d_gated = dotf(branch, w_proj[...], NT)
        act = th * sg
        d_act = d_gated * gain
        left = (d_act * sg * (1.0 - th * th)).astype(bf16)
        right = (d_act * act * (1.0 - sg)).astype(bf16)
        return act, d_gated, branch, alive, left, right

    @pl.when(j == 0)
    def _():
        def ends(ref, at):
            return jnp.concatenate(
                [ref[i, at : at + HALO], ref[i, at + HALO + rows : at + 2 * HALO + rows]], axis=0
            )

        *_, left, right = body(
            ends(hidden, 0),
            ends(hidden, DILATION),
            ends(hidden, 2 * DILATION),
            mask_ends[i, :, 0:128],
            mask_ends[i, :, 128:256],
            mask_ends[i, :, 256:384],
            jnp.concatenate([low[2, i], high[2, i]], axis=0),
            jnp.concatenate([low[3, i], high[3, i]], axis=0),
        )
        d_conv[i, 0:HALO, :width] = left[:HALO]
        d_conv[i, 0:HALO, width:] = right[:HALO]
        d_conv[i, HALO + rows :, :width] = left[HALO:]
        d_conv[i, HALO + rows :, width:] = right[HALO:]
        columns[...] = jnp.zeros(columns.shape, f32)

    base = pl.multiple_of(j * tile, tile)

    size = tile // CONV_SUBS
    gated_all, branch_all = [], []
    for low_row in range(0, tile, size):
        part_rows = slice(low_row, low_row + size)

        def at(ref, offset, low_row=low_row):
            return ref[i, pl.ds(base + offset + low_row, size)]

        act, d_gated, branch, alive, left, right = body(
            at(hidden, HALO),
            at(hidden, HALO + DILATION),
            at(hidden, HALO + 2 * DILATION),
            masks[0, part_rows, 0:128],
            masks[0, part_rows, 128:256],
            masks[0, part_rows, 256:384],
            res[0, part_rows],
            skip[0, part_rows],
        )
        d_conv[i, pl.ds(base + HALO + low_row, size), :width] = left
        d_conv[i, pl.ds(base + HALO + low_row, size), width:] = right
        gated_rows = (act * gain + shift).astype(bf16)
        columns[:, :width] += jnp.sum((d_gated * act).reshape(size // 8, 8, width), axis=0)
        columns[:, width:] += jnp.sum(d_gated.reshape(size // 8, 8, width), axis=0)
        out = dotf(gated_rows, w_proj[...])
        frame_rows = frames[0, part_rows].astype(f32)
        res_out[0, part_rows] = ((frame_rows + out[:, :width]) * (SQRT_HALF * alive)).astype(bf16)
        skip_out[0, part_rows] = (out[:, width:] * alive).astype(bf16)
        gated_all.append(gated_rows)
        branch_all.append(branch)
    part = dotf(jnp.concatenate(gated_all, axis=0), jnp.concatenate(branch_all, axis=0), TN)

    @pl.when(first)
    def _():
        proj_total[...] = part

    @pl.when(jnp.logical_not(first))
    def _():
        proj_total[...] += part

    last = j == rows // tile - 1
    copies = [
        pltpu.make_async_copy(d_conv.at[m], d_conv_copy.at[m], sems.at[m]) for m in range(MICRO)
    ]
    for m in range(MICRO):
        pl.when(last & (i == m))(copies[m].start)

        @pl.when(last & (i == m))
        def _(m=m):
            sums[m : m + 1] = jnp.sum(columns[...], axis=0, keepdims=True)

    @pl.when(last & (i == MICRO - 1))
    def _():
        mine, other = halves_of(place[0], width)
        send[0] = proj_total[:, pl.ds(other, width)].astype(bf16)
        keep[0] = proj_total[:, pl.ds(mine, width)]
        for copy in (*copies, weights_away):
            copy.wait()


def conv_grad_kernel(place, hidden, masks, d_conv, keep, send):
    t = pl.program_id(0)
    micro, width = hidden.shape[0], hidden.shape[2]
    rows = d_conv.shape[1] - 2 * HALO
    mine, other = halves_of(place[0], width)

    for tap, lane in ((0, 0), (1, None), (2, 128)):

        @pl.when(t == tap)
        def _(tap=tap, lane=lane):
            def tap_rows(i):
                part = hidden[i, HALO + DILATION * tap : HALO + DILATION * tap + rows]
                return part if lane is None else part * lanes(masks[i, :, lane : lane + 128], width)

            for columns, ref in ((other, send), (mine, keep)):
                total = dotf(tap_rows(0), d_conv[0, HALO : HALO + rows, pl.ds(columns, width)], TN)
                for i in range(1, micro):
                    total = total + dotf(
                        tap_rows(i), d_conv[i, HALO : HALO + rows, pl.ds(columns, width)], TN
                    )
                ref[tap] = total.astype(ref.dtype)


def hidden_grad_kernel(
    tile, place, d_conv, masks, hots, frames, res, cond, w_conv, gain_cond, gain_step, embed,
    grad_frames, keep, send, total, window, sems,
):
    i, j = pl.program_id(0), pl.program_id(1)
    steps = pl.num_programs(1)
    width = frames.shape[2]
    now = i * steps + j

    def fetch(step):
        start = pl.multiple_of(HALO - DILATION + (step % steps) * tile, DILATION)
        return pltpu.make_async_copy(
            d_conv.at[step // steps, pl.ds(start, tile + 2 * DILATION)],
            window.at[step % 2],
            sems.at[step % 2],
        )

    @pl.when(now == 0)
    def _():
        fetch(0).start()

    @pl.when(now + 1 < MICRO * steps)
    def _():
        fetch(now + 1).start()

    fetch(now).wait()
    slot = now % 2
    size = tile // HIDDEN_SUBS
    films = []
    for low_row in range(0, tile, size):
        part_rows = slice(low_row, low_row + size)
        gain = dotf(cond[0, part_rows], gain_cond[...]) + dotf(hots[0, part_rows], gain_step[...])
        taps = []
        for tap, lane in ((2, 0), (1, None), (0, 128)):
            start = low_row + (2 - tap) * DILATION
            rows = window[slot, start : start + size]
            if lane is not None:
                rows = rows * lanes(masks[0, part_rows, lane : lane + 128], 2 * width)
            taps.append(dotf(rows, w_conv[tap], NT))
        d_hidden = taps[0] + taps[1] + taps[2]
        alive = lanes(masks[0, part_rows, 256:384].astype(f32), width)
        grad_frames[0, part_rows] = res[0, part_rows].astype(f32) * (SQRT_HALF * alive) + d_hidden * (
            1.0 + gain
        )
        films.append(
            jnp.concatenate(
                [(d_hidden * frames[0, part_rows].astype(f32)).astype(bf16), d_hidden.astype(bf16)], axis=1
            )
        )
    part = dotf(
        jnp.concatenate([cond[0], hots[0]], axis=1), jnp.concatenate(films, axis=0), TN
    )

    @pl.when(now == 0)
    def _():
        total[...] = part

    @pl.when(now > 0)
    def _():
        total[...] += part

    @pl.when(now == MICRO * steps - 1)
    def _():
        mine, other = halves_of(place[0], width)
        count = embed.shape[0]
        for columns, ref in ((other, send), (mine, keep)):
            ref[0] = total[:width, pl.ds(columns, width)].astype(ref.dtype)
            d_step = total[width : width + count, pl.ds(columns, width)]
            step = jnp.zeros((width, width), f32)
            for term in split_rows(d_step, 3):
                step = step + dotf(embed[...], term, TN)
            ref[1] = step.astype(ref.dtype)


def head_masks(width):
    column = lax.broadcasted_iota(jnp.int32, (1, width), 1)
    size = width // HEADS
    return [((column >= h * size) & (column < (h + 1) * size)).astype(f32) for h in range(HEADS)]


def attention_kernel(
    members, layout, place, every_prompt, queries, own_key, own_value, own_query, own_out, own_film, here, over, core, both,
    film, prompt, probs, keys, values, spread, summaries, totals, w_key, w_value, w_query, w_out, w_film,
):
    count, micro, shard, width = every_prompt.shape
    assemble(
        place,
        members,
        layout,
        (own_key, own_value, own_query, own_out, own_film),
        quarters_of(place, (here, over, core, both)),
        (w_key, w_value, w_query, w_out, w_film),
    )
    masks = head_masks(width)
    scale = 1.0 / math.sqrt(width // HEADS)
    for d in range(count):
        for i in range(micro):
            prompt[i, d * shard : (d + 1) * shard] = every_prompt[d, i]
    query = dotf(queries[...], w_query[...])
    spread[...] = jnp.concatenate([(query * mask).astype(bf16) for mask in masks], axis=0)
    for i in range(micro):
        keys[i] = dotf(prompt[i], w_key[...]).astype(bf16)
        values[i] = dotf(prompt[i], w_value[...]).astype(bf16)
        scores = dotf(spread[...], keys[i], NT) * scale
        weights = jnp.exp(scores - jnp.max(scores, axis=1, keepdims=True))
        weights = weights / jnp.sum(weights, axis=1, keepdims=True)
        probs[i] = weights
        heads = dotf(weights.astype(bf16), values[i])
        context = heads[:QUERIES] * masks[0]
        for h in range(1, HEADS):
            context = context + heads[h * QUERIES : (h + 1) * QUERIES] * masks[h]
        context = context.astype(bf16)
        mixed = dotf(context, w_out[...])
        summary = jnp.mean(mixed, axis=0, keepdims=True).astype(bf16)
        summary = jnp.broadcast_to(summary.astype(f32), (8, width))
        summaries[i] = summary
        totals[i] = jnp.broadcast_to(
            jnp.sum(context.astype(f32), axis=0, keepdims=True), (8, width)
        )
        wide = jnp.concatenate([summary, summary], axis=0).astype(bf16)
        film[i] = dotf(wide, w_film[...])[:8]


def exact_dot(row, matrix):
    terms = split_rows(row, 3)
    stacked = jnp.concatenate(
        [term.astype(f32) for term in terms] + [jnp.zeros((13, row.shape[1]), f32)], axis=0
    )
    return jnp.sum(dotf(stacked.astype(bf16), matrix, NT), axis=0, keepdims=True)


SMALL_ROWS = QUERIES + 5 * 8


def attention_grad_kernel(
    place, sums, prompt, probs, keys, values, spread, summaries, totals, w_key, w_value, w_out, w_film,
    grad_prompt, keep, small, pair,
):
    micro, length, width = prompt.shape
    masks = head_masks(width)
    scale = 1.0 / math.sqrt(width // HEADS)
    mine, _ = halves_of(place[0], width)
    shard = grad_prompt.shape[1]
    own = pl.multiple_of(place[1] * shard, shard)
    d_query_total = jnp.zeros((QUERIES, width), f32)
    small[...] = jnp.zeros(small.shape, f32)
    for i in range(micro):
        d_film = sums[i : i + 1]
        d_mixed = exact_dot(d_film, w_film[...]) / QUERIES
        d_context = exact_dot(d_mixed, w_out[...]).astype(bf16).astype(f32)
        d_heads = jnp.concatenate(
            [d_context * mask for mask in masks] + [jnp.zeros((8, width), f32)], axis=0
        ).astype(bf16)
        d_probs = dotf(d_heads, values[i], NT)
        d_probs = jnp.concatenate(
            [jnp.broadcast_to(d_probs[h : h + 1], (QUERIES, length)) for h in range(HEADS)], axis=0
        )
        weights = probs[i]
        row_sums = jnp.sum(weights * d_probs, axis=1, keepdims=True)
        d_scores = (weights * (d_probs - row_sums)).astype(bf16)
        heads = dotf(d_scores, keys[i])
        d_query = heads[:QUERIES] * masks[0]
        for h in range(1, HEADS):
            d_query = d_query + heads[h * QUERIES : (h + 1) * QUERIES] * masks[h]
        d_query_total = d_query_total + d_query * scale
        pair[i, :, :width] = (dotf(d_scores, spread[...], TN) * scale).astype(bf16)
        wide = jnp.concatenate(
            [jnp.broadcast_to(d_context * mask, (QUERIES, width)) for mask in masks], axis=0
        ).astype(bf16)
        pair[i, :, width:] = dotf(weights.astype(bf16), wide, TN).astype(bf16)
        grad_prompt[i] = dotf(pair[i, pl.ds(own, shard), :width], w_key[...], NT) + dotf(
            pair[i, pl.ds(own, shard), width:], w_value[...], NT
        )
        rows = (summaries[i, 0:1], d_film[:, :width], d_film[:, width:], totals[i, 0:1], d_mixed)
        for k, row in enumerate(rows):
            at = QUERIES + 8 * k + i
            small[at : at + 1] = row
    small[0:QUERIES] = d_query_total
    grad = jnp.zeros((width, width), f32)
    for i in range(micro):
        grad = grad + dotf(prompt[i], pair[i, :, pl.ds(mine, width)], TN)
    keep[...] = grad


def exact_outer(left, right):
    one = [t.astype(f32) for t in split_rows(left, 3)]
    two = [t.astype(f32) for t in split_rows(right, 3)]
    picks = ((0, 0), (0, 1), (0, 2), (1, 0), (1, 1), (2, 0))
    stacked = [jnp.concatenate([side[p[k]] for p in picks], axis=0) for k, side in ((0, one), (1, two))]
    return dotf(stacked[0].astype(bf16), stacked[1].astype(bf16), TN)


def small_grad_kernel(place, packs, queries, w_query, g_queries, g_query, g_out, g_film, rows_of, queries_of):
    members, _, width = packs.shape
    member = place[2]
    shard = g_query.shape[0]
    start = pl.multiple_of(member * shard, shard)

    def group(k):
        at = QUERIES + 8 * k
        return jnp.concatenate([packs[m, at : at + 8] for m in range(members)], axis=0)

    rows_of[...] = exact_outer(
        group(0), jnp.concatenate([group(1), group(2)], axis=1)
    )
    g_film[...] = rows_of[pl.ds(start, shard)]
    rows_of[:, :width] = exact_outer(group(3), group(4))
    g_out[...] = rows_of[pl.ds(start, shard), :width]
    d_query = packs[0, 0:QUERIES]
    for m in range(1, members):
        d_query = d_query + packs[m, 0:QUERIES]
    rows_of[:, width:] = exact_outer(queries[...].astype(f32), d_query)
    g_query[...] = rows_of[pl.ds(start, shard), width:]
    terms = jnp.concatenate(split_rows(d_query, 3), axis=0)
    product = dotf(terms, w_query[...], NT)
    queries_of[...] = product[:QUERIES] + product[QUERIES : 2 * QUERIES] + product[2 * QUERIES :]
    count = g_queries.shape[0]
    for m in range(members):

        @pl.when(member == m)
        def _(m=m):
            g_queries[...] = queries_of[m * count : (m + 1) * count]


def swapped(array, axis, bit):
    count = lax.axis_size(axis)
    return lax.ppermute(array, axis, [(i, i ^ bit) for i in range(count)])


def bit_of(axis, bit):
    return (lax.axis_index(axis) // bit) % 2


def bits_of(axis):
    count = lax.axis_size(axis)
    assert count & (count - 1) == 0
    return [1 << b for b in range(count.bit_length() - 1)]


def rounded(array):
    return lax.reduce_precision(array, 8, 7)


def parted(total, axis, bit, dim):
    size = total.shape[dim] // 2
    mine = bit_of(axis, bit)
    away = lax.dynamic_slice_in_dim(total, (1 - mine) * size, size, dim).astype(bf16)
    return away, lax.dynamic_slice_in_dim(total, mine * size, size, dim)


def halvings(order):
    members = [("fsdp", bit, 1) for bit in reversed(bits_of("fsdp"))]
    second = [("tm", 2, 2)]
    return members + second if order == 0 else second + members


def doubled(mine, theirs, axis, bit, dim):
    clear = bit_of(axis, bit) == 0
    return jnp.concatenate(
        [jnp.where(clear, mine, theirs), jnp.where(clear, theirs, mine)], axis=dim
    )


def behind(array, *others):
    return lax.optimization_barrier((array, *others))[0]


def gathered(packed, members, early=(), late=(), bit_2=2):
    every = packed[None]
    for bit in bits_of("fsdp"):
        theirs = swapped(every, "fsdp", bit)
        every = theirs if members == 2 else jnp.concatenate([every, theirs], axis=0)
    here = every if members == 2 else every[1:]
    if early:
        here = behind(here, *early)
    over = swapped(here, "tm", bit_2)
    if late:
        over = behind(over, *late)
    return here, over, swapped(here, "tm", 1), swapped(over, "tm", 1)


class Reduction:
    def __init__(self, halves):
        members = lax.axis_size("fsdp")
        self.steps = [halvings(k) for k in range(2)]
        self.totals = []
        for keeps, received in halves:
            total = jnp.concatenate(
                [k + r.astype(f32) for k, r in zip(keeps, received, strict=True)], axis=0
            )
            parts, rows, width = total.shape
            self.totals.append(total.reshape(parts, members, 2, rows // members // 2, width))
        self.send()

    def send(self):
        pairs = [parted(t, *s[0]) for t, s in zip(self.totals, self.steps, strict=True)]
        self.aways, self.kept = zip(*pairs, strict=True)
        self.raw = [swapped(a, *s[0][:2]) for a, s in zip(self.aways, self.steps, strict=True)]

    def absorb(self, *others):
        self.totals = [
            k + behind(r, *others).astype(f32) for k, r in zip(self.kept, self.raw, strict=True)
        ]
        self.steps = [s[1:] for s in self.steps]
        if self.steps[0]:
            self.send()

    def absorb_all(self, *others):
        while self.steps[0]:
            self.absorb(*others)

    def start_third(self):
        total = jnp.concatenate(self.totals, axis=0)
        total = total.reshape(total.shape[0], total.shape[3], total.shape[4])
        self.away, self.own = parted(total, "tm", 4, 1)
        self.raw = swapped(self.away, "tm", 4)

    def fold(self, *others):
        self.total = self.own + behind(self.raw, *others).astype(f32)

    def start_double(self, bit):
        self.own = rounded(self.total)
        self.away = self.own.astype(bf16)
        self.raw = swapped(self.away, "tm", bit)

    def start_gather(self):
        self.away = rounded(self.total).astype(bf16)
        self.raw = [swapped(self.away, "tm", bits) for bits in (4, 2, 6)]

    def gather(self):
        clear = bit_of("tm", 4) == 0
        pairs = []
        for one, two in ((self.away, self.raw[0]), (self.raw[1], self.raw[2])):
            pairs.append([jnp.where(clear, one, two), jnp.where(clear, two, one)])
        clear = bit_of("tm", 2) == 0
        rows = [jnp.where(clear, a, b) for a, b in zip(pairs[0] + pairs[1], pairs[1] + pairs[0], strict=True)]
        own = jnp.concatenate(rows, axis=1)
        return own, swapped(own, "tm", 1)


def join_kernel(place, own, other, *outs):
    width = own.shape[2]
    mine, theirs = halves_of(place[0], width)
    first = 0
    for out in outs:
        for source, columns in ((own, mine), (other, theirs)):
            if len(out.shape) == 2:
                out[:, pl.ds(columns, width)] = source[first].astype(f32)
            else:
                count = out.shape[0]
                out[:, :, pl.ds(columns, width)] = source[first : first + count].astype(f32)
        first += 1 if len(out.shape) == 2 else out.shape[0]


def step_embedding(pack_steps, width):
    half_width = width // 2
    freqs = jnp.exp(jnp.arange(half_width).astype(f32) * (-math.log(10000.0) / half_width))
    angles = pack_steps.astype(f32)[:, None] * freqs[None, :]
    return jnp.concatenate([jnp.sin(angles), jnp.cos(angles)], axis=1)


def per_device(
    frames, conditioning, lengths, steps, prompt, queries, w_step, w_cond, w_conv, w_query, w_key,
    w_value, w_out, w_film, w_proj, grad_res, grad_skip,
):
    rows, width = frames.shape[2:]
    wide = 2 * width
    tile = rows // 3 if rows % 48 == 0 else rows
    tiles = (MICRO, rows // tile)
    conv_tile, hidden_tile = CONV_TILE, HIDDEN_TILE
    tm_count, tm_index = lax.axis_size("tm"), lax.axis_index("tm")
    members, member = lax.axis_size("fsdp"), lax.axis_index("fsdp")
    shard_rows = w_cond.shape[0]
    shard_queries = queries.shape[0]
    frames, cond, res, skip = frames[:, 0], conditioning[:, 0], grad_res[:, 0], grad_skip[:, 0]
    core = tm_index % 2
    quarter = core * 2 + (tm_index // 2) % 2
    other_quarter = core * 2 + (tm_index // 4) % 2
    place = jnp.stack([core, tm_index, member, quarter, other_quarter]).astype(jnp.int32)

    part = shard_rows // 4

    def pack(weights, layouts, heights, name, after=()):
        return call(
            functools.partial(pack_kernel, layouts),
            (1,),
            [scalars(place)] + [hbm(w) for w in weights],
            [new_fixed((height, wide), bf16) for height in heights],
            name,
            2,
            scratch=[pltpu.VMEM((height, wide), f32) for height in heights]
            + [pltpu.SemaphoreType.DMA((10,))],
            after=after,
        )

    layout_1 = [(0, 0), (part, 0)]
    layout_2 = [(0, 0), (0, width), (part, 0), (part, width), (2 * part, 0)]
    layout_3 = [(k * part, 0) for k in range(4)]
    taps_3 = [4, (0, 0, 0), (part, 0, 1), (2 * part, 0, 2), (3 * part, 0)]
    (first,) = pack([w_cond, w_step], [[3, *layout_1]], [2 * part], "pack_first")

    edge = (4, MICRO, HALO, width)
    last_rows, first_rows = call(
        edges_kernel,
        (1,),
        [hbm(a) for a in (frames, cond, res, skip)],
        [new_fixed(edge, bf16), new_fixed(edge, bf16)],
        "edges",
        1,
        scratch=[pltpu.SemaphoreType.DMA((8,))],
        after=[first],
    )
    low = lax.ppermute(last_rows, "tm", [(d, d + 1) for d in range(tm_count - 1)])
    high = lax.ppermute(first_rows, "tm", [(d + 1, d) for d in range(tm_count - 1)])

    second, third = pack(
        [w_key, w_value, w_query, w_out, w_film, w_conv, w_conv, w_conv, w_proj],
        [[3, *layout_2], taps_3],
        [3 * part, 4 * part],
        "pack_rest",
        after=[last_rows],
    )
    utters = lengths.shape[2]
    slot = -(-utters // 32) * 32
    hots = 2 * MICRO * slot
    masks, hot, mask_ends, hot_ends = call(
        functools.partial(masks_kernel, rows, slot, tm_count * rows),
        (1,),
        [scalars(place), scalars(lengths[:, 0])],
        [new((MICRO, n, lane), bf16) for n in (rows, 2 * HALO) for lane in (384, hots)],
        "masks",
        5,
        after=[second],
    )
    first_quarters = gathered(first, members, early=[second], late=[mask_ends])
    every_prompt = jnp.broadcast_to(behind(prompt, second)[None, :, 0], (tm_count, MICRO, *prompt.shape[2:]))
    every_prompt = lax.all_to_all(every_prompt, "tm", 0, 0)
    full_queries = behind(queries, second).astype(bf16)
    for bit in bits_of("fsdp"):
        full_queries = doubled(full_queries, swapped(full_queries, "fsdp", bit), "fsdp", bit, 0)

    slots = jnp.pad(steps[:, 0], ((0, 0), (0, slot - utters))).reshape(-1)
    embed = step_embedding(slots, width).astype(bf16)

    hidden, gain_cond, gain_step = call(
        functools.partial(film_kernel, tile, members, layout_1),
        tiles,
        [
            scalars(place),
            blocks(frames, tile),
            blocks(cond, tile),
            whole(low),
            whole(high),
            blocks(hot, tile),
            whole(hot_ends),
            whole(embed),
            whole(w_cond),
            whole(w_step),
            *[fixed(q) for q in first_quarters],
        ],
        [
            new_fixed((MICRO, rows + 2 * HALO + 2 * DILATION, width), bf16),
            new((width, width), bf16),
            new((hots, width), bf16),
        ],
        "film",
        1,
        scratch=[
            pltpu.VMEM((width, wide), bf16),
            pltpu.VMEM((width, wide), bf16),
            pltpu.VMEM((hots, wide), bf16),
        ],
        after=[full_queries],
    )
    second_quarters = gathered(second, members, early=[mask_ends], late=[gain_step])
    third_quarters = gathered(third, members, early=[mask_ends], late=[gain_step], bit_2=4)
    length = tm_count * prompt.shape[2]
    film, prompt_full, probs, keys, values, spread, summaries, totals, *fulls = call(
        functools.partial(attention_kernel, members, layout_2),
        (1,),
        [scalars(place)]
        + [whole(a) for a in (every_prompt, full_queries)]
        + [whole(w) for w in (w_key, w_value, w_query, w_out, w_film)]
        + [fixed(a) for a in second_quarters],
        [
            new((MICRO, 8, wide)),
            new((MICRO, length, width), bf16),
            new((MICRO, HEADS * QUERIES, length)),
            new((MICRO, length, width), bf16),
            new((MICRO, length, width), bf16),
            new((HEADS * QUERIES, width), bf16),
            new((MICRO, 8, width)),
            new((MICRO, 8, width)),
            *[new((width, width), bf16)] * 4,
            new((width, wide), bf16),
        ],
        "attention",
        5,
    )

    full_key, full_value, full_query, full_out, full_film = fulls

    d_conv, d_conv_copy, conv_copy, sums, proj_keep, proj_send, res_out, skip_out = call(
        functools.partial(conv_kernel, conv_tile, members, layout_3),
        (MICRO, rows // conv_tile),
        [
            scalars(place),
            fixed(hidden),
            blocks(masks, conv_tile),
            whole(mask_ends),
            blocks(frames, conv_tile),
            blocks(res, conv_tile),
            blocks(skip, conv_tile),
            whole(low),
            whole(high),
            whole(film),
            whole(w_conv),
            whole(w_proj),
            *[fixed(q) for q in third_quarters],
        ],
        [
            new_fixed((MICRO, rows + 2 * HALO, wide), bf16),
            new_hbm((MICRO, rows + 2 * HALO, wide), bf16),
            new_hbm((3 * width, wide), bf16),
            new((8, wide)),
            new_fixed((1, width, width)),
            new_fixed((1, width, width), bf16),
            new_blocks((MICRO, rows, width), bf16, conv_tile),
            new_blocks((MICRO, rows, width), bf16, conv_tile),
        ],
        "conv",
        32,
        scratch=[
            pltpu.VMEM((3 * width, wide), bf16),
            pltpu.VMEM((width, wide), bf16),
            pltpu.VMEM((width, wide), f32),
            pltpu.VMEM((8, wide), f32),
            pltpu.SemaphoreType.DMA((3,)),
        ],
    )

    proj_received = swapped(proj_send, "tm", 1)
    sums_near = swapped(sums, "tm", 1)
    conv_keep, conv_send = call(
        conv_grad_kernel,
        (3,),
        [scalars(place), fixed(hidden), whole(masks), fixed(d_conv)],
        [new_fixed((3, width, width)), new_fixed((3, width, width), bf16)],
        "conv_grad",
        13.5,
    )
    conv_received = swapped(conv_send, "tm", 1)
    sums = sums + behind(sums_near, conv_send)
    sums_far = swapped(sums, "tm", 2)
    conv_proj = Reduction(
        [
            ([conv_keep[:2]], [conv_received[:2]]),
            ([conv_keep[2:], proj_keep], [conv_received[2:], proj_received]),
        ]
    )
    sums = sums + behind(sums_far, *conv_proj.aways)
    sums_far = swapped(sums, "tm", 4)
    grad_frames, keep, send = call(
        functools.partial(hidden_grad_kernel, hidden_tile),
        (MICRO, rows // hidden_tile),
        [scalars(place), hbm(d_conv_copy)]
        + [blocks(a, hidden_tile) for a in (masks, hot, frames, res, cond)]
        + [whole(a) for a in (conv_copy.reshape(3, width, wide), gain_cond, gain_step, embed)],
        [
            new_blocks((MICRO, rows, width), f32, hidden_tile),
            new_fixed((2, width, width)),
            new_fixed((2, width, width), bf16),
        ],
        "hidden_grad",
        27,
        scratch=[
            pltpu.VMEM((width + hots, wide), f32),
            pltpu.VMEM((2, hidden_tile + 2 * DILATION, wide), bf16),
            pltpu.SemaphoreType.DMA((2,)),
        ],
        after=[*conv_proj.aways, sums],
    )
    send, sums_far, *conv_proj.raw = lax.optimization_barrier((send, sums_far, *conv_proj.raw))
    received = swapped(send, "tm", 1)
    conv_proj.absorb()
    sums = sums + sums_far
    for bit in bits_of("tm")[3:-1]:
        sums = sums + swapped(sums, "tm", bit)
    sums_far = swapped(sums, "tm", bits_of("tm")[-1])
    received = behind(received, *conv_proj.aways, sums)
    cond_step = Reduction([([keep[:1]], [received[:1]]), ([keep[1:]], [received[1:]])])
    sums_far = behind(sums_far, *cond_step.aways)
    conv_proj.absorb_all(*cond_step.aways)
    conv_proj.start_third()
    cond_step.absorb_all(conv_proj.away)
    cond_step.start_third()
    conv_proj.fold(cond_step.away)
    first_bit, *more_bits = bits_of("tm")[3:]
    conv_proj.start_double(first_bit)
    cond_step.fold(conv_proj.away)
    cond_step.start_double(first_bit)
    sums = sums + behind(sums_far, cond_step.away)
    grad_prompt, pair, small = call(
        attention_grad_kernel,
        (1,),
        [scalars(place)]
        + [
            whole(a)
            for a in (
                sums, prompt_full, probs, keys, values, spread, summaries, totals, full_key, full_value, full_out,
                full_film,
            )
        ],
        [new((MICRO, length // tm_count, width)), new((width, width)), new((SMALL_ROWS, width))],
        "attention_grad",
        7,
        scratch=[pltpu.VMEM((MICRO, length, wide), bf16)],
    )
    small, pair, conv_proj.raw = lax.optimization_barrier((small, pair, conv_proj.raw))
    for bit in reversed(bits_of("fsdp")):
        away, pair = parted(pair, "fsdp", bit, 0)
        pair = pair + swapped(away, "fsdp", bit).astype(f32)
    pair = rounded(pair).astype(bf16)
    pair_other = swapped(pair, "tm", 1)
    clear = bit_of("tm", 1) == 0
    grad_key = jnp.where(clear, pair, pair_other).astype(f32)
    grad_value = jnp.where(clear, pair_other, pair).astype(f32)

    packs = small[None]
    for bit in bits_of("fsdp"):
        packs = jnp.concatenate([packs, swapped(packs, "fsdp", bit)], axis=0)
    grad_queries, grad_query, grad_out, grad_film = call(
        small_grad_kernel,
        (1,),
        [scalars(place), whole(packs), whole(full_queries), whole(full_query)],
        [
            new((shard_queries, width)),
            new((shard_rows, width)),
            new((shard_rows, width)),
            new((shard_rows, wide)),
        ],
        "small_grads",
        3.3,
        scratch=[pltpu.VMEM((width, wide), f32), pltpu.VMEM((QUERIES, width), f32)],
    )

    def join(halves, shapes, name):
        return call(
            join_kernel,
            (1,),
            [scalars(place)] + [fixed(a) for a in halves],
            [new(shape) for shape in shapes],
            name,
            3,
        )

    flat, tall = (shard_rows, wide), (3, shard_rows, wide)
    for bit in more_bits:
        conv_proj.fold(cond_step.away)
        conv_proj.start_double(bit)
        cond_step.fold(conv_proj.away)
        cond_step.start_double(bit)
    conv_proj.fold()
    conv_proj.start_gather()
    cond_step.fold(conv_proj.away, grad_queries)
    cond_step.start_gather()
    conv_proj = conv_proj.gather()
    cond_step = cond_step.gather()
    grad_cond, grad_step = join(cond_step, [flat, flat], "join_cond_step")
    grad_conv, grad_proj = join(conv_proj, [tall, flat], "join_conv_proj")
    return (
        res_out[:, None],
        skip_out[:, None],
        grad_frames[:, None],
        grad_prompt[:, None],
        grad_queries,
        grad_step,
        grad_cond,
        grad_conv,
        grad_query,
        grad_key,
        grad_value,
        grad_out,
        grad_film,
        grad_proj,
    )


def solution(mesh):
    packed = P(None, "fsdp", "tm", None)
    short = P(None, "fsdp", None)
    weight = P("fsdp", None)
    taps = P(None, "fsdp", None)
    in_specs = (packed, packed, short, short, packed) + (weight,) * 3 + (taps,) + (weight,) * 6 + (packed,) * 2
    out_specs = (packed,) * 4 + (weight,) * 3 + (taps,) + (weight,) * 6
    return jax.shard_map(
        per_device, mesh=mesh, in_specs=in_specs, out_specs=out_specs, check_vma=False
    )
```

```python
import functools
import math

import jax
import jax.numpy as jnp
from jax import lax
from jax.experimental import pallas as pl
from jax.experimental.pallas import tpu as pltpu
from jax.sharding import PartitionSpec as P

HEADS = 8
QUERIES = 32
DILATION = 16
MICRO = 2
HALO = 2 * DILATION

SQRT_HALF = 0.7071067811865476
VMEM_LIMIT = 40 * 2**20
CONV_TILE, CONV_SUBS = 768, 1
HIDDEN_TILE, HIDDEN_SUBS = 768, 1
NT = ((1,), (1,))
TN = ((0,), (0,))
bf16 = jnp.bfloat16
f32 = jnp.float32


def dotf(left, right, dims=((1,), (0,))):
    return lax.dot_general(left, right, (dims, ((), ())), preferred_element_type=f32)


def lanes(block, width):
    return jnp.concatenate([block] * (width // block.shape[1]), axis=1)


VSPEC = pl.BlockSpec(memory_space=pltpu.VMEM)
SSPEC = pl.BlockSpec(memory_space=pltpu.SMEM)
ANYSPEC = pl.BlockSpec(memory_space=pl.ANY)


def fixed(array):
    return pltpu.with_memory_space_constraint(array, pltpu.VMEM), VSPEC


def whole(array):
    return pltpu.with_memory_space_constraint(array, pltpu.HBM), pl.BlockSpec(array.shape, lambda *_: (0,) * array.ndim)


def blocks(array, tile, first=0):
    return pltpu.with_memory_space_constraint(array, pltpu.HBM), pl.BlockSpec(
        (1, tile, array.shape[2]), lambda i, j: (i + first, j, 0)
    )


def hbm(array):
    return pltpu.with_memory_space_constraint(array, pltpu.HBM), pl.BlockSpec(memory_space=pltpu.HBM)


def scalars(array):
    return array, SSPEC


def call(kernel, grid, ins, outs, name, micros, scratch=(), after=(), aliases=None):
    count, waits = len(ins), len(after)

    def body(*refs):
        kernel(*refs[:count], *refs[count + waits :])

    return pl.pallas_call(
        body,
        grid=grid,
        in_specs=[spec for _, spec in ins] + [ANYSPEC] * waits,
        out_specs=[spec for _, spec in outs],
        out_shape=[out for out, _ in outs],
        scratch_shapes=scratch,
        input_output_aliases=aliases or {},
        cost_estimate=pl.CostEstimate(
            flops=int(micros * 1e9), bytes_accessed=2**12, transcendentals=0
        ),
        compiler_params=pltpu.CompilerParams(vmem_limit_bytes=VMEM_LIMIT),
        name=name,
    )(*[array for array, _ in ins], *after)


def new(shape, kind=f32):
    return pltpu.HBM(shape, kind), pl.BlockSpec(shape, lambda *_: (0,) * len(shape))


def new_fixed(shape, kind=f32):
    return pltpu.VMEM(shape, kind), VSPEC


def new_hbm(shape, kind=f32):
    return pltpu.HBM(shape, kind), pl.BlockSpec(memory_space=pltpu.HBM)


def new_blocks(shape, kind, tile, first=0):
    return pltpu.HBM(shape, kind), pl.BlockSpec(
        (1, tile, shape[2]), lambda i, j: (i + first, j, 0)
    )


def split_rows(row, parts):
    terms = []
    for _ in range(parts):
        term = row.astype(bf16)
        terms.append(term)
        row = row - term.astype(f32)
    return terms


def pack_kernel(layouts, place, *refs):
    count = sum(len(layout) - 1 for layout in layouts)
    weights, refs = list(refs[:count]), refs[count:]
    outs, helds, sems = refs[: len(layouts)], refs[len(layouts) : -1], refs[-1]
    copies = []
    for (which, *layout), held in zip(layouts, helds, strict=True):
        for row, column, *tap in layout:
            weight = weights.pop(0)
            view = weight.at[tap[0]] if tap else weight
            rows = view.shape[0] // 4
            start = pl.multiple_of(place[which] * rows, rows)
            copies.append(
                pltpu.make_async_copy(
                    view.at[pl.ds(start, rows)],
                    held.at[pl.ds(row, rows), pl.ds(column, view.shape[1])],
                    sems.at[len(copies)],
                )
            )
    for copy in copies:
        copy.start()
    for copy in copies:
        copy.wait()
    for out, held in zip(outs, helds, strict=True):
        out[...] = held[...].astype(bf16)


def edges_kernel(*refs):
    arrays, (last, first, sems) = refs[:-3], refs[-3:]
    copies = []
    for k, array in enumerate(arrays):
        rows = array.shape[1]
        copies.append(
            pltpu.make_async_copy(array.at[:, pl.ds(rows - HALO, HALO)], last.at[k], sems.at[2 * k])
        )
        copies.append(
            pltpu.make_async_copy(array.at[:, pl.ds(0, HALO)], first.at[k], sems.at[2 * k + 1])
        )
    for copy in copies:
        copy.start()
    for copy in copies:
        copy.wait()


def assemble(place, members, layout, shards, sources, fulls):
    member = place[2]
    for shard, full, (row, column) in zip(shards, fulls, layout, strict=True):
        rows, width = shard.shape
        part = rows // 4
        full[pl.ds(pl.multiple_of(member * rows, part), rows)] = shard[...].astype(bf16)
        for j in range(1, members):
            for source, quarter in sources:
                start = pl.multiple_of((member ^ j) * rows + quarter * part, part)
                full[pl.ds(start, part)] = source[j - 1, row : row + part, column : column + width]


def quarters_of(place, arrays, which=3):
    return [(array, place[which] ^ k) for k, array in enumerate(arrays)]


def masks_kernel(rows, slot, total, place, lengths, masks, hot, ends, hot_ends):
    micro, utters = lengths.shape
    hots = hot.shape[2]
    lane = lax.broadcasted_iota(jnp.int32, (1, hots), 1)
    lane = jnp.where(lane >= micro * slot, lane - micro * slot, lane)
    row = lax.broadcasted_iota(jnp.int32, (hots, 128), 0)
    count = jnp.where(row < micro * slot, 1.0, 0.0).astype(bf16)
    first = place[1] * rows - HALO
    chunk = rows // 6
    for i in range(micro):
        opens = jnp.full((1, hots), total, jnp.int32)
        closes = jnp.zeros((1, hots), jnp.int32)
        end = jnp.int32(0)
        for u in range(utters):
            mine = lane == i * slot + u
            if u == utters - 1:
                alive_until = end
            opens = jnp.where(mine, end, opens)
            end = end + lengths[i, u]
            closes = jnp.where(mine, end, closes)

        def rows_of(start, size, i=i, opens=opens, closes=closes, alive_until=alive_until):
            position = lax.broadcasted_iota(jnp.int32, (size, hots), 0) + start

            def one_hot(offset):
                shifted = position + offset
                return jnp.where((shifted >= opens) & (shifted < closes), 1.0, 0.0).astype(bf16)

            here = one_hot(0)
            low = dotf(here * one_hot(-DILATION), count).astype(bf16)
            high = dotf(here * one_hot(DILATION), count).astype(bf16)
            alive = (position[:, :128] < alive_until) & (position[:, :128] >= 0)
            alive = jnp.where(alive, 1.0, 0.0).astype(bf16)
            return jnp.concatenate([low, high, alive], axis=1), here

        ends[i, 0:HALO], hot_ends[i, 0:HALO] = rows_of(first, HALO)
        ends[i, HALO:], hot_ends[i, HALO:] = rows_of(first + HALO + rows, HALO)

        @pl.loop(0, rows // chunk)
        def _(k, i=i, rows_of=rows_of):
            at = pl.multiple_of(k * chunk, chunk)
            some, here = rows_of(first + HALO + at, chunk)
            masks[i, pl.ds(at, chunk)] = some
            hot[i, pl.ds(at, chunk)] = here


def film_kernel(
    tile, members, layout, place, frames, cond, low, high, hots, hot_ends, embed, own_cond, own_step, here, over, core, both,
    hidden, gain_cond, gain_step, w_cond, w_step, film_rows,
):
    i, j = pl.program_id(0), pl.program_id(1)
    width = frames.shape[2]
    rows = hidden.shape[1] - 2 * HALO - 2 * DILATION

    @pl.when((i == 0) & (j == 0))
    def _():
        sources = quarters_of(place, (here, over, core, both))
        assemble(place, members, layout, (own_cond, own_step), sources, (w_cond, w_step))
        step_film = dotf(embed[...], w_step[...])
        film_rows[...] = jnp.concatenate(split_rows(step_film, 2), axis=0)
        gain_cond[...] = w_cond[:, :width]
        gain_step[...] = film_rows[:, :width]

    def film(frame_rows, cond_rows, hot):
        both = dotf(cond_rows, w_cond[...]) + dotf(hot, film_rows[...])
        return (frame_rows.astype(f32) * (1.0 + both[:, :width]) + both[:, width:]).astype(bf16)

    @pl.when(j == 0)
    def _():
        edge = film(
            jnp.concatenate([low[0, i], high[0, i]], axis=0),
            jnp.concatenate([low[1, i], high[1, i]], axis=0),
            hot_ends[i],
        )
        nothing = jnp.zeros((DILATION, width), bf16)
        hidden[i, 0:DILATION] = nothing
        hidden[i, DILATION : DILATION + HALO] = edge[:HALO]
        hidden[i, DILATION + HALO + rows : DILATION + 2 * HALO + rows] = edge[HALO:]
        hidden[i, DILATION + 2 * HALO + rows :] = nothing

    base = pl.multiple_of(j * tile, tile)
    hidden[i, pl.ds(DILATION + HALO + base, tile)] = film(frames[0], cond[0], hots[0])


def halves_of(core, width):
    mine = pl.multiple_of(core * width, width)
    other = pl.multiple_of((1 - core) * width, width)
    return mine, other


def conv_kernel(
    tile, members, layout, place, hidden, masks, mask_ends, frames, res, skip, low, high, film, own_conv, own_proj,
    here, over, core, both,
    d_conv, d_conv_copy, conv_copy, sums, keep, send, res_out, skip_out,
    w_conv, w_proj, proj_total, columns, sems,
):
    i, j = pl.program_id(0), pl.program_id(1)
    width = res.shape[2]
    rows = d_conv.shape[1] - 2 * HALO
    gain, shift = 1.0 + film[i, 0:1, :width], film[i, 0:1, width:]
    first = (i == 0) & (j == 0)
    weights_away = pltpu.make_async_copy(w_conv, conv_copy, sems.at[2])

    @pl.when(first)
    def _():
        own = [own_conv.at[t] for t in range(3)]
        full = [w_conv.at[pl.ds(t * width, width)] for t in range(3)]
        sources = quarters_of(place, (here, over, core, both), 4)
        assemble(place, members, layout, [*own, own_proj], sources, [*full, w_proj])
        weights_away.start()
        sums[...] = jnp.zeros(sums.shape, f32)

    def body(before, now, later, keep_low, keep_high, alive, res_rows, skip_rows):
        taps = jnp.concatenate(
            [before * lanes(keep_low, width), now, later * lanes(keep_high, width)], axis=1
        )
        conv = dotf(taps, w_conv[...])
        th = jnp.tanh(conv[:, :width])
        sg = 0.5 + 0.5 * jnp.tanh(0.5 * conv[:, width:])
        alive = lanes(alive.astype(f32), width)
        branch = jnp.concatenate(
            [
                (res_rows.astype(f32) * (SQRT_HALF * alive)).astype(bf16),
                (skip_rows.astype(f32) * alive).astype(bf16),
            ],
            axis=1,
        )
        d_gated = dotf(branch, w_proj[...], NT)
        act = th * sg
        d_act = d_gated * gain
        left = (d_act * sg * (1.0 - th * th)).astype(bf16)
        right = (d_act * act * (1.0 - sg)).astype(bf16)
        return act, d_gated, branch, alive, left, right

    @pl.when(j == 0)
    def _():
        def ends(ref, at):
            return jnp.concatenate(
                [ref[i, at : at + HALO], ref[i, at + HALO + rows : at + 2 * HALO + rows]], axis=0
            )

        *_, left, right = body(
            ends(hidden, 0),
            ends(hidden, DILATION),
            ends(hidden, 2 * DILATION),
            mask_ends[i, :, 0:128],
            mask_ends[i, :, 128:256],
            mask_ends[i, :, 256:384],
            jnp.concatenate([low[2, i], high[2, i]], axis=0),
            jnp.concatenate([low[3, i], high[3, i]], axis=0),
        )
        d_conv[i, 0:HALO, :width] = left[:HALO]
        d_conv[i, 0:HALO, width:] = right[:HALO]
        d_conv[i, HALO + rows :, :width] = left[HALO:]
        d_conv[i, HALO + rows :, width:] = right[HALO:]
        columns[...] = jnp.zeros(columns.shape, f32)

    base = pl.multiple_of(j * tile, tile)

    size = tile // CONV_SUBS
    gated_all, branch_all = [], []
    for low_row in range(0, tile, size):
        part_rows = slice(low_row, low_row + size)

        def at(ref, offset, low_row=low_row):
            return ref[i, pl.ds(base + offset + low_row, size)]

        act, d_gated, branch, alive, left, right = body(
            at(hidden, HALO),
            at(hidden, HALO + DILATION),
            at(hidden, HALO + 2 * DILATION),
            masks[0, part_rows, 0:128],
            masks[0, part_rows, 128:256],
            masks[0, part_rows, 256:384],
            res[0, part_rows],
            skip[0, part_rows],
        )
        d_conv[i, pl.ds(base + HALO + low_row, size), :width] = left
        d_conv[i, pl.ds(base + HALO + low_row, size), width:] = right
        gated_rows = (act * gain + shift).astype(bf16)
        columns[:, :width] += jnp.sum((d_gated * act).reshape(size // 8, 8, width), axis=0)
        columns[:, width:] += jnp.sum(d_gated.reshape(size // 8, 8, width), axis=0)
        out = dotf(gated_rows, w_proj[...])
        frame_rows = frames[0, part_rows].astype(f32)
        res_out[0, part_rows] = ((frame_rows + out[:, :width]) * (SQRT_HALF * alive)).astype(bf16)
        skip_out[0, part_rows] = (out[:, width:] * alive).astype(bf16)
        gated_all.append(gated_rows)
        branch_all.append(branch)
    part = dotf(jnp.concatenate(gated_all, axis=0), jnp.concatenate(branch_all, axis=0), TN)

    @pl.when(first)
    def _():
        proj_total[...] = part

    @pl.when(jnp.logical_not(first))
    def _():
        proj_total[...] += part

    last = j == rows // tile - 1
    copies = [
        pltpu.make_async_copy(d_conv.at[m], d_conv_copy.at[m], sems.at[m]) for m in range(MICRO)
    ]
    for m in range(MICRO):
        pl.when(last & (i == m))(copies[m].start)

        @pl.when(last & (i == m))
        def _(m=m):
            sums[m : m + 1] = jnp.sum(columns[...], axis=0, keepdims=True)

    @pl.when(last & (i == MICRO - 1))
    def _():
        mine, other = halves_of(place[0], width)
        send[0] = proj_total[:, pl.ds(other, width)].astype(bf16)
        keep[0] = proj_total[:, pl.ds(mine, width)]
        for copy in (*copies, weights_away):
            copy.wait()


def conv_grad_kernel(place, hidden, masks, d_conv, keep, send):
    t = pl.program_id(0)
    micro, width = hidden.shape[0], hidden.shape[2]
    rows = d_conv.shape[1] - 2 * HALO
    mine, other = halves_of(place[0], width)

    for tap, lane in ((0, 0), (1, None), (2, 128)):

        @pl.when(t == tap)
        def _(tap=tap, lane=lane):
            def tap_rows(i):
                part = hidden[i, HALO + DILATION * tap : HALO + DILATION * tap + rows]
                return part if lane is None else part * lanes(masks[i, :, lane : lane + 128], width)

            for columns, ref in ((other, send), (mine, keep)):
                total = dotf(tap_rows(0), d_conv[0, HALO : HALO + rows, pl.ds(columns, width)], TN)
                for i in range(1, micro):
                    total = total + dotf(
                        tap_rows(i), d_conv[i, HALO : HALO + rows, pl.ds(columns, width)], TN
                    )
                ref[tap] = total.astype(ref.dtype)


def hidden_grad_kernel(
    tile, place, d_conv, masks, hots, frames, res, cond, w_conv, gain_cond, gain_step, embed,
    grad_frames, keep, send, total, window, sems,
):
    i, j = pl.program_id(0), pl.program_id(1)
    steps = pl.num_programs(1)
    width = frames.shape[2]
    now = i * steps + j

    def fetch(step):
        start = pl.multiple_of(HALO - DILATION + (step % steps) * tile, DILATION)
        return pltpu.make_async_copy(
            d_conv.at[step // steps, pl.ds(start, tile + 2 * DILATION)],
            window.at[step % 2],
            sems.at[step % 2],
        )

    @pl.when(now == 0)
    def _():
        fetch(0).start()

    @pl.when(now + 1 < MICRO * steps)
    def _():
        fetch(now + 1).start()

    fetch(now).wait()
    slot = now % 2
    size = tile // HIDDEN_SUBS
    films = []
    for low_row in range(0, tile, size):
        part_rows = slice(low_row, low_row + size)
        gain = dotf(cond[0, part_rows], gain_cond[...]) + dotf(hots[0, part_rows], gain_step[...])
        taps = []
        for tap, lane in ((2, 0), (1, None), (0, 128)):
            start = low_row + (2 - tap) * DILATION
            rows = window[slot, start : start + size]
            if lane is not None:
                rows = rows * lanes(masks[0, part_rows, lane : lane + 128], 2 * width)
            taps.append(dotf(rows, w_conv[tap], NT))
        d_hidden = taps[0] + taps[1] + taps[2]
        alive = lanes(masks[0, part_rows, 256:384].astype(f32), width)
        grad_frames[0, part_rows] = res[0, part_rows].astype(f32) * (SQRT_HALF * alive) + d_hidden * (
            1.0 + gain
        )
        films.append(
            jnp.concatenate(
                [(d_hidden * frames[0, part_rows].astype(f32)).astype(bf16), d_hidden.astype(bf16)], axis=1
            )
        )
    part = dotf(
        jnp.concatenate([cond[0], hots[0]], axis=1), jnp.concatenate(films, axis=0), TN
    )

    @pl.when(now == 0)
    def _():
        total[...] = part

    @pl.when(now > 0)
    def _():
        total[...] += part

    @pl.when(now == MICRO * steps - 1)
    def _():
        mine, other = halves_of(place[0], width)
        count = embed.shape[0]
        for columns, ref in ((other, send), (mine, keep)):
            ref[0] = total[:width, pl.ds(columns, width)].astype(ref.dtype)
            d_step = total[width : width + count, pl.ds(columns, width)]
            step = jnp.zeros((width, width), f32)
            for term in split_rows(d_step, 3):
                step = step + dotf(embed[...], term, TN)
            ref[1] = step.astype(ref.dtype)


def head_masks(width):
    column = lax.broadcasted_iota(jnp.int32, (1, width), 1)
    size = width // HEADS
    return [((column >= h * size) & (column < (h + 1) * size)).astype(f32) for h in range(HEADS)]


def attention_kernel(
    members, layout, place, every_prompt, queries, own_key, own_value, own_query, own_out, own_film, here, over, core, both,
    film, prompt, probs, keys, values, spread, summaries, totals, w_key, w_value, w_query, w_out, w_film,
):
    count, micro, shard, width = every_prompt.shape
    assemble(
        place,
        members,
        layout,
        (own_key, own_value, own_query, own_out, own_film),
        quarters_of(place, (here, over, core, both)),
        (w_key, w_value, w_query, w_out, w_film),
    )
    masks = head_masks(width)
    scale = 1.0 / math.sqrt(width // HEADS)
    for d in range(count):
        for i in range(micro):
            prompt[i, d * shard : (d + 1) * shard] = every_prompt[d, i]
    query = dotf(queries[...], w_query[...])
    spread[...] = jnp.concatenate([(query * mask).astype(bf16) for mask in masks], axis=0)
    for i in range(micro):
        keys[i] = dotf(prompt[i], w_key[...]).astype(bf16)
        values[i] = dotf(prompt[i], w_value[...]).astype(bf16)
        scores = dotf(spread[...], keys[i], NT) * scale
        weights = jnp.exp(scores - jnp.max(scores, axis=1, keepdims=True))
        weights = weights / jnp.sum(weights, axis=1, keepdims=True)
        probs[i] = weights
        heads = dotf(weights.astype(bf16), values[i])
        context = heads[:QUERIES] * masks[0]
        for h in range(1, HEADS):
            context = context + heads[h * QUERIES : (h + 1) * QUERIES] * masks[h]
        context = context.astype(bf16)
        mixed = dotf(context, w_out[...])
        summary = jnp.mean(mixed, axis=0, keepdims=True).astype(bf16)
        summary = jnp.broadcast_to(summary.astype(f32), (8, width))
        summaries[i] = summary
        totals[i] = jnp.broadcast_to(
            jnp.sum(context.astype(f32), axis=0, keepdims=True), (8, width)
        )
        wide = jnp.concatenate([summary, summary], axis=0).astype(bf16)
        film[i] = dotf(wide, w_film[...])[:8]


def exact_dot(row, matrix):
    terms = split_rows(row, 3)
    stacked = jnp.concatenate(
        [term.astype(f32) for term in terms] + [jnp.zeros((13, row.shape[1]), f32)], axis=0
    )
    return jnp.sum(dotf(stacked.astype(bf16), matrix, NT), axis=0, keepdims=True)


SMALL_ROWS = QUERIES + 5 * 8


def attention_grad_kernel(
    place, sums, prompt, probs, keys, values, spread, summaries, totals, w_key, w_value, w_out, w_film,
    grad_prompt, keep, small, pair,
):
    micro, length, width = prompt.shape
    masks = head_masks(width)
    scale = 1.0 / math.sqrt(width // HEADS)
    mine, _ = halves_of(place[0], width)
    shard = grad_prompt.shape[1]
    own = pl.multiple_of(place[1] * shard, shard)
    d_query_total = jnp.zeros((QUERIES, width), f32)
    small[...] = jnp.zeros(small.shape, f32)
    for i in range(micro):
        d_film = sums[i : i + 1]
        d_mixed = exact_dot(d_film, w_film[...]) / QUERIES
        d_context = exact_dot(d_mixed, w_out[...]).astype(bf16).astype(f32)
        d_heads = jnp.concatenate(
            [d_context * mask for mask in masks] + [jnp.zeros((8, width), f32)], axis=0
        ).astype(bf16)
        d_probs = dotf(d_heads, values[i], NT)
        d_probs = jnp.concatenate(
            [jnp.broadcast_to(d_probs[h : h + 1], (QUERIES, length)) for h in range(HEADS)], axis=0
        )
        weights = probs[i]
        row_sums = jnp.sum(weights * d_probs, axis=1, keepdims=True)
        d_scores = (weights * (d_probs - row_sums)).astype(bf16)
        heads = dotf(d_scores, keys[i])
        d_query = heads[:QUERIES] * masks[0]
        for h in range(1, HEADS):
            d_query = d_query + heads[h * QUERIES : (h + 1) * QUERIES] * masks[h]
        d_query_total = d_query_total + d_query * scale
        pair[i, :, :width] = (dotf(d_scores, spread[...], TN) * scale).astype(bf16)
        wide = jnp.concatenate(
            [jnp.broadcast_to(d_context * mask, (QUERIES, width)) for mask in masks], axis=0
        ).astype(bf16)
        pair[i, :, width:] = dotf(weights.astype(bf16), wide, TN).astype(bf16)
        grad_prompt[i] = dotf(pair[i, pl.ds(own, shard), :width], w_key[...], NT) + dotf(
            pair[i, pl.ds(own, shard), width:], w_value[...], NT
        )
        rows = (summaries[i, 0:1], d_film[:, :width], d_film[:, width:], totals[i, 0:1], d_mixed)
        for k, row in enumerate(rows):
            at = QUERIES + 8 * k + i
            small[at : at + 1] = row
    small[0:QUERIES] = d_query_total
    grad = jnp.zeros((width, width), f32)
    for i in range(micro):
        grad = grad + dotf(prompt[i], pair[i, :, pl.ds(mine, width)], TN)
    keep[...] = grad


def exact_outer(left, right):
    one = [t.astype(f32) for t in split_rows(left, 3)]
    two = [t.astype(f32) for t in split_rows(right, 3)]
    picks = ((0, 0), (0, 1), (0, 2), (1, 0), (1, 1), (2, 0))
    stacked = [jnp.concatenate([side[p[k]] for p in picks], axis=0) for k, side in ((0, one), (1, two))]
    return dotf(stacked[0].astype(bf16), stacked[1].astype(bf16), TN)


def small_grad_kernel(place, packs, queries, w_query, g_queries, g_query, g_out, g_film, rows_of, queries_of):
    members, _, width = packs.shape
    member = place[2]
    shard = g_query.shape[0]
    start = pl.multiple_of(member * shard, shard)

    def group(k):
        at = QUERIES + 8 * k
        return jnp.concatenate([packs[m, at : at + 8] for m in range(members)], axis=0)

    rows_of[...] = exact_outer(
        group(0), jnp.concatenate([group(1), group(2)], axis=1)
    )
    g_film[...] = rows_of[pl.ds(start, shard)]
    rows_of[:, :width] = exact_outer(group(3), group(4))
    g_out[...] = rows_of[pl.ds(start, shard), :width]
    d_query = packs[0, 0:QUERIES]
    for m in range(1, members):
        d_query = d_query + packs[m, 0:QUERIES]
    rows_of[:, width:] = exact_outer(queries[...].astype(f32), d_query)
    g_query[...] = rows_of[pl.ds(start, shard), width:]
    terms = jnp.concatenate(split_rows(d_query, 3), axis=0)
    product = dotf(terms, w_query[...], NT)
    queries_of[...] = product[:QUERIES] + product[QUERIES : 2 * QUERIES] + product[2 * QUERIES :]
    count = g_queries.shape[0]
    for m in range(members):

        @pl.when(member == m)
        def _(m=m):
            g_queries[...] = queries_of[m * count : (m + 1) * count]


def swapped(array, axis, bit):
    count = lax.axis_size(axis)
    return lax.ppermute(array, axis, [(i, i ^ bit) for i in range(count)])


def bit_of(axis, bit):
    return (lax.axis_index(axis) // bit) % 2


def bits_of(axis):
    count = lax.axis_size(axis)
    assert count & (count - 1) == 0
    return [1 << b for b in range(count.bit_length() - 1)]


def rounded(array):
    return lax.reduce_precision(array, 8, 7)


def parted(total, axis, bit, dim):
    size = total.shape[dim] // 2
    mine = bit_of(axis, bit)
    away = lax.dynamic_slice_in_dim(total, (1 - mine) * size, size, dim).astype(bf16)
    return away, lax.dynamic_slice_in_dim(total, mine * size, size, dim)


def halvings(order):
    members = [("fsdp", bit, 1) for bit in reversed(bits_of("fsdp"))]
    second = [("tm", 2, 2)]
    return members + second if order == 0 else second + members


def doubled(mine, theirs, axis, bit, dim):
    clear = bit_of(axis, bit) == 0
    return jnp.concatenate(
        [jnp.where(clear, mine, theirs), jnp.where(clear, theirs, mine)], axis=dim
    )


def behind(array, *others):
    return lax.optimization_barrier((array, *others))[0]


def gathered(packed, members, early=(), late=(), bit_2=2):
    every = packed[None]
    for bit in bits_of("fsdp"):
        theirs = swapped(every, "fsdp", bit)
        every = theirs if members == 2 else jnp.concatenate([every, theirs], axis=0)
    here = every if members == 2 else every[1:]
    if early:
        here = behind(here, *early)
    over = swapped(here, "tm", bit_2)
    if late:
        over = behind(over, *late)
    return here, over, swapped(here, "tm", 1), swapped(over, "tm", 1)


class Reduction:
    def __init__(self, halves):
        members = lax.axis_size("fsdp")
        self.steps = [halvings(k) for k in range(2)]
        self.totals = []
        for keeps, received in halves:
            total = jnp.concatenate(
                [k + r.astype(f32) for k, r in zip(keeps, received, strict=True)], axis=0
            )
            parts, rows, width = total.shape
            self.totals.append(total.reshape(parts, members, 2, rows // members // 2, width))
        self.send()

    def send(self):
        pairs = [parted(t, *s[0]) for t, s in zip(self.totals, self.steps, strict=True)]
        self.aways, self.kept = zip(*pairs, strict=True)
        self.raw = [swapped(a, *s[0][:2]) for a, s in zip(self.aways, self.steps, strict=True)]

    def absorb(self, *others):
        self.totals = [
            k + behind(r, *others).astype(f32) for k, r in zip(self.kept, self.raw, strict=True)
        ]
        self.steps = [s[1:] for s in self.steps]
        if self.steps[0]:
            self.send()

    def absorb_all(self, *others):
        while self.steps[0]:
            self.absorb(*others)

    def start_third(self):
        total = jnp.concatenate(self.totals, axis=0)
        total = total.reshape(total.shape[0], total.shape[3], total.shape[4])
        self.away, self.own = parted(total, "tm", 4, 1)
        self.raw = swapped(self.away, "tm", 4)

    def fold(self, *others):
        self.total = self.own + behind(self.raw, *others).astype(f32)

    def start_double(self, bit):
        self.own = rounded(self.total)
        self.away = self.own.astype(bf16)
        self.raw = swapped(self.away, "tm", bit)

    def start_gather(self):
        self.away = rounded(self.total).astype(bf16)
        self.raw = [swapped(self.away, "tm", bits) for bits in (4, 2, 6)]

    def gather(self):
        clear = bit_of("tm", 4) == 0
        pairs = []
        for one, two in ((self.away, self.raw[0]), (self.raw[1], self.raw[2])):
            pairs.append([jnp.where(clear, one, two), jnp.where(clear, two, one)])
        clear = bit_of("tm", 2) == 0
        rows = [jnp.where(clear, a, b) for a, b in zip(pairs[0] + pairs[1], pairs[1] + pairs[0], strict=True)]
        own = jnp.concatenate(rows, axis=1)
        return own, swapped(own, "tm", 1)


def join_kernel(place, own_first, other_first, own, other, out_first, out_second, out_taps, out_last):
    width = own.shape[2]
    mine, theirs = halves_of(place[0], width)
    for first, rest, columns in ((own_first, own, mine), (other_first, other, theirs)):
        out_first[:, pl.ds(columns, width)] = first[0].astype(f32)
        out_second[:, pl.ds(columns, width)] = first[1].astype(f32)
        out_taps[:, :, pl.ds(columns, width)] = rest[0:3].astype(f32)
        out_last[:, pl.ds(columns, width)] = rest[3].astype(f32)


def step_embedding(pack_steps, width):
    half_width = width // 2
    freqs = jnp.exp(jnp.arange(half_width).astype(f32) * (-math.log(10000.0) / half_width))
    angles = pack_steps.astype(f32)[:, None] * freqs[None, :]
    return jnp.concatenate([jnp.sin(angles), jnp.cos(angles)], axis=1)


def per_device(
    frames, conditioning, lengths, steps, prompt, queries, w_step, w_cond, w_conv, w_query, w_key,
    w_value, w_out, w_film, w_proj, grad_res, grad_skip,
):
    rows, width = frames.shape[2:]
    wide = 2 * width
    tile = rows // 3 if rows % 48 == 0 else rows
    tiles = (MICRO, rows // tile)
    conv_tile, hidden_tile = CONV_TILE, HIDDEN_TILE
    tm_count, tm_index = lax.axis_size("tm"), lax.axis_index("tm")
    members, member = lax.axis_size("fsdp"), lax.axis_index("fsdp")
    shard_rows = w_cond.shape[0]
    shard_queries = queries.shape[0]
    frames, cond, res, skip = frames[:, 0], conditioning[:, 0], grad_res[:, 0], grad_skip[:, 0]
    core = tm_index % 2
    quarter = core * 2 + (tm_index // 2) % 2
    other_quarter = core * 2 + (tm_index // 4) % 2
    place = jnp.stack([core, tm_index, member, quarter, other_quarter]).astype(jnp.int32)

    part = shard_rows // 4

    def pack(weights, layouts, heights, name, after=()):
        return call(
            functools.partial(pack_kernel, layouts),
            (1,),
            [scalars(place)] + [hbm(w) for w in weights],
            [new_fixed((height, wide), bf16) for height in heights],
            name,
            2,
            scratch=[pltpu.VMEM((height, wide), f32) for height in heights]
            + [pltpu.SemaphoreType.DMA((10,))],
            after=after,
        )

    layout_1 = [(0, 0), (part, 0)]
    layout_2 = [(0, 0), (0, width), (part, 0), (part, width), (2 * part, 0)]
    layout_3 = [(k * part, 0) for k in range(4)]
    taps_3 = [4, (0, 0, 0), (part, 0, 1), (2 * part, 0, 2), (3 * part, 0)]
    (first,) = pack([w_cond, w_step], [[3, *layout_1]], [2 * part], "pack_first")

    edge = (4, MICRO, HALO, width)
    last_rows, first_rows = call(
        edges_kernel,
        (1,),
        [hbm(a) for a in (frames, cond, res, skip)],
        [new_fixed(edge, bf16), new_fixed(edge, bf16)],
        "edges",
        1,
        scratch=[pltpu.SemaphoreType.DMA((8,))],
        after=[first],
    )
    low = lax.ppermute(last_rows, "tm", [(d, d + 1) for d in range(tm_count - 1)])
    high = lax.ppermute(first_rows, "tm", [(d + 1, d) for d in range(tm_count - 1)])

    second, third = pack(
        [w_key, w_value, w_query, w_out, w_film, w_conv, w_conv, w_conv, w_proj],
        [[3, *layout_2], taps_3],
        [3 * part, 4 * part],
        "pack_rest",
        after=[last_rows],
    )
    utters = lengths.shape[2]
    slot = -(-utters // 32) * 32
    hots = 2 * MICRO * slot
    masks, hot, mask_ends, hot_ends = call(
        functools.partial(masks_kernel, rows, slot, tm_count * rows),
        (1,),
        [scalars(place), scalars(lengths[:, 0])],
        [new((MICRO, n, lane), bf16) for n in (rows, 2 * HALO) for lane in (384, hots)],
        "masks",
        5,
        after=[second],
    )
    first_quarters = gathered(first, members, early=[second], late=[mask_ends])
    every_prompt = jnp.broadcast_to(behind(prompt, second)[None, :, 0], (tm_count, MICRO, *prompt.shape[2:]))
    every_prompt = lax.all_to_all(every_prompt, "tm", 0, 0)
    full_queries = behind(queries, second).astype(bf16)
    for bit in bits_of("fsdp"):
        full_queries = doubled(full_queries, swapped(full_queries, "fsdp", bit), "fsdp", bit, 0)

    slots = jnp.pad(steps[:, 0], ((0, 0), (0, slot - utters))).reshape(-1)
    embed = step_embedding(slots, width).astype(bf16)

    hidden, gain_cond, gain_step = call(
        functools.partial(film_kernel, tile, members, layout_1),
        tiles,
        [
            scalars(place),
            blocks(frames, tile),
            blocks(cond, tile),
            whole(low),
            whole(high),
            blocks(hot, tile),
            whole(hot_ends),
            whole(embed),
            whole(w_cond),
            whole(w_step),
            *[fixed(q) for q in first_quarters],
        ],
        [
            new_fixed((MICRO, rows + 2 * HALO + 2 * DILATION, width), bf16),
            new((width, width), bf16),
            new((hots, width), bf16),
        ],
        "film",
        1,
        scratch=[
            pltpu.VMEM((width, wide), bf16),
            pltpu.VMEM((width, wide), bf16),
            pltpu.VMEM((hots, wide), bf16),
        ],
        after=[full_queries],
    )
    second_quarters = gathered(second, members, early=[mask_ends], late=[gain_step])
    third_quarters = gathered(third, members, early=[mask_ends], late=[gain_step], bit_2=4)
    length = tm_count * prompt.shape[2]
    film, prompt_full, probs, keys, values, spread, summaries, totals, *fulls = call(
        functools.partial(attention_kernel, members, layout_2),
        (1,),
        [scalars(place)]
        + [whole(a) for a in (every_prompt, full_queries)]
        + [whole(w) for w in (w_key, w_value, w_query, w_out, w_film)]
        + [fixed(a) for a in second_quarters],
        [
            new((MICRO, 8, wide)),
            new((MICRO, length, width), bf16),
            new((MICRO, HEADS * QUERIES, length)),
            new((MICRO, length, width), bf16),
            new((MICRO, length, width), bf16),
            new((HEADS * QUERIES, width), bf16),
            new((MICRO, 8, width)),
            new((MICRO, 8, width)),
            *[new((width, width), bf16)] * 4,
            new((width, wide), bf16),
        ],
        "attention",
        5,
    )

    full_key, full_value, full_query, full_out, full_film = fulls

    d_conv, d_conv_copy, conv_copy, sums, proj_keep, proj_send, res_out, skip_out = call(
        functools.partial(conv_kernel, conv_tile, members, layout_3),
        (MICRO, rows // conv_tile),
        [
            scalars(place),
            fixed(hidden),
            blocks(masks, conv_tile),
            whole(mask_ends),
            blocks(frames, conv_tile),
            blocks(res, conv_tile),
            blocks(skip, conv_tile),
            whole(low),
            whole(high),
            whole(film),
            whole(w_conv),
            whole(w_proj),
            *[fixed(q) for q in third_quarters],
        ],
        [
            new_fixed((MICRO, rows + 2 * HALO, wide), bf16),
            new_hbm((MICRO, rows + 2 * HALO, wide), bf16),
            new_hbm((3 * width, wide), bf16),
            new((8, wide)),
            new_fixed((1, width, width)),
            new_fixed((1, width, width), bf16),
            new_blocks((MICRO, rows, width), bf16, conv_tile),
            new_blocks((MICRO, rows, width), bf16, conv_tile),
        ],
        "conv",
        32,
        scratch=[
            pltpu.VMEM((3 * width, wide), bf16),
            pltpu.VMEM((width, wide), bf16),
            pltpu.VMEM((width, wide), f32),
            pltpu.VMEM((8, wide), f32),
            pltpu.SemaphoreType.DMA((3,)),
        ],
    )

    proj_received = swapped(proj_send, "tm", 1)
    sums_near = swapped(sums, "tm", 1)
    conv_keep, conv_send = call(
        conv_grad_kernel,
        (3,),
        [scalars(place), fixed(hidden), whole(masks), fixed(d_conv)],
        [new_fixed((3, width, width)), new_fixed((3, width, width), bf16)],
        "conv_grad",
        13.5,
    )
    conv_received = swapped(conv_send, "tm", 1)
    sums = sums + behind(sums_near, conv_send)
    sums_far = swapped(sums, "tm", 2)
    conv_proj = Reduction(
        [
            ([conv_keep[:2]], [conv_received[:2]]),
            ([conv_keep[2:], proj_keep], [conv_received[2:], proj_received]),
        ]
    )
    sums = sums + behind(sums_far, *conv_proj.aways)
    sums_far = swapped(sums, "tm", 4)
    grad_frames, keep, send = call(
        functools.partial(hidden_grad_kernel, hidden_tile),
        (MICRO, rows // hidden_tile),
        [scalars(place), hbm(d_conv_copy)]
        + [blocks(a, hidden_tile) for a in (masks, hot, frames, res, cond)]
        + [whole(a) for a in (conv_copy.reshape(3, width, wide), gain_cond, gain_step, embed)],
        [
            new_blocks((MICRO, rows, width), f32, hidden_tile),
            new_fixed((2, width, width)),
            new_fixed((2, width, width), bf16),
        ],
        "hidden_grad",
        27,
        scratch=[
            pltpu.VMEM((width + hots, wide), f32),
            pltpu.VMEM((2, hidden_tile + 2 * DILATION, wide), bf16),
            pltpu.SemaphoreType.DMA((2,)),
        ],
        after=[*conv_proj.aways, sums],
    )
    send, sums_far, *conv_proj.raw = lax.optimization_barrier((send, sums_far, *conv_proj.raw))
    received = swapped(send, "tm", 1)
    conv_proj.absorb()
    sums = sums + sums_far
    for bit in bits_of("tm")[3:-1]:
        sums = sums + swapped(sums, "tm", bit)
    sums_far = swapped(sums, "tm", bits_of("tm")[-1])
    received = behind(received, *conv_proj.aways, sums)
    cond_step = Reduction([([keep[:1]], [received[:1]]), ([keep[1:]], [received[1:]])])
    sums_far = behind(sums_far, *cond_step.aways)
    conv_proj.absorb_all(*cond_step.aways)
    conv_proj.start_third()
    cond_step.absorb_all(conv_proj.away)
    cond_step.start_third()
    conv_proj.fold(cond_step.away)
    first_bit, *more_bits = bits_of("tm")[3:]
    conv_proj.start_double(first_bit)
    cond_step.fold(conv_proj.away)
    cond_step.start_double(first_bit)
    sums = sums + behind(sums_far, cond_step.away)
    grad_prompt, pair, small = call(
        attention_grad_kernel,
        (1,),
        [scalars(place)]
        + [
            whole(a)
            for a in (
                sums, prompt_full, probs, keys, values, spread, summaries, totals, full_key, full_value, full_out,
                full_film,
            )
        ],
        [new((MICRO, length // tm_count, width)), new((width, width)), new((SMALL_ROWS, width))],
        "attention_grad",
        7,
        scratch=[pltpu.VMEM((MICRO, length, wide), bf16)],
    )
    small, pair, conv_proj.raw = lax.optimization_barrier((small, pair, conv_proj.raw))
    for bit in reversed(bits_of("fsdp")):
        away, pair = parted(pair, "fsdp", bit, 0)
        pair = pair + swapped(away, "fsdp", bit).astype(f32)
    pair = rounded(pair).astype(bf16)
    pair_other = swapped(pair, "tm", 1)
    clear = bit_of("tm", 1) == 0
    grad_key = jnp.where(clear, pair, pair_other).astype(f32)
    grad_value = jnp.where(clear, pair_other, pair).astype(f32)

    packs = small[None]
    for bit in bits_of("fsdp"):
        packs = jnp.concatenate([packs, swapped(packs, "fsdp", bit)], axis=0)

    flat, tall = (shard_rows, wide), (3, shard_rows, wide)
    for bit in more_bits:
        conv_proj.fold(cond_step.away)
        conv_proj.start_double(bit)
        cond_step.fold(conv_proj.away)
        cond_step.start_double(bit)
    conv_proj.fold()
    conv_proj.start_gather()
    cond_step.fold(conv_proj.away, packs, pair)
    cond_step.start_gather()
    grad_queries, grad_query, grad_out, grad_film = call(
        small_grad_kernel,
        (1,),
        [scalars(place), whole(packs), whole(full_queries), whole(full_query)],
        [
            new((shard_queries, width)),
            new((shard_rows, width)),
            new((shard_rows, width)),
            new((shard_rows, wide)),
        ],
        "small_grads",
        3.3,
        scratch=[pltpu.VMEM((width, wide), f32), pltpu.VMEM((QUERIES, width), f32)],
        after=[cond_step.away],
    )
    grad_queries, grad_key, *cond_step.raw = lax.optimization_barrier(
        (grad_queries, grad_key, *cond_step.raw)
    )
    conv_proj = conv_proj.gather()
    cond_step = cond_step.gather()
    grad_cond, grad_step, grad_conv, grad_proj = call(
        join_kernel,
        (1,),
        [scalars(place)] + [fixed(a) for a in (*cond_step, *conv_proj)],
        [new(shape) for shape in (flat, flat, tall, flat)],
        "join",
        4,
    )
    return (
        res_out[:, None],
        skip_out[:, None],
        grad_frames[:, None],
        grad_prompt[:, None],
        grad_queries,
        grad_step,
        grad_cond,
        grad_conv,
        grad_query,
        grad_key,
        grad_value,
        grad_out,
        grad_film,
        grad_proj,
    )


def solution(mesh):
    packed = P(None, "fsdp", "tm", None)
    short = P(None, "fsdp", None)
    weight = P("fsdp", None)
    taps = P(None, "fsdp", None)
    in_specs = (packed, packed, short, short, packed) + (weight,) * 3 + (taps,) + (weight,) * 6 + (packed,) * 2
    out_specs = (packed,) * 4 + (weight,) * 3 + (taps,) + (weight,) * 6
    return jax.shard_map(
        per_device, mesh=mesh, in_specs=in_specs, out_specs=out_specs, check_vma=False
    )
```

```python
import functools
import math

import jax
import jax.numpy as jnp
from jax import lax
from jax.experimental import pallas as pl
from jax.experimental.pallas import tpu as pltpu
from jax.sharding import PartitionSpec as P

HEADS = 8
QUERIES = 32
DILATION = 16
MICRO = 2
HALO = 2 * DILATION

SQRT_HALF = 0.7071067811865476
VMEM_LIMIT = 40 * 2**20
CONV_TILE, CONV_SUBS = 768, 1
HIDDEN_TILE, HIDDEN_SUBS = 768, 1
NT = ((1,), (1,))
TN = ((0,), (0,))
bf16 = jnp.bfloat16
f32 = jnp.float32


def dotf(left, right, dims=((1,), (0,))):
    return lax.dot_general(left, right, (dims, ((), ())), preferred_element_type=f32)


def lanes(block, width):
    return jnp.concatenate([block] * (width // block.shape[1]), axis=1)


VSPEC = pl.BlockSpec(memory_space=pltpu.VMEM)
SSPEC = pl.BlockSpec(memory_space=pltpu.SMEM)
ANYSPEC = pl.BlockSpec(memory_space=pl.ANY)


def fixed(array):
    return pltpu.with_memory_space_constraint(array, pltpu.VMEM), VSPEC


def whole(array):
    return pltpu.with_memory_space_constraint(array, pltpu.HBM), pl.BlockSpec(array.shape, lambda *_: (0,) * array.ndim)


def blocks(array, tile, first=0):
    return pltpu.with_memory_space_constraint(array, pltpu.HBM), pl.BlockSpec(
        (1, tile, array.shape[2]), lambda i, j: (i + first, j, 0)
    )


def hbm(array):
    return pltpu.with_memory_space_constraint(array, pltpu.HBM), pl.BlockSpec(memory_space=pltpu.HBM)


def scalars(array):
    return array, SSPEC


def call(kernel, grid, ins, outs, name, micros, scratch=(), after=(), aliases=None):
    count, waits = len(ins), len(after)

    def body(*refs):
        kernel(*refs[:count], *refs[count + waits :])

    return pl.pallas_call(
        body,
        grid=grid,
        in_specs=[spec for _, spec in ins] + [ANYSPEC] * waits,
        out_specs=[spec for _, spec in outs],
        out_shape=[out for out, _ in outs],
        scratch_shapes=scratch,
        input_output_aliases=aliases or {},
        cost_estimate=pl.CostEstimate(
            flops=int(micros * 1e9), bytes_accessed=2**12, transcendentals=0
        ),
        compiler_params=pltpu.CompilerParams(vmem_limit_bytes=VMEM_LIMIT),
        name=name,
    )(*[array for array, _ in ins], *after)


def new(shape, kind=f32):
    return pltpu.HBM(shape, kind), pl.BlockSpec(shape, lambda *_: (0,) * len(shape))


def new_fixed(shape, kind=f32):
    return pltpu.VMEM(shape, kind), VSPEC


def new_hbm(shape, kind=f32):
    return pltpu.HBM(shape, kind), pl.BlockSpec(memory_space=pltpu.HBM)


def new_blocks(shape, kind, tile, first=0):
    return pltpu.HBM(shape, kind), pl.BlockSpec(
        (1, tile, shape[2]), lambda i, j: (i + first, j, 0)
    )


def split_rows(row, parts):
    terms = []
    for _ in range(parts):
        term = row.astype(bf16)
        terms.append(term)
        row = row - term.astype(f32)
    return terms


def pack_kernel(layouts, place, *refs):
    count = sum(len(layout) - 1 for layout in layouts)
    weights, refs = list(refs[:count]), refs[count:]
    outs, helds, sems = refs[: len(layouts)], refs[len(layouts) : -1], refs[-1]
    copies = []
    for (which, *layout), held in zip(layouts, helds, strict=True):
        for row, column, *tap in layout:
            weight = weights.pop(0)
            view = weight.at[tap[0]] if tap else weight
            rows = view.shape[0] // 4
            start = pl.multiple_of(place[which] * rows, rows)
            copies.append(
                pltpu.make_async_copy(
                    view.at[pl.ds(start, rows)],
                    held.at[pl.ds(row, rows), pl.ds(column, view.shape[1])],
                    sems.at[len(copies)],
                )
            )
    for copy in copies:
        copy.start()
    for copy in copies:
        copy.wait()
    for out, held in zip(outs, helds, strict=True):
        out[...] = held[...].astype(bf16)


def edges_kernel(*refs):
    arrays, (last, first, sems) = refs[:-3], refs[-3:]
    copies = []
    for k, array in enumerate(arrays):
        rows = array.shape[1]
        copies.append(
            pltpu.make_async_copy(array.at[:, pl.ds(rows - HALO, HALO)], last.at[k], sems.at[2 * k])
        )
        copies.append(
            pltpu.make_async_copy(array.at[:, pl.ds(0, HALO)], first.at[k], sems.at[2 * k + 1])
        )
    for copy in copies:
        copy.start()
    for copy in copies:
        copy.wait()


def assemble(place, members, layout, shards, sources, fulls):
    member = place[2]
    for shard, full, (row, column) in zip(shards, fulls, layout, strict=True):
        rows, width = shard.shape
        part = rows // 4
        full[pl.ds(pl.multiple_of(member * rows, part), rows)] = shard[...].astype(bf16)
        for j in range(1, members):
            for source, quarter in sources:
                start = pl.multiple_of((member ^ j) * rows + quarter * part, part)
                full[pl.ds(start, part)] = source[j - 1, row : row + part, column : column + width]


def quarters_of(place, arrays, which=3):
    return [(array, place[which] ^ k) for k, array in enumerate(arrays)]


def masks_kernel(rows, slot, total, place, lengths, masks, hot, ends, hot_ends):
    micro, utters = lengths.shape
    hots = hot.shape[2]
    lane = lax.broadcasted_iota(jnp.int32, (1, hots), 1)
    lane = jnp.where(lane >= micro * slot, lane - micro * slot, lane)
    row = lax.broadcasted_iota(jnp.int32, (hots, 128), 0)
    count = jnp.where(row < micro * slot, 1.0, 0.0).astype(bf16)
    first = place[1] * rows - HALO
    chunk = rows // 6
    for i in range(micro):
        opens = jnp.full((1, hots), total, jnp.int32)
        closes = jnp.zeros((1, hots), jnp.int32)
        end = jnp.int32(0)
        for u in range(utters):
            mine = lane == i * slot + u
            if u == utters - 1:
                alive_until = end
            opens = jnp.where(mine, end, opens)
            end = end + lengths[i, u]
            closes = jnp.where(mine, end, closes)

        def rows_of(start, size, i=i, opens=opens, closes=closes, alive_until=alive_until):
            position = lax.broadcasted_iota(jnp.int32, (size, hots), 0) + start

            def one_hot(offset):
                shifted = position + offset
                return jnp.where((shifted >= opens) & (shifted < closes), 1.0, 0.0).astype(bf16)

            here = one_hot(0)
            low = dotf(here * one_hot(-DILATION), count).astype(bf16)
            high = dotf(here * one_hot(DILATION), count).astype(bf16)
            alive = (position[:, :128] < alive_until) & (position[:, :128] >= 0)
            alive = jnp.where(alive, 1.0, 0.0).astype(bf16)
            return jnp.concatenate([low, high, alive], axis=1), here

        ends[i, 0:HALO], hot_ends[i, 0:HALO] = rows_of(first, HALO)
        ends[i, HALO:], hot_ends[i, HALO:] = rows_of(first + HALO + rows, HALO)

        @pl.loop(0, rows // chunk)
        def _(k, i=i, rows_of=rows_of):
            at = pl.multiple_of(k * chunk, chunk)
            some, here = rows_of(first + HALO + at, chunk)
            masks[i, pl.ds(at, chunk)] = some
            hot[i, pl.ds(at, chunk)] = here


def film_kernel(
    tile, members, layout, place, frames, cond, low, high, hots, hot_ends, embed, own_cond, own_step, here, over, core, both,
    hidden, gain_cond, gain_step, w_cond, w_step, film_rows,
):
    i, j = pl.program_id(0), pl.program_id(1)
    width = frames.shape[2]
    rows = hidden.shape[1] - 2 * HALO - 2 * DILATION

    @pl.when((i == 0) & (j == 0))
    def _():
        sources = quarters_of(place, (here, over, core, both))
        assemble(place, members, layout, (own_cond, own_step), sources, (w_cond, w_step))
        step_film = dotf(embed[...], w_step[...])
        film_rows[...] = jnp.concatenate(split_rows(step_film, 2), axis=0)
        gain_cond[...] = w_cond[:, :width]
        gain_step[...] = film_rows[:, :width]

    def film(frame_rows, cond_rows, hot):
        both = dotf(cond_rows, w_cond[...]) + dotf(hot, film_rows[...])
        return (frame_rows.astype(f32) * (1.0 + both[:, :width]) + both[:, width:]).astype(bf16)

    @pl.when(j == 0)
    def _():
        edge = film(
            jnp.concatenate([low[0, i], high[0, i]], axis=0),
            jnp.concatenate([low[1, i], high[1, i]], axis=0),
            hot_ends[i],
        )
        nothing = jnp.zeros((DILATION, width), bf16)
        hidden[i, 0:DILATION] = nothing
        hidden[i, DILATION : DILATION + HALO] = edge[:HALO]
        hidden[i, DILATION + HALO + rows : DILATION + 2 * HALO + rows] = edge[HALO:]
        hidden[i, DILATION + 2 * HALO + rows :] = nothing

    base = pl.multiple_of(j * tile, tile)
    hidden[i, pl.ds(DILATION + HALO + base, tile)] = film(frames[0], cond[0], hots[0])


def halves_of(core, width):
    mine = pl.multiple_of(core * width, width)
    other = pl.multiple_of((1 - core) * width, width)
    return mine, other


def conv_kernel(
    tile, members, layout, place, hidden, masks, mask_ends, frames, res, skip, low, high, film, own_conv, own_proj,
    here, over, core, both,
    d_conv, d_conv_copy, conv_copy, sums, keep, send, res_out, skip_out,
    w_conv, w_proj, proj_total, columns, sems,
):
    i, j = pl.program_id(0), pl.program_id(1)
    width = res.shape[2]
    rows = d_conv.shape[1] - 2 * HALO
    gain, shift = 1.0 + film[i, 0:1, :width], film[i, 0:1, width:]
    first = (i == 0) & (j == 0)
    weights_away = pltpu.make_async_copy(w_conv, conv_copy, sems.at[2])

    @pl.when(first)
    def _():
        own = [own_conv.at[t] for t in range(3)]
        full = [w_conv.at[pl.ds(t * width, width)] for t in range(3)]
        sources = quarters_of(place, (here, over, core, both), 4)
        assemble(place, members, layout, [*own, own_proj], sources, [*full, w_proj])
        weights_away.start()
        sums[...] = jnp.zeros(sums.shape, f32)

    def body(before, now, later, keep_low, keep_high, alive, res_rows, skip_rows):
        taps = jnp.concatenate(
            [before * lanes(keep_low, width), now, later * lanes(keep_high, width)], axis=1
        )
        conv = dotf(taps, w_conv[...])
        th = jnp.tanh(conv[:, :width])
        sg = 0.5 + 0.5 * jnp.tanh(0.5 * conv[:, width:])
        alive = lanes(alive.astype(f32), width)
        branch = jnp.concatenate(
            [
                (res_rows.astype(f32) * (SQRT_HALF * alive)).astype(bf16),
                (skip_rows.astype(f32) * alive).astype(bf16),
            ],
            axis=1,
        )
        d_gated = dotf(branch, w_proj[...], NT)
        act = th * sg
        d_act = d_gated * gain
        left = (d_act * sg * (1.0 - th * th)).astype(bf16)
        right = (d_act * act * (1.0 - sg)).astype(bf16)
        return act, d_gated, branch, alive, left, right

    @pl.when(j == 0)
    def _():
        def ends(ref, at):
            return jnp.concatenate(
                [ref[i, at : at + HALO], ref[i, at + HALO + rows : at + 2 * HALO + rows]], axis=0
            )

        *_, left, right = body(
            ends(hidden, 0),
            ends(hidden, DILATION),
            ends(hidden, 2 * DILATION),
            mask_ends[i, :, 0:128],
            mask_ends[i, :, 128:256],
            mask_ends[i, :, 256:384],
            jnp.concatenate([low[2, i], high[2, i]], axis=0),
            jnp.concatenate([low[3, i], high[3, i]], axis=0),
        )
        d_conv[i, 0:HALO, :width] = left[:HALO]
        d_conv[i, 0:HALO, width:] = right[:HALO]
        d_conv[i, HALO + rows :, :width] = left[HALO:]
        d_conv[i, HALO + rows :, width:] = right[HALO:]
        columns[...] = jnp.zeros(columns.shape, f32)

    base = pl.multiple_of(j * tile, tile)

    size = tile // CONV_SUBS
    gated_all, branch_all = [], []
    for low_row in range(0, tile, size):
        part_rows = slice(low_row, low_row + size)

        def at(ref, offset, low_row=low_row):
            return ref[i, pl.ds(base + offset + low_row, size)]

        act, d_gated, branch, alive, left, right = body(
            at(hidden, HALO),
            at(hidden, HALO + DILATION),
            at(hidden, HALO + 2 * DILATION),
            masks[0, part_rows, 0:128],
            masks[0, part_rows, 128:256],
            masks[0, part_rows, 256:384],
            res[0, part_rows],
            skip[0, part_rows],
        )
        d_conv[i, pl.ds(base + HALO + low_row, size), :width] = left
        d_conv[i, pl.ds(base + HALO + low_row, size), width:] = right
        gated_rows = (act * gain + shift).astype(bf16)
        columns[:, :width] += jnp.sum((d_gated * act).reshape(size // 8, 8, width), axis=0)
        columns[:, width:] += jnp.sum(d_gated.reshape(size // 8, 8, width), axis=0)
        out = dotf(gated_rows, w_proj[...])
        frame_rows = frames[0, part_rows].astype(f32)
        res_out[0, part_rows] = ((frame_rows + out[:, :width]) * (SQRT_HALF * alive)).astype(bf16)
        skip_out[0, part_rows] = (out[:, width:] * alive).astype(bf16)
        gated_all.append(gated_rows)
        branch_all.append(branch)
    part = dotf(jnp.concatenate(gated_all, axis=0), jnp.concatenate(branch_all, axis=0), TN)

    @pl.when(first)
    def _():
        proj_total[...] = part

    @pl.when(jnp.logical_not(first))
    def _():
        proj_total[...] += part

    last = j == rows // tile - 1
    copies = [
        pltpu.make_async_copy(d_conv.at[m], d_conv_copy.at[m], sems.at[m]) for m in range(MICRO)
    ]
    for m in range(MICRO):
        pl.when(last & (i == m))(copies[m].start)

        @pl.when(last & (i == m))
        def _(m=m):
            sums[m : m + 1] = jnp.sum(columns[...], axis=0, keepdims=True)

    @pl.when(last & (i == MICRO - 1))
    def _():
        mine, other = halves_of(place[0], width)
        send[0] = proj_total[:, pl.ds(other, width)].astype(bf16)
        keep[0] = proj_total[:, pl.ds(mine, width)]
        for copy in (*copies, weights_away):
            copy.wait()


def conv_grad_kernel(place, hidden, masks, d_conv, keep, send):
    t = pl.program_id(0)
    micro, width = hidden.shape[0], hidden.shape[2]
    rows = d_conv.shape[1] - 2 * HALO
    mine, other = halves_of(place[0], width)

    for tap, lane in ((0, 0), (1, None), (2, 128)):

        @pl.when(t == tap)
        def _(tap=tap, lane=lane):
            def tap_rows(i):
                part = hidden[i, HALO + DILATION * tap : HALO + DILATION * tap + rows]
                return part if lane is None else part * lanes(masks[i, :, lane : lane + 128], width)

            for columns, ref in ((other, send), (mine, keep)):
                total = dotf(tap_rows(0), d_conv[0, HALO : HALO + rows, pl.ds(columns, width)], TN)
                for i in range(1, micro):
                    total = total + dotf(
                        tap_rows(i), d_conv[i, HALO : HALO + rows, pl.ds(columns, width)], TN
                    )
                ref[tap] = total.astype(ref.dtype)


def hidden_grad_kernel(
    tile, place, d_conv, masks, hots, frames, res, cond, w_conv, gain_cond, gain_step, embed,
    grad_frames, keep, send, total, window, sems,
):
    i, j = pl.program_id(0), pl.program_id(1)
    steps = pl.num_programs(1)
    width = frames.shape[2]
    now = i * steps + j

    def fetch(step):
        start = pl.multiple_of(HALO - DILATION + (step % steps) * tile, DILATION)
        return pltpu.make_async_copy(
            d_conv.at[step // steps, pl.ds(start, tile + 2 * DILATION)],
            window.at[step % 2],
            sems.at[step % 2],
        )

    @pl.when(now == 0)
    def _():
        fetch(0).start()

    @pl.when(now + 1 < MICRO * steps)
    def _():
        fetch(now + 1).start()

    fetch(now).wait()
    slot = now % 2
    size = tile // HIDDEN_SUBS
    films = []
    for low_row in range(0, tile, size):
        part_rows = slice(low_row, low_row + size)
        gain = dotf(cond[0, part_rows], gain_cond[...]) + dotf(hots[0, part_rows], gain_step[...])
        taps = []
        for tap, lane in ((2, 0), (1, None), (0, 128)):
            start = low_row + (2 - tap) * DILATION
            rows = window[slot, start : start + size]
            if lane is not None:
                rows = rows * lanes(masks[0, part_rows, lane : lane + 128], 2 * width)
            taps.append(dotf(rows, w_conv[tap], NT))
        d_hidden = taps[0] + taps[1] + taps[2]
        alive = lanes(masks[0, part_rows, 256:384].astype(f32), width)
        grad_frames[0, part_rows] = res[0, part_rows].astype(f32) * (SQRT_HALF * alive) + d_hidden * (
            1.0 + gain
        )
        films.append(
            jnp.concatenate(
                [(d_hidden * frames[0, part_rows].astype(f32)).astype(bf16), d_hidden.astype(bf16)], axis=1
            )
        )
    part = dotf(
        jnp.concatenate([cond[0], hots[0]], axis=1), jnp.concatenate(films, axis=0), TN
    )

    @pl.when(now == 0)
    def _():
        total[...] = part

    @pl.when(now > 0)
    def _():
        total[...] += part

    @pl.when(now == MICRO * steps - 1)
    def _():
        mine, other = halves_of(place[0], width)
        count = embed.shape[0]
        for columns, ref in ((other, send), (mine, keep)):
            ref[0] = total[:width, pl.ds(columns, width)].astype(ref.dtype)
            d_step = total[width : width + count, pl.ds(columns, width)]
            step = jnp.zeros((width, width), f32)
            for term in split_rows(d_step, 3):
                step = step + dotf(embed[...], term, TN)
            ref[1] = step.astype(ref.dtype)


def head_masks(width):
    column = lax.broadcasted_iota(jnp.int32, (1, width), 1)
    size = width // HEADS
    return [((column >= h * size) & (column < (h + 1) * size)).astype(f32) for h in range(HEADS)]


def attention_kernel(
    members, layout, place, every_prompt, queries, own_key, own_value, own_query, own_out, own_film, here, over, core, both,
    film, prompt, probs, keys, values, spread, summaries, totals, w_key, w_value, w_query, w_out, w_film,
):
    count, micro, shard, width = every_prompt.shape
    assemble(
        place,
        members,
        layout,
        (own_key, own_value, own_query, own_out, own_film),
        quarters_of(place, (here, over, core, both)),
        (w_key, w_value, w_query, w_out, w_film),
    )
    masks = head_masks(width)
    scale = 1.0 / math.sqrt(width // HEADS)
    for d in range(count):
        for i in range(micro):
            prompt[i, d * shard : (d + 1) * shard] = every_prompt[d, i]
    query = dotf(queries[...], w_query[...])
    spread[...] = jnp.concatenate([(query * mask).astype(bf16) for mask in masks], axis=0)
    for i in range(micro):
        keys[i] = dotf(prompt[i], w_key[...]).astype(bf16)
        values[i] = dotf(prompt[i], w_value[...]).astype(bf16)
        scores = dotf(spread[...], keys[i], NT) * scale
        weights = jnp.exp(scores - jnp.max(scores, axis=1, keepdims=True))
        weights = weights / jnp.sum(weights, axis=1, keepdims=True)
        probs[i] = weights
        heads = dotf(weights.astype(bf16), values[i])
        context = heads[:QUERIES] * masks[0]
        for h in range(1, HEADS):
            context = context + heads[h * QUERIES : (h + 1) * QUERIES] * masks[h]
        context = context.astype(bf16)
        mixed = dotf(context, w_out[...])
        summary = jnp.mean(mixed, axis=0, keepdims=True).astype(bf16)
        summary = jnp.broadcast_to(summary.astype(f32), (8, width))
        summaries[i] = summary
        totals[i] = jnp.broadcast_to(
            jnp.sum(context.astype(f32), axis=0, keepdims=True), (8, width)
        )
        wide = jnp.concatenate([summary, summary], axis=0).astype(bf16)
        film[i] = dotf(wide, w_film[...])[:8]


def exact_dot(row, matrix):
    terms = split_rows(row, 3)
    stacked = jnp.concatenate(
        [term.astype(f32) for term in terms] + [jnp.zeros((13, row.shape[1]), f32)], axis=0
    )
    return jnp.sum(dotf(stacked.astype(bf16), matrix, NT), axis=0, keepdims=True)


SMALL_ROWS = QUERIES + 5 * 8


def attention_grad_kernel(
    place, sums, prompt, probs, keys, values, spread, summaries, totals, w_key, w_value, w_out, w_film,
    grad_prompt, keep, small, pair,
):
    micro, length, width = prompt.shape
    masks = head_masks(width)
    scale = 1.0 / math.sqrt(width // HEADS)
    mine, _ = halves_of(place[0], width)
    shard = grad_prompt.shape[1]
    own = pl.multiple_of(place[1] * shard, shard)
    d_query_total = jnp.zeros((QUERIES, width), f32)
    small[...] = jnp.zeros(small.shape, f32)
    for i in range(micro):
        d_film = sums[i : i + 1]
        d_mixed = exact_dot(d_film, w_film[...]) / QUERIES
        d_context = exact_dot(d_mixed, w_out[...]).astype(bf16).astype(f32)
        d_heads = jnp.concatenate(
            [d_context * mask for mask in masks] + [jnp.zeros((8, width), f32)], axis=0
        ).astype(bf16)
        d_probs = dotf(d_heads, values[i], NT)
        d_probs = jnp.concatenate(
            [jnp.broadcast_to(d_probs[h : h + 1], (QUERIES, length)) for h in range(HEADS)], axis=0
        )
        weights = probs[i]
        row_sums = jnp.sum(weights * d_probs, axis=1, keepdims=True)
        d_scores = (weights * (d_probs - row_sums)).astype(bf16)
        heads = dotf(d_scores, keys[i])
        d_query = heads[:QUERIES] * masks[0]
        for h in range(1, HEADS):
            d_query = d_query + heads[h * QUERIES : (h + 1) * QUERIES] * masks[h]
        d_query_total = d_query_total + d_query * scale
        pair[i, :, :width] = (dotf(d_scores, spread[...], TN) * scale).astype(bf16)
        wide = jnp.concatenate(
            [jnp.broadcast_to(d_context * mask, (QUERIES, width)) for mask in masks], axis=0
        ).astype(bf16)
        pair[i, :, width:] = dotf(weights.astype(bf16), wide, TN).astype(bf16)
        grad_prompt[i] = dotf(pair[i, pl.ds(own, shard), :width], w_key[...], NT) + dotf(
            pair[i, pl.ds(own, shard), width:], w_value[...], NT
        )
        rows = (summaries[i, 0:1], d_film[:, :width], d_film[:, width:], totals[i, 0:1], d_mixed)
        for k, row in enumerate(rows):
            at = QUERIES + 8 * k + i
            small[at : at + 1] = row
    small[0:QUERIES] = d_query_total
    grad = jnp.zeros((width, width), f32)
    for i in range(micro):
        grad = grad + dotf(prompt[i], pair[i, :, pl.ds(mine, width)], TN)
    keep[...] = grad


def exact_outer(left, right):
    one = [t.astype(f32) for t in split_rows(left, 3)]
    two = [t.astype(f32) for t in split_rows(right, 3)]
    picks = ((0, 0), (0, 1), (0, 2), (1, 0), (1, 1), (2, 0))
    stacked = [jnp.concatenate([side[p[k]] for p in picks], axis=0) for k, side in ((0, one), (1, two))]
    return dotf(stacked[0].astype(bf16), stacked[1].astype(bf16), TN)


def small_grad_kernel(place, packs, queries, w_query, g_queries, g_query, g_out, g_film, rows_of, queries_of):
    members, _, width = packs.shape
    member = place[2]
    shard = g_query.shape[0]
    start = pl.multiple_of(member * shard, shard)

    def group(k):
        at = QUERIES + 8 * k
        return jnp.concatenate([packs[m, at : at + 8] for m in range(members)], axis=0)

    rows_of[...] = exact_outer(
        group(0), jnp.concatenate([group(1), group(2)], axis=1)
    )
    g_film[...] = rows_of[pl.ds(start, shard)]
    rows_of[:, :width] = exact_outer(group(3), group(4))
    g_out[...] = rows_of[pl.ds(start, shard), :width]
    d_query = packs[0, 0:QUERIES]
    for m in range(1, members):
        d_query = d_query + packs[m, 0:QUERIES]
    rows_of[:, width:] = exact_outer(queries[...].astype(f32), d_query)
    g_query[...] = rows_of[pl.ds(start, shard), width:]
    terms = jnp.concatenate(split_rows(d_query, 3), axis=0)
    product = dotf(terms, w_query[...], NT)
    queries_of[...] = product[:QUERIES] + product[QUERIES : 2 * QUERIES] + product[2 * QUERIES :]
    count = g_queries.shape[0]
    for m in range(members):

        @pl.when(member == m)
        def _(m=m):
            g_queries[...] = queries_of[m * count : (m + 1) * count]


def swapped(array, axis, bit):
    count = lax.axis_size(axis)
    return lax.ppermute(array, axis, [(i, i ^ bit) for i in range(count)])


def bit_of(axis, bit):
    return (lax.axis_index(axis) // bit) % 2


def bits_of(axis):
    count = lax.axis_size(axis)
    assert count & (count - 1) == 0
    return [1 << b for b in range(count.bit_length() - 1)]


def rounded(array):
    return lax.reduce_precision(array, 8, 7)


def parted(total, axis, bit, dim):
    size = total.shape[dim] // 2
    mine = bit_of(axis, bit)
    away = lax.dynamic_slice_in_dim(total, (1 - mine) * size, size, dim).astype(bf16)
    return away, lax.dynamic_slice_in_dim(total, mine * size, size, dim)


def halvings(order):
    members = [("fsdp", bit, 1) for bit in reversed(bits_of("fsdp"))]
    second = [("tm", 2, 2)]
    return members + second if order == 0 else second + members


def doubled(mine, theirs, axis, bit, dim):
    clear = bit_of(axis, bit) == 0
    return jnp.concatenate(
        [jnp.where(clear, mine, theirs), jnp.where(clear, theirs, mine)], axis=dim
    )


def behind(array, *others):
    return lax.optimization_barrier((array, *others))[0]


def gathered(packed, members, early=(), late=(), bit_2=2):
    every = packed[None]
    for bit in bits_of("fsdp"):
        theirs = swapped(every, "fsdp", bit)
        every = theirs if members == 2 else jnp.concatenate([every, theirs], axis=0)
    here = every if members == 2 else every[1:]
    if early:
        here = behind(here, *early)
    over = swapped(here, "tm", bit_2)
    if late:
        over = behind(over, *late)
    return here, over, swapped(here, "tm", 1), swapped(over, "tm", 1)


class Reduction:
    def __init__(self, halves):
        members = lax.axis_size("fsdp")
        self.steps = [halvings(k) for k in range(2)]
        self.totals = []
        for keeps, received in halves:
            total = jnp.concatenate(
                [k + r.astype(f32) for k, r in zip(keeps, received, strict=True)], axis=0
            )
            parts, rows, width = total.shape
            self.totals.append(total.reshape(parts, members, 2, rows // members // 2, width))
        self.send()

    def send(self):
        pairs = [parted(t, *s[0]) for t, s in zip(self.totals, self.steps, strict=True)]
        self.aways, self.kept = zip(*pairs, strict=True)
        self.raw = [swapped(a, *s[0][:2]) for a, s in zip(self.aways, self.steps, strict=True)]

    def absorb(self, *others):
        self.totals = [
            k + behind(r, *others).astype(f32) for k, r in zip(self.kept, self.raw, strict=True)
        ]
        self.steps = [s[1:] for s in self.steps]
        if self.steps[0]:
            self.send()

    def absorb_all(self, *others):
        while self.steps[0]:
            self.absorb(*others)

    def start_third(self):
        total = jnp.concatenate(self.totals, axis=0)
        total = total.reshape(total.shape[0], total.shape[3], total.shape[4])
        self.away, self.own = parted(total, "tm", 4, 1)
        self.raw = swapped(self.away, "tm", 4)

    def fold(self, *others):
        self.total = self.own + behind(self.raw, *others).astype(f32)

    def start_double(self, bit):
        self.own = rounded(self.total)
        self.away = self.own.astype(bf16)
        self.raw = swapped(self.away, "tm", bit)

    def start_gather(self):
        self.away = rounded(self.total).astype(bf16)
        self.raw = [swapped(self.away, "tm", bits) for bits in (4, 2, 6)]

    def gather(self):
        clear = bit_of("tm", 4) == 0
        pairs = []
        for one, two in ((self.away, self.raw[0]), (self.raw[1], self.raw[2])):
            pairs.append([jnp.where(clear, one, two), jnp.where(clear, two, one)])
        clear = bit_of("tm", 2) == 0
        rows = [jnp.where(clear, a, b) for a, b in zip(pairs[0] + pairs[1], pairs[1] + pairs[0], strict=True)]
        own = jnp.concatenate(rows, axis=1)
        return own, swapped(own, "tm", 1)


def join_kernel(place, own_first, other_first, own, other, out_first, out_second, out_taps, out_last):
    width = own.shape[2]
    mine, theirs = halves_of(place[0], width)
    for first, rest, columns in ((own_first, own, mine), (other_first, other, theirs)):
        out_first[:, pl.ds(columns, width)] = first[0].astype(f32)
        out_second[:, pl.ds(columns, width)] = first[1].astype(f32)
        out_taps[:, :, pl.ds(columns, width)] = rest[0:3].astype(f32)
        out_last[:, pl.ds(columns, width)] = rest[3].astype(f32)


def step_embedding(pack_steps, width):
    half_width = width // 2
    freqs = jnp.exp(jnp.arange(half_width).astype(f32) * (-math.log(10000.0) / half_width))
    angles = pack_steps.astype(f32)[:, None] * freqs[None, :]
    return jnp.concatenate([jnp.sin(angles), jnp.cos(angles)], axis=1)


def per_device(
    frames, conditioning, lengths, steps, prompt, queries, w_step, w_cond, w_conv, w_query, w_key,
    w_value, w_out, w_film, w_proj, grad_res, grad_skip,
):
    rows, width = frames.shape[2:]
    wide = 2 * width
    tile = rows // 3 if rows % 48 == 0 else rows
    tiles = (MICRO, rows // tile)
    conv_tile, hidden_tile = CONV_TILE, HIDDEN_TILE
    tm_count, tm_index = lax.axis_size("tm"), lax.axis_index("tm")
    members, member = lax.axis_size("fsdp"), lax.axis_index("fsdp")
    shard_rows = w_cond.shape[0]
    shard_queries = queries.shape[0]
    frames, cond, res, skip = frames[:, 0], conditioning[:, 0], grad_res[:, 0], grad_skip[:, 0]
    core = tm_index % 2
    quarter = core * 2 + (tm_index // 2) % 2
    other_quarter = core * 2 + (tm_index // 4) % 2
    place = jnp.stack([core, tm_index, member, quarter, other_quarter]).astype(jnp.int32)

    part = shard_rows // 4

    def pack(weights, layouts, heights, name, after=()):
        return call(
            functools.partial(pack_kernel, layouts),
            (1,),
            [scalars(place)] + [hbm(w) for w in weights],
            [new_fixed((height, wide), bf16) for height in heights],
            name,
            2,
            scratch=[pltpu.VMEM((height, wide), f32) for height in heights]
            + [pltpu.SemaphoreType.DMA((10,))],
            after=after,
        )

    layout_1 = [(0, 0), (part, 0)]
    layout_2 = [(0, 0), (0, width), (part, 0), (part, width), (2 * part, 0)]
    layout_3 = [(k * part, 0) for k in range(4)]
    taps_3 = [4, (0, 0, 0), (part, 0, 1), (2 * part, 0, 2), (3 * part, 0)]
    (first,) = pack([w_cond, w_step], [[3, *layout_1]], [2 * part], "pack_first")

    edge = (4, MICRO, HALO, width)
    last_rows, first_rows = call(
        edges_kernel,
        (1,),
        [hbm(a) for a in (frames, cond, res, skip)],
        [new_fixed(edge, bf16), new_fixed(edge, bf16)],
        "edges",
        1,
        scratch=[pltpu.SemaphoreType.DMA((8,))],
        after=[first],
    )
    low = lax.ppermute(last_rows, "tm", [(d, d + 1) for d in range(tm_count - 1)])
    high = lax.ppermute(first_rows, "tm", [(d + 1, d) for d in range(tm_count - 1)])

    second, third = pack(
        [w_key, w_value, w_query, w_out, w_film, w_conv, w_conv, w_conv, w_proj],
        [[3, *layout_2], taps_3],
        [3 * part, 4 * part],
        "pack_rest",
        after=[last_rows],
    )
    utters = lengths.shape[2]
    slot = -(-utters // 32) * 32
    hots = 2 * MICRO * slot
    masks, hot, mask_ends, hot_ends = call(
        functools.partial(masks_kernel, rows, slot, tm_count * rows),
        (1,),
        [scalars(place), scalars(lengths[:, 0])],
        [new((MICRO, n, lane), bf16) for n in (rows, 2 * HALO) for lane in (384, hots)],
        "masks",
        5,
        after=[second],
    )
    first_quarters = gathered(first, members, early=[second], late=[mask_ends])
    every_prompt = jnp.broadcast_to(behind(prompt, mask_ends)[None, :, 0], (tm_count, MICRO, *prompt.shape[2:]))
    every_prompt = lax.all_to_all(every_prompt, "tm", 0, 0)
    full_queries = behind(queries, second).astype(bf16)
    for bit in bits_of("fsdp"):
        full_queries = doubled(full_queries, swapped(full_queries, "fsdp", bit), "fsdp", bit, 0)

    slots = jnp.pad(steps[:, 0], ((0, 0), (0, slot - utters))).reshape(-1)
    embed = step_embedding(slots, width).astype(bf16)

    hidden, gain_cond, gain_step = call(
        functools.partial(film_kernel, tile, members, layout_1),
        tiles,
        [
            scalars(place),
            blocks(frames, tile),
            blocks(cond, tile),
            whole(low),
            whole(high),
            blocks(hot, tile),
            whole(hot_ends),
            whole(embed),
            whole(w_cond),
            whole(w_step),
            *[fixed(q) for q in first_quarters],
        ],
        [
            new_fixed((MICRO, rows + 2 * HALO + 2 * DILATION, width), bf16),
            new((width, width), bf16),
            new((hots, width), bf16),
        ],
        "film",
        1,
        scratch=[
            pltpu.VMEM((width, wide), bf16),
            pltpu.VMEM((width, wide), bf16),
            pltpu.VMEM((hots, wide), bf16),
        ],
        after=[full_queries],
    )
    second_quarters = gathered(second, members, early=[mask_ends], late=[gain_step])
    third_quarters = gathered(third, members, early=[mask_ends], late=[gain_step], bit_2=4)
    length = tm_count * prompt.shape[2]
    film, prompt_full, probs, keys, values, spread, summaries, totals, *fulls = call(
        functools.partial(attention_kernel, members, layout_2),
        (1,),
        [scalars(place)]
        + [whole(a) for a in (every_prompt, full_queries)]
        + [whole(w) for w in (w_key, w_value, w_query, w_out, w_film)]
        + [fixed(a) for a in second_quarters],
        [
            new((MICRO, 8, wide)),
            new((MICRO, length, width), bf16),
            new((MICRO, HEADS * QUERIES, length)),
            new((MICRO, length, width), bf16),
            new((MICRO, length, width), bf16),
            new((HEADS * QUERIES, width), bf16),
            new((MICRO, 8, width)),
            new((MICRO, 8, width)),
            *[new((width, width), bf16)] * 4,
            new((width, wide), bf16),
        ],
        "attention",
        5,
    )

    full_key, full_value, full_query, full_out, full_film = fulls

    d_conv, d_conv_copy, conv_copy, sums, proj_keep, proj_send, res_out, skip_out = call(
        functools.partial(conv_kernel, conv_tile, members, layout_3),
        (MICRO, rows // conv_tile),
        [
            scalars(place),
            fixed(hidden),
            blocks(masks, conv_tile),
            whole(mask_ends),
            blocks(frames, conv_tile),
            blocks(res, conv_tile),
            blocks(skip, conv_tile),
            whole(low),
            whole(high),
            whole(film),
            whole(w_conv),
            whole(w_proj),
            *[fixed(q) for q in third_quarters],
        ],
        [
            new_fixed((MICRO, rows + 2 * HALO, wide), bf16),
            new_hbm((MICRO, rows + 2 * HALO, wide), bf16),
            new_hbm((3 * width, wide), bf16),
            new((8, wide)),
            new_fixed((1, width, width)),
            new_fixed((1, width, width), bf16),
            new_blocks((MICRO, rows, width), bf16, conv_tile),
            new_blocks((MICRO, rows, width), bf16, conv_tile),
        ],
        "conv",
        32,
        scratch=[
            pltpu.VMEM((3 * width, wide), bf16),
            pltpu.VMEM((width, wide), bf16),
            pltpu.VMEM((width, wide), f32),
            pltpu.VMEM((8, wide), f32),
            pltpu.SemaphoreType.DMA((3,)),
        ],
    )

    proj_received = swapped(proj_send, "tm", 1)
    sums_near = swapped(sums, "tm", 1)
    conv_keep, conv_send = call(
        conv_grad_kernel,
        (3,),
        [scalars(place), fixed(hidden), whole(masks), fixed(d_conv)],
        [new_fixed((3, width, width)), new_fixed((3, width, width), bf16)],
        "conv_grad",
        13.5,
    )
    conv_received = swapped(conv_send, "tm", 1)
    sums = sums + behind(sums_near, conv_send)
    sums_far = swapped(sums, "tm", 2)
    conv_proj = Reduction(
        [
            ([conv_keep[:2]], [conv_received[:2]]),
            ([conv_keep[2:], proj_keep], [conv_received[2:], proj_received]),
        ]
    )
    sums = sums + behind(sums_far, *conv_proj.aways)
    sums_far = swapped(sums, "tm", 4)
    grad_frames, keep, send = call(
        functools.partial(hidden_grad_kernel, hidden_tile),
        (MICRO, rows // hidden_tile),
        [scalars(place), hbm(d_conv_copy)]
        + [blocks(a, hidden_tile) for a in (masks, hot, frames, res, cond)]
        + [whole(a) for a in (conv_copy.reshape(3, width, wide), gain_cond, gain_step, embed)],
        [
            new_blocks((MICRO, rows, width), f32, hidden_tile),
            new_fixed((2, width, width)),
            new_fixed((2, width, width), bf16),
        ],
        "hidden_grad",
        27,
        scratch=[
            pltpu.VMEM((width + hots, wide), f32),
            pltpu.VMEM((2, hidden_tile + 2 * DILATION, wide), bf16),
            pltpu.SemaphoreType.DMA((2,)),
        ],
        after=[*conv_proj.aways, sums],
    )
    send, sums_far, *conv_proj.raw = lax.optimization_barrier((send, sums_far, *conv_proj.raw))
    received = swapped(send, "tm", 1)
    conv_proj.absorb()
    sums = sums + sums_far
    for bit in bits_of("tm")[3:-1]:
        sums = sums + swapped(sums, "tm", bit)
    sums_far = swapped(sums, "tm", bits_of("tm")[-1])
    received = behind(received, *conv_proj.aways, sums)
    cond_step = Reduction([([keep[:1]], [received[:1]]), ([keep[1:]], [received[1:]])])
    sums_far = behind(sums_far, *cond_step.aways)
    conv_proj.absorb_all(*cond_step.aways)
    conv_proj.start_third()
    cond_step.absorb_all(conv_proj.away)
    cond_step.start_third()
    conv_proj.fold(cond_step.away)
    first_bit, *more_bits = bits_of("tm")[3:]
    conv_proj.start_double(first_bit)
    cond_step.fold(conv_proj.away)
    cond_step.start_double(first_bit)
    sums = sums + behind(sums_far, cond_step.away)
    grad_prompt, pair, small = call(
        attention_grad_kernel,
        (1,),
        [scalars(place)]
        + [
            whole(a)
            for a in (
                sums, prompt_full, probs, keys, values, spread, summaries, totals, full_key, full_value, full_out,
                full_film,
            )
        ],
        [new((MICRO, length // tm_count, width)), new((width, width)), new((SMALL_ROWS, width))],
        "attention_grad",
        7,
        scratch=[pltpu.VMEM((MICRO, length, wide), bf16)],
    )
    small, pair, conv_proj.raw = lax.optimization_barrier((small, pair, conv_proj.raw))
    for bit in reversed(bits_of("fsdp")):
        away, pair = parted(pair, "fsdp", bit, 0)
        pair = pair + swapped(away, "fsdp", bit).astype(f32)
    pair = rounded(pair).astype(bf16)
    pair_other = swapped(pair, "tm", 1)
    clear = bit_of("tm", 1) == 0
    grad_key = jnp.where(clear, pair, pair_other).astype(f32)
    grad_value = jnp.where(clear, pair_other, pair).astype(f32)

    packs = small[None]
    for bit in bits_of("fsdp"):
        packs = jnp.concatenate([packs, swapped(packs, "fsdp", bit)], axis=0)

    flat, tall = (shard_rows, wide), (3, shard_rows, wide)
    for bit in more_bits:
        conv_proj.fold(cond_step.away)
        conv_proj.start_double(bit)
        cond_step.fold(conv_proj.away)
        cond_step.start_double(bit)
    conv_proj.fold()
    conv_proj.start_gather()
    cond_step.fold(conv_proj.away, packs, pair)
    cond_step.start_gather()
    grad_queries, grad_query, grad_out, grad_film = call(
        small_grad_kernel,
        (1,),
        [scalars(place), whole(packs), whole(full_queries), whole(full_query)],
        [
            new((shard_queries, width)),
            new((shard_rows, width)),
            new((shard_rows, width)),
            new((shard_rows, wide)),
        ],
        "small_grads",
        3.3,
        scratch=[pltpu.VMEM((width, wide), f32), pltpu.VMEM((QUERIES, width), f32)],
        after=[cond_step.away],
    )
    grad_queries, grad_key, *cond_step.raw = lax.optimization_barrier(
        (grad_queries, grad_key, *cond_step.raw)
    )
    conv_proj = conv_proj.gather()
    cond_step = cond_step.gather()
    grad_cond, grad_step, grad_conv, grad_proj = call(
        join_kernel,
        (1,),
        [scalars(place)] + [fixed(a) for a in (*cond_step, *conv_proj)],
        [new(shape) for shape in (flat, flat, tall, flat)],
        "join",
        4,
    )
    return (
        res_out[:, None],
        skip_out[:, None],
        grad_frames[:, None],
        grad_prompt[:, None],
        grad_queries,
        grad_step,
        grad_cond,
        grad_conv,
        grad_query,
        grad_key,
        grad_value,
        grad_out,
        grad_film,
        grad_proj,
    )


def solution(mesh):
    packed = P(None, "fsdp", "tm", None)
    short = P(None, "fsdp", None)
    weight = P("fsdp", None)
    taps = P(None, "fsdp", None)
    in_specs = (packed, packed, short, short, packed) + (weight,) * 3 + (taps,) + (weight,) * 6 + (packed,) * 2
    out_specs = (packed,) * 4 + (weight,) * 3 + (taps,) + (weight,) * 6
    return jax.shard_map(
        per_device, mesh=mesh, in_specs=in_specs, out_specs=out_specs, check_vma=False
    )
```
